32 devices in a mesh: dp: 8 (over z, y), seq: 4 (over x, core).
Axes of the slice: x: 2, y: 2, z: 4, core: 2. Of those that a mesh axis runs over, the one named last changes fastest.
Arguments:
- tokens: bfloat16 [2048, 8, 768], P('seq', 'dp'), may hold values from -6 to 6
- cotangent: bfloat16 [2048, 8, 768], P('seq', 'dp'), may hold values from -6 to 6
- loss_mask: int32 [2048, 8], P('seq', 'dp'), may hold values 0 or 1
- segments: int32 [2048, 8], P(None, 'dp'), may hold values from 0 to 7, as said below
- params: float32 [55552, 128], replicated, may hold values from -3 to 3, as said below
- first_moment: float32 [55552, 128], P(('dp', 'seq')), may hold values from -0.6 to 0.6
- second_moment: float32 [55552, 128], P(('dp', 'seq')), may hold values from 0.01 to 1
Outputs:
- block_output: bfloat16 [2048, 8, 768], P('seq', 'dp')
- input_grad: bfloat16 [2048, 8, 768], P('seq', 'dp')
- new_params: float32 [55552, 128], P(('dp', 'seq'))
- new_first: float32 [55552, 128], P(('dp', 'seq'))
- new_second: float32 [55552, 128], P(('dp', 'seq'))
- bias_down_grad: float32 [768], replicated
The draws below stay inside these ranges and needn't reach their ends.
Inputs may be any that keep to these rules, and one draw needn't show every extreme that they name: `segments`: in every row the numbers start at 0 and never fall; a document is a run of equal numbers. Of rows 4k to 4k + 3, exactly one holds a single document. `params`: the first 7087104 entries hold the block's parameters in the order of the steps; the rest are unused.
All inputs are finite; a program needn't handle non-finite values. No bound on the sum of `loss_mask` on one device may be relied on, other than what follows from the above.
Results may differ from the reference program's by a relative error of at most 0.015.
Values may be sent and summed in bfloat16 or wider, within the bound.
No kernel may reach another device: no remote copies, remote signals or barrier semaphores. Data moves between devices by JAX's collectives and lax.ppermute only.
A program may use at most 256 MiB of HBM per device.

```python
import math
import jax
import jax.numpy as jnp
from jax import lax

D = 768
HEADS = 12
HEAD_DIM = 64
FF = 3072
DOC_LEN = 256
STEP = 4
LEN = 2048
ROWS = 8
PARAMS = 7087104
PROWS = 55552
N_DP = 8
N_SEQ = 4


def draw_segments(key, part):
    key = jax.random.fold_in(key, 11)
    start_key, row_key = jax.random.split(key)
    starts = (jax.random.randint(start_key, (LEN, ROWS), 0, DOC_LEN) == 0).astype(jnp.int32)
    chosen = jax.random.randint(row_key, (ROWS // 4,), 0, 4)
    row_index = jnp.arange(ROWS)
    whole_row = row_index % 4 == jnp.repeat(chosen, 4)
    regular_row = (row_index == (chosen[0] + 1) % 4) & jnp.logical_not(whole_row)
    position = jnp.arange(LEN)[:, None]
    regular_starts = (position % DOC_LEN == 0).astype(jnp.int32)
    starts = jnp.where(regular_row[None, :], regular_starts, starts)
    first_cell = position == 0
    starts = jnp.where(whole_row[None, :] | first_cell, 0, starts)
    numbers = jnp.cumsum(starts, axis=0)
    return jnp.minimum(numbers, LEN // DOC_LEN - 1).astype(jnp.int32)


def draw_params(key, part):
    key = jax.random.fold_in(key, 23)
    regions = [(D, 1.0, 0.2), (D, 0.0, 0.5), (3 * D * D, 0.0, HEAD_DIM ** (-0.5)), (D, 0.0, 1.0), (D, 0.0, 1.0), (D * D, 0.0, 0.5), (D, 0.0, 1.0), (D, 1.0, 0.2), (D, 0.0, 0.5), (D * FF, 0.0, D ** (-0.5)), (FF, 0.0, 1.0), (FF * D, 0.0, 24.0 ** (-0.5)), (D, 0.0, 1.0)]
    total = PROWS * 128
    flat_index = jnp.arange(total, dtype=jnp.int32)
    centre = jnp.zeros((total,), jnp.float32)
    spread = jnp.full((total,), 0.1, jnp.float32)
    offset = 0
    for entries, middle, width_scale in regions:
        inside = (flat_index >= offset) & (flat_index < offset + entries)
        centre = jnp.where(inside, middle, centre)
        spread = jnp.where(inside, width_scale, spread)
        offset += entries
    unit = jnp.clip(jax.random.normal(key, (total,), jnp.float32), -3.0, 3.0)
    return (centre + spread * unit).reshape(PROWS, 128)


def plant(values, rng, least, high):
    longest = values.shape.index(max(values.shape))
    spots = []
    for shift in (0, 1):
        where = [jax.random.randint(jax.random.fold_in(rng, axis), (), 0, length) for axis, length in enumerate(values.shape)]
        where[longest] = (where[longest] + shift) % values.shape[longest]
        spots.append(tuple(where))
    return values.at[spots[0]].set(least).at[spots[1]].set(high)


def block_scale(rng, shape, pieces, low, top_value):
    factor_of = 1.0
    for dim, parts in pieces:
        steps = jax.random.uniform(jax.random.fold_in(jax.random.fold_in(rng, 6), dim), (parts,), jnp.float32, low / len(pieces), top_value / len(pieces))
        factor_of = factor_of * jnp.repeat(jnp.exp(steps), shape[dim] // parts).reshape((-1,) + (1,) * (len(shape) - 1 - dim))
    return factor_of


def centred(rng, shape, scale, reach, shards=(), held_as=jnp.bfloat16):
    values = jax.random.normal(rng, shape, jnp.float32) * scale
    if len(shards) > 0:
        values = block_scale(rng, shape, shards, -0.22, 0.18) * values
    return jnp.clip(values, min=-reach, max=reach).astype(held_as)


def setup_inputs(seed: int = 0) -> dict:
    seeds = jax.random.split(jax.random.key(seed), 8)
    tokens = centred(seeds[0], (LEN, ROWS, D), 1.0, 6.0, ((0, 4), (1, 8)))
    cotangent = centred(seeds[1], (LEN, ROWS, D), 1.0, 6.0, ((0, 4), (1, 8)))
    loss_mask = plant((jax.random.randint(seeds[2], (LEN, ROWS), 0, 8) < 7).astype(jnp.int32), jax.random.fold_in(seeds[2], 1), 0, 1)
    segments = draw_segments(jax.random.fold_in(seeds[7], 71), 0)
    params = draw_params(jax.random.fold_in(seeds[7], 71), 0)
    first_moment = centred(seeds[5], (PROWS, 128), 0.1, 0.6, ((0, 32),), jnp.float32)
    second_moment = jnp.clip(jnp.exp(math.log(1.0) - 4.6051702 * jax.random.uniform(seeds[6], (PROWS, 128), jnp.float32) ** block_scale(seeds[6], (PROWS, 128), ((0, 32),), -0.2, 0.2)), 0.01, 1.0)
    return {"tokens": tokens, "cotangent": cotangent, "loss_mask": loss_mask, "segments": segments, "params": params, "first_moment": first_moment, "second_moment": second_moment}


@jax.custom_vjp
def low(v):
    return lax.optimization_barrier(v.astype(jnp.bfloat16)).astype(jnp.float32)

@jax.custom_vjp
def low_back(v):
    return v

def low_keep(v):
    return (low(v), None)

def low_pass(kept, grad):
    return (grad,)

def back_keep(v):
    return (v, None)

def back_low(kept, grad):
    return (low(grad),)
low.defvjp(low_keep, low_pass)
low_back.defvjp(back_keep, back_low)
norm_epsilon = 1e-05
branch_scale = 48.0 ** (-0.5)
first_decay = 0.9
second_decay = 0.95
adam_epsilon = 1e-08
base_rate = 0.1
group_rows = 4

def param_extents(width, hidden):
    return [(width,), (width,), (width, 3 * width), (width,), (width,), (width, width), (width,), (width,), (width,), (width, hidden), (hidden,), (hidden, width), (width,)]

def matrix_spans(width, hidden):
    span_list = []
    offset = 0
    for extent in param_extents(width, hidden):
        entries = math.prod(extent)
        if len(extent) == 2:
            span_list.append((offset, offset + entries))
        offset += entries
    return span_list

def unpack(flat, width, hidden):
    weights = []
    offset = 0
    for extent in param_extents(width, hidden):
        entries = math.prod(extent)
        weights.append(flat[offset:offset + entries].reshape(extent))
        offset += entries
    return weights

def rate_table(first_row, row_count):
    flat_index = (first_row + jnp.arange(row_count, dtype=jnp.int32))[:, None] * 128 + jnp.arange(128, dtype=jnp.int32)[None, :]
    in_matrix = jnp.zeros(flat_index.shape, bool)
    for span_begin, finish in matrix_spans(D, FF):
        in_matrix = in_matrix | (flat_index >= span_begin) & (flat_index < finish)
    return jnp.where(in_matrix, base_rate / D, base_rate)

def layer_norm(values, gain, shift):
    center = values - lax.optimization_barrier(jnp.mean(values, axis=-1, keepdims=True))
    spread = lax.optimization_barrier(jnp.mean(center * center, axis=-1, keepdims=True))
    return center * lax.rsqrt(spread + norm_epsilon) * gain + shift

def mix(left, right, form):
    return jnp.einsum(form, left, right, precision=lax.Precision.HIGHEST)

def attention(queries, keys_part, values_part, seg_block):
    positions = jnp.arange(LEN, dtype=jnp.int32)
    allowed = (positions[None, :] <= positions[:, None])[None] & (seg_block.T[:, :, None] == seg_block.T[:, None, :])
    scores = low_back(mix(queries, keys_part, 'qghd,kghd->ghqk') / HEAD_DIM)
    scores = jnp.where(allowed[:, None], scores, -1e+30)
    probs = low(jax.nn.softmax(scores, axis=-1))
    return mix(probs, values_part, 'ghqk,kghd->qghd')

def block_group(weights, inputs, seg_block):
    gain_one, shift_one, w_qkv, bias_query, bias_value, w_out, bias_out, gain_two, shift_two, w_up, bias_up, w_down, bias_down = weights
    group = inputs.shape[1]
    normed_one = low(layer_norm(inputs, gain_one, shift_one))
    projected = mix(normed_one, low(w_qkv), 'lgd,de->lge')
    queries = low(low_back(projected[..., :D] + bias_query))
    keys_part = low(low_back(projected[..., D:2 * D]))
    values_part = low(low_back(projected[..., 2 * D:] + bias_value))
    head_shape = (LEN, group, HEADS, HEAD_DIM)
    mixed = attention(queries.reshape(head_shape), keys_part.reshape(head_shape), values_part.reshape(head_shape), seg_block)
    mixed = low(low_back(mixed.reshape(LEN, group, D)))
    attn_out = low_back(mix(mixed, low(w_out), 'lgd,de->lge') + bias_out)
    resid_one = inputs + branch_scale * attn_out
    normed_two = low(layer_norm(resid_one, gain_two, shift_two))
    up_proj = low_back(mix(normed_two, low(w_up), 'lgd,df->lgf') + bias_up)
    active = low(jax.nn.gelu(up_proj, approximate=True))
    mlp_out = low_back(mix(active, low(w_down), 'lgf,fd->lgd') + bias_down)
    return resid_one + branch_scale * mlp_out

def reference(tokens, cotangent, loss_mask, segments, params, first_moment, second_moment):
    groups = ROWS // group_rows
    weights = tuple(unpack(params.reshape(-1)[:PARAMS], D, FF))
    inputs = tokens.astype(jnp.float32)
    seg_groups = segments.reshape(LEN, groups, group_rows).transpose(1, 0, 2)

    def whole(weight_tuple, acts):
        grouped = acts.reshape(LEN, groups, group_rows, D).transpose(1, 0, 2, 3)
        step_fn = jax.checkpoint(lambda pair: block_group(weight_tuple, pair[0], pair[1]))
        result = lax.map(step_fn, (grouped, seg_groups))
        return result.transpose(1, 0, 2, 3).reshape(LEN, ROWS, D)
    output, pullback = jax.vjp(whole, weights, inputs)
    grad_out = cotangent.astype(jnp.float32) * loss_mask.astype(jnp.float32)[..., None]
    weight_grads, input_grad = pullback(grad_out)
    padding = PROWS * 128 - PARAMS
    flat_grads = jnp.concatenate([grad_piece.reshape(-1) for grad_piece in weight_grads] + [jnp.zeros((padding,), jnp.float32)])
    grads_mean = flat_grads.reshape(PROWS, 128) / (N_DP * N_SEQ)
    bias_down_grad = grads_mean.reshape(-1)[PARAMS - D:PARAMS]
    new_first = first_decay * first_moment + (1.0 - first_decay) * grads_mean
    new_second = second_decay * second_moment + (1.0 - second_decay) * grads_mean * grads_mean
    fix_one = 1.0 - first_decay ** STEP
    fix_two = 1.0 - second_decay ** STEP
    update = new_first / fix_one / (jnp.sqrt(new_second / fix_two) + adam_epsilon)
    new_params = params - rate_table(0, PROWS) * update
    return (output.astype(jnp.bfloat16), input_grad.astype(jnp.bfloat16), new_params, new_first, new_second, bias_down_grad)
```

```python
from functools import partial
import math

import jax
import jax.numpy as jnp
from jax import lax
from jax.sharding import PartitionSpec as P

D = 768
HEADS = 12
HEAD_DIM = 64
FF = 3072
STEP = 4


norm_epsilon = 1e-05
branch_scale = 48.0 ** (-0.5)
first_decay = 0.9
second_decay = 0.95
adam_epsilon = 1e-08
base_rate = 0.1
masked_score = -1e30


def param_extents(width, hidden):
    return [
        (width,),
        (width,),
        (width, 3 * width),
        (width,),
        (width,),
        (width, width),
        (width,),
        (width,),
        (width,),
        (width, hidden),
        (hidden,),
        (hidden, width),
        (width,),
    ]


def unpack(flat, width, hidden):
    weights = []
    offset = 0
    for extent in param_extents(width, hidden):
        entries = math.prod(extent)
        weights.append(flat[offset : offset + entries].reshape(extent))
        offset += entries
    return weights


def rate_table(first_row, row_count, width, hidden):
    flat_index = (first_row + jnp.arange(row_count, dtype=jnp.int32))[:, None] * 128 + jnp.arange(
        128, dtype=jnp.int32
    )[None, :]
    in_matrix = jnp.zeros(flat_index.shape, bool)
    offset = 0
    for extent in param_extents(width, hidden):
        entries = math.prod(extent)
        if len(extent) == 2:
            in_matrix = in_matrix | (flat_index >= offset) & (flat_index < offset + entries)
        offset += entries
    return jnp.where(in_matrix, base_rate / width, base_rate)


def layer_norm(values, gain, shift):
    center = values - jnp.mean(values, axis=-1, keepdims=True)
    spread = jnp.mean(center * center, axis=-1, keepdims=True)
    return center * lax.rsqrt(spread + norm_epsilon) * gain + shift


def visible(segments, query_segs, query_pos, key_start, key_count):
    key_segs = lax.dynamic_slice_in_dim(segments, key_start, key_count, 0)
    key_pos = key_start + jnp.arange(key_count, dtype=jnp.int32)
    allowed = (key_pos[None, :] <= query_pos[:, None])[None] & (
        query_segs.T[:, :, None] == key_segs.T[:, None, :]
    )
    last_key = jnp.maximum(jnp.minimum(key_start + key_count - 1, query_pos[-1]), 0)
    reach = lax.dynamic_slice_in_dim(segments, last_key, 1, 0)[0]
    active = (key_start <= query_pos[-1]) & jnp.any(reach >= query_segs[0])
    return (allowed, active)


from jax.experimental import pallas as pl
from jax.experimental.pallas import tpu as pltpu

f32 = jnp.float32
bf16 = jnp.bfloat16
LANES = 128


def rounded(value):
    return lax.reduce_precision(value, 8, 7).astype(bf16)


def copy_body(a_ref, o_ref):
    o_ref[...] = a_ref[...]


def bit_pairs(size, bit, sender=lambda place: True):
    return [(n, n ^ bit) for n in range(size) if sender(n)]


def swap(value, axis, bit):
    return lax.ppermute(value, axis, bit_pairs(lax.axis_size(axis), bit))


def halves(value, axis, which):
    size = value.shape[axis] // 2
    own = lax.dynamic_slice_in_dim(value, which * size, size, axis)
    other = lax.dynamic_slice_in_dim(value, (1 - which) * size, size, axis)
    return own, other


def add(a, b):
    return rounded(a.astype(f32) + b.astype(f32))


def core_window(shard_rows):
    return (shard_rows + 15) // 16 * 16


def reduce_plane(piece, shard_rows):
    core = lax.axis_index("seq") % 2
    x = lax.axis_index("seq") // 2
    y = lax.axis_index("dp") % 2
    window = core_window(shard_rows)
    blocks = piece.reshape(2, 2, 2 * shard_rows, LANES)
    first, second = blocks[:, :, :window], blocks[:, :, 2 * shard_rows - window :]
    own = jnp.where(core == 0, first, second)
    other = jnp.where(core == 0, second, first)
    blocks = add(own, swap(other, "seq", 1))
    cut = window // 32 * 16
    one, two = blocks[:, :, :cut], blocks[:, :, cut:]
    own_one, other_one = halves(one, 1, x)
    own_two, other_two = halves(two, 0, y)
    got_one, got_two = swap(other_one, "seq", 2), swap(other_two, "dp", 1)
    one, two = add(own_one, got_one), add(own_two, got_two)
    own_one, other_one = halves(one, 0, y)
    own_two, other_two = halves(two, 1, x)
    got_one, got_two = swap(other_one, "dp", 1), swap(other_two, "seq", 2)
    one, two = add(own_one, got_one), add(own_two, got_two)
    return jnp.concatenate([one, two], axis=2).reshape(window, LANES)


def reduce_up(part, plane):
    size = lax.axis_size("dp")
    bit = 1
    while bit < size // 2:

        def sender(n):
            z = n // 2
            return (z ^ plane) & bit != 0 and (z ^ plane) & (bit - 1) == 0

        part = add(part, lax.ppermute(part, "dp", bit_pairs(size, 2 * bit, sender)))
        bit *= 2
    return part


def shards(tokens, cotangent, loss_mask, segments, params, first_moment, second_moment):
    f32 = jnp.float32
    bf16 = jnp.bfloat16
    seq_rows, batch_rows, width = tokens.shape
    seq_parts = lax.axis_size("seq")
    query_start = lax.axis_index("seq") * seq_rows
    score_scale = 1.0 / HEAD_DIM
    (
        gain_one,
        shift_one,
        w_qkv,
        bias_query,
        bias_value,
        w_out,
        bias_out,
        gain_two,
        shift_two,
        w_up,
        bias_up,
        w_down,
        bias_down,
    ) = unpack(params.reshape(-1), D, FF)
    qkv_low = w_qkv.astype(bf16)
    out_low = w_out.astype(bf16)
    up_low = w_up.astype(bf16)
    down_low = w_down.astype(bf16)
    inputs = tokens.astype(f32)
    normed_one, norm_one_back = jax.vjp(layer_norm, inputs, gain_one, shift_one)
    normed_one_low = normed_one.astype(bf16)
    projected = jnp.einsum("sbd,de->sbe", normed_one_low, qkv_low, preferred_element_type=f32)
    queries = (projected[..., :D] + bias_query).astype(bf16)
    keys_values = jnp.concatenate(
        [projected[..., D : 2 * D], projected[..., 2 * D :] + bias_value], axis=-1
    ).astype(bf16)
    query_segs = lax.dynamic_slice_in_dim(segments, query_start, seq_rows, 0)
    query_pos = query_start + jnp.arange(seq_rows, dtype=jnp.int32)
    head_shape = (seq_rows, batch_rows, HEADS, HEAD_DIM)
    query_heads = queries.reshape(head_shape)
    start_state = (
        jnp.full((batch_rows, HEADS, seq_rows), masked_score, f32),
        jnp.zeros((batch_rows, HEADS, seq_rows), f32),
        jnp.zeros((batch_rows, HEADS, seq_rows, HEAD_DIM), f32),
    )
    kv_piece = lax.all_gather(keys_values, "seq", axis=0, tiled=True)
    key_count = kv_piece.shape[0]
    allowed, active = visible(segments, query_segs, query_pos, jnp.int32(0), key_count)

    def update(state):
        run_max, run_sum, run_acc = state
        key_heads = kv_piece[..., :D].reshape(key_count, batch_rows, HEADS, HEAD_DIM)
        value_heads = kv_piece[..., D:].reshape(key_count, batch_rows, HEADS, HEAD_DIM)
        scores = (
            jnp.einsum("qbhd,kbhd->bhqk", query_heads, key_heads, preferred_element_type=f32)
            * score_scale
        )
        masked = jnp.where(allowed[:, None], scores, masked_score)
        new_max = jnp.maximum(run_max, jnp.max(masked, axis=-1))
        weights_exp = jnp.where(allowed[:, None], jnp.exp(masked - new_max[..., None]), 0.0)
        new_sum = jnp.sum(weights_exp, axis=-1)
        new_acc = jnp.einsum(
            "bhqk,kbhd->bhqd", weights_exp.astype(bf16), value_heads, preferred_element_type=f32
        )
        return (new_max, new_sum, new_acc)

    run_max, run_sum, run_acc = lax.cond(active, update, lambda state: state, start_state)
    log_total = run_max + jnp.log(run_sum)
    attn_heads = (run_acc / run_sum[..., None]).transpose(2, 0, 1, 3)
    attn_low = attn_heads.reshape(seq_rows, batch_rows, D).astype(bf16)
    attn_y = jnp.einsum("sbd,de->sbe", attn_low, out_low, preferred_element_type=f32) + bias_out
    resid_one = inputs + branch_scale * attn_y
    normed_two, norm_two_back = jax.vjp(layer_norm, resid_one, gain_two, shift_two)
    normed_two_low = normed_two.astype(bf16)
    up_proj = (
        jnp.einsum("sbd,df->sbf", normed_two_low, up_low, preferred_element_type=f32) + bias_up
    )
    active_up, gelu_back = jax.vjp(partial(jax.nn.gelu, approximate=True), up_proj)
    active_low = active_up.astype(bf16)
    mlp_y = jnp.einsum("sbf,fd->sbd", active_low, down_low, preferred_element_type=f32) + bias_down
    block_output = (resid_one + branch_scale * mlp_y).astype(bf16)
    grad_out = cotangent.astype(f32) * loss_mask.astype(f32)[..., None]
    d_mlp = (branch_scale * grad_out).astype(bf16)
    grad_down = jnp.einsum("sbf,sbd->fd", active_low, d_mlp, preferred_element_type=f32)
    d_bias_down = jnp.sum(d_mlp.astype(f32), axis=(0, 1))
    d_active = jnp.einsum("sbd,fd->sbf", d_mlp, down_low, preferred_element_type=f32)
    d_up = gelu_back(d_active)[0].astype(bf16)
    grad_up = jnp.einsum("sbd,sbf->df", normed_two_low, d_up, preferred_element_type=f32)
    d_bias_up = jnp.sum(d_up.astype(f32), axis=(0, 1))
    d_normed_two = jnp.einsum("sbf,df->sbd", d_up, up_low, preferred_element_type=f32)
    d_resid_part, d_gain_two, d_shift_two = norm_two_back(d_normed_two)
    d_resid_one = grad_out + d_resid_part
    d_attn_y = (branch_scale * d_resid_one).astype(bf16)
    grad_out_w = jnp.einsum("sbd,sbe->de", attn_low, d_attn_y, preferred_element_type=f32)
    d_bias_out = jnp.sum(d_attn_y.astype(f32), axis=(0, 1))
    d_attn_low = jnp.einsum("sbe,de->sbd", d_attn_y, out_low, preferred_element_type=f32).astype(
        bf16
    )
    d_heads = d_attn_low.reshape(head_shape)
    delta = jnp.sum(d_heads.astype(f32) * attn_heads, axis=-1).transpose(1, 2, 0)
    gathered = lax.all_gather(keys_values, "seq", axis=0, tiled=True)
    kv_blocks = gathered.reshape(seq_parts, seq_rows, batch_rows, 2 * D)

    def back_block(grad_query, pair):
        kv_piece, block_number = pair
        key_start = block_number * seq_rows
        allowed, active = visible(segments, query_segs, query_pos, key_start, seq_rows)

        def compute(grad_acc):
            key_heads = kv_piece[..., :D].reshape(head_shape)
            value_heads = kv_piece[..., D:].reshape(head_shape)
            scores = (
                jnp.einsum("qbhd,kbhd->bhqk", query_heads, key_heads, preferred_element_type=f32)
                * score_scale
            )
            masked = jnp.where(allowed[:, None], scores, masked_score)
            probs = jnp.where(allowed[:, None], jnp.exp(masked - log_total[..., None]), 0.0)
            d_probs = jnp.einsum(
                "qbhd,kbhd->bhqk", d_heads, value_heads, preferred_element_type=f32
            )
            d_scores = (probs * (d_probs - delta[..., None])).astype(bf16)
            grad_acc = (
                grad_acc
                + jnp.einsum("bhqk,kbhd->bhqd", d_scores, key_heads, preferred_element_type=f32)
                * score_scale
            )
            grad_key = (
                jnp.einsum("bhqk,qbhd->kbhd", d_scores, query_heads, preferred_element_type=f32)
                * score_scale
            )
            grad_value = jnp.einsum(
                "bhqk,qbhd->kbhd", probs.astype(bf16), d_heads, preferred_element_type=f32
            )
            kv_term = jnp.concatenate(
                [
                    grad_key.reshape(seq_rows, batch_rows, D),
                    grad_value.reshape(seq_rows, batch_rows, D),
                ],
                axis=-1,
            )
            return (grad_acc, kv_term)

        def passby(grad_acc):
            return (grad_acc, jnp.zeros((seq_rows, batch_rows, 2 * D), f32))

        return lax.cond(active, compute, passby, grad_query)

    grad_query, kv_terms = lax.scan(
        back_block,
        jnp.zeros((batch_rows, HEADS, seq_rows, HEAD_DIM), f32),
        (kv_blocks, jnp.arange(seq_parts, dtype=jnp.int32)),
    )
    kv_terms = kv_terms.reshape(seq_parts * seq_rows, batch_rows, 2 * D)
    kv_grad_low = (
        lax.psum_scatter(kv_terms.astype(jnp.bfloat16), "seq", scatter_dimension=0, tiled=True)
        .astype(jnp.float32)
        .astype(bf16)
    )
    query_grad_low = grad_query.transpose(2, 0, 1, 3).reshape(seq_rows, batch_rows, D).astype(bf16)
    d_projected = jnp.concatenate([query_grad_low, kv_grad_low], axis=-1)
    d_bias_query = jnp.sum(query_grad_low.astype(f32), axis=(0, 1))
    d_bias_value = jnp.sum(kv_grad_low[..., D:].astype(f32), axis=(0, 1))
    grad_qkv = jnp.einsum("sbd,sbe->de", normed_one_low, d_projected, preferred_element_type=f32)
    d_normed_one = jnp.einsum("sbe,de->sbd", d_projected, qkv_low, preferred_element_type=f32)
    d_input_part, d_gain_one, d_shift_one = norm_one_back(d_normed_one)
    input_grad = (d_resid_one + d_input_part).astype(bf16)
    grad_list = [
        d_gain_one,
        d_shift_one,
        grad_qkv,
        d_bias_query,
        d_bias_value,
        grad_out_w,
        d_bias_out,
        d_gain_two,
        d_shift_two,
        grad_up,
        d_bias_up,
        grad_down,
        d_bias_down,
    ]
    total_rows = params.shape[0]
    used = sum((math.prod(extent) for extent in param_extents(D, FF)))
    flat_grads = jnp.concatenate(
        [grad_piece.reshape(-1) for grad_piece in grad_list]
        + [jnp.zeros((total_rows * 128 - used,), f32)]
    ).reshape(total_rows, 128)
    shard_rows = first_moment.shape[0]
    first_row = lax.axis_index(("dp", "seq")) * shard_rows
    core = lax.axis_index("seq") % 2
    plane_rows = 8 * shard_rows
    own_plane = lax.axis_index("dp") // 2
    window = core_window(shard_rows)
    low_grads = rounded(flat_grads)
    summed = jnp.zeros((window, LANES), bf16)
    for plane in reversed(range(total_rows // plane_rows)):
        piece = low_grads[plane * plane_rows : (plane + 1) * plane_rows]
        part = reduce_up(reduce_plane(piece, shard_rows), plane)
        summed = jnp.where(own_plane == plane, part, summed)
    summed = pl.pallas_call(copy_body, out_shape=jax.ShapeDtypeStruct(summed.shape, bf16))(summed)
    summed = summed.astype(f32)
    summed = jnp.where(core == 0, summed[:shard_rows], summed[window - shard_rows :])
    grads_mean = summed / lax.axis_size(("dp", "seq"))
    bias_down_grad = lax.psum(d_bias_down, ("dp", "seq")) / lax.axis_size(("dp", "seq"))
    own_params = lax.dynamic_slice_in_dim(params, first_row, shard_rows, 0)
    new_first = first_decay * first_moment + (1.0 - first_decay) * grads_mean
    new_second = second_decay * second_moment + (1.0 - second_decay) * grads_mean * grads_mean
    fix_one = 1.0 - first_decay**STEP
    fix_two = 1.0 - second_decay**STEP
    update = new_first / fix_one / (jnp.sqrt(new_second / fix_two) + adam_epsilon)
    new_params = own_params - rate_table(first_row, shard_rows, D, FF) * update
    return (block_output, input_grad, new_params, new_first, new_second, bias_down_grad)


def solution(mesh):
    return jax.shard_map(
        shards,
        mesh=mesh,
        in_specs=(
            P("seq", "dp", None),
            P("seq", "dp", None),
            P("seq", "dp"),
            P(None, "dp"),
            P(),
            P(("dp", "seq"), None),
            P(("dp", "seq"), None),
        ),
        out_specs=(
            P("seq", "dp", None),
            P("seq", "dp", None),
            P(("dp", "seq"), None),
            P(("dp", "seq"), None),
            P(("dp", "seq"), None),
            P(),
        ),
        check_vma=False,
    )
```

```python
from functools import partial
import math

import jax
import jax.numpy as jnp
from jax import lax
from jax.experimental import pallas as pl
from jax.experimental.pallas import tpu as pltpu
from jax.sharding import PartitionSpec as P

D = 768
HEADS = 12
HEAD_DIM = 64
FF = 3072
STEP = 4
LANES = 128
BLK = 256

norm_epsilon = 1e-05
branch_scale = 48.0 ** (-0.5)
first_decay = 0.9
second_decay = 0.95
adam_epsilon = 1e-08
base_rate = 0.1
masked_score = -1e30
LOG2E = 1.4426950408889634
score_factor = LOG2E / HEAD_DIM

f32 = jnp.float32
bf16 = jnp.bfloat16

ROW_G1, ROW_S1 = 0, 6
ROW_QKV = 12
ROW_BQ = ROW_QKV + D * 3 * D // LANES
ROW_BV = ROW_BQ + 6
ROW_WO = ROW_BV + 6
ROW_BO = ROW_WO + D * D // LANES
ROW_G2, ROW_S2 = ROW_BO + 6, ROW_BO + 12
ROW_FC = ROW_BO + 18
ROW_BFC = ROW_FC + D * FF // LANES
ROW_PR = ROW_BFC + FF // LANES
ROW_BPR = ROW_PR + D * FF // LANES
ROW_END = ROW_BPR + 6

VMEM = 56 * 1024 * 1024


def params_of(limit=VMEM):
    return pltpu.CompilerParams(vmem_limit_bytes=limit)


def down16(row):
    return row // 16 * 16


def unpack_body(x_ref, o_ref, *, shift, rows, blocks):
    for j in range(blocks):
        o_ref[:, j * LANES : (j + 1) * LANES] = x_ref[
            pl.ds(shift + j, rows, stride=blocks), :
        ].astype(bf16)


def unpack_matrix(params, row, rows, columns, chunk):
    blocks = columns // LANES
    base = row // 8 * 8
    shift = row - base
    size = chunk * blocks
    return pl.pallas_call(
        partial(unpack_body, shift=shift, rows=chunk, blocks=blocks),
        grid=(rows // chunk,),
        in_specs=[
            pl.BlockSpec(
                (pl.Element(size + 8), pl.Element(LANES)), lambda i: (pl.multiple_of(base + i * size, 8), 0)
            )
        ],
        out_specs=pl.BlockSpec((chunk, columns), lambda i: (i, 0)),
        out_shape=jax.ShapeDtypeStruct((rows, columns), bf16),
        compiler_params=params_of(),
    )(params)


def grad_body(a_ref, b_ref, o_ref, hold, *, shift, rows, blocks, chunks):
    step = pl.program_id(0)
    size = rows * blocks

    @pl.when(step == 0)
    def _():
        hold[pl.ds(0, 16), :] = jnp.zeros((16, LANES), f32)

    @pl.when(step > 0)
    def _():
        hold[pl.ds(0, 16), :] = hold[pl.ds(size, 16), :]

    @pl.when(step < chunks)
    def _():
        product = lax.dot_general(
            a_ref[...], b_ref[...], (((0,), (0,)), ((), ())), preferred_element_type=f32
        )
        for j in range(blocks):
            hold[pl.ds(shift + j, rows, stride=blocks), :] = product[
                :, j * LANES : (j + 1) * LANES
            ]
        o_ref[...] = hold[pl.ds(0, size), :].astype(bf16)

    @pl.when(step == chunks)
    def _():
        row = lax.broadcasted_iota(jnp.int32, (16, LANES), 0)
        o_ref[...] = jnp.zeros_like(o_ref)
        o_ref[pl.ds(0, 16), :] = jnp.where(row < shift, hold[pl.ds(0, 16), :], 0.0).astype(bf16)


def weight_grad(a, b, row, window_end, chunk=128):
    tokens, rows = a.shape
    columns = b.shape[1]
    blocks = columns // LANES
    base = down16(row)
    chunks = rows // chunk
    size = chunk * blocks
    return pl.pallas_call(
        partial(grad_body, shift=row - base, rows=chunk, blocks=blocks, chunks=chunks),
        grid=(chunks + 1,),
        in_specs=[
            pl.BlockSpec((tokens, chunk), lambda i: (0, jnp.minimum(i, chunks - 1))),
            pl.BlockSpec((tokens, columns), lambda i: (0, 0)),
        ],
        out_specs=pl.BlockSpec((size, LANES), lambda i: (i, 0)),
        out_shape=jax.ShapeDtypeStruct((window_end - base, LANES), bf16),
        scratch_shapes=[pltpu.VMEM((size + 16, LANES), f32)],
        compiler_params=params_of(),
    )(a, b)


nt_dims = (((1,), (1,)), ((), ()))
nn_dims = (((1,), (0,)), ((), ()))


def dot(a, b, dims=nn_dims):
    return lax.dot_general(a, b, dims, preferred_element_type=f32)


def head_lanes(value, odd):
    lane = lax.broadcasted_iota(jnp.int32, value.shape, 1)
    keep = (lane >= HEAD_DIM) if odd else (lane < HEAD_DIM)
    return jnp.where(keep, value, jnp.zeros_like(value))


def for_blocks(place_ref, seg_ref, segk_ref, segq_ref, bias_ref, i, step):
    q_start = place_ref[i]
    k_base = place_ref[2]
    count = place_ref[3 + i]
    q_first = seg_ref[0, q_start]
    q_last = seg_ref[0, q_start + BLK - 1]

    def visit(n, carry):
        kb = count - 1 - n
        k_start = k_base + kb * BLK
        k_first = seg_ref[0, k_start]
        k_last = seg_ref[0, k_start + BLK - 1]
        active = k_last >= q_first
        plain = (k_first == q_last) & (k_start + BLK <= q_start)

        @pl.when(active & plain)
        def _():
            step(kb, False)

        @pl.when(active & jnp.logical_not(plain))
        def _():
            k_pos = k_start + lax.broadcasted_iota(jnp.int32, (BLK, BLK), 0)
            q_pos = q_start + lax.broadcasted_iota(jnp.int32, (BLK, BLK), 1)
            same = segk_ref[pl.ds(k_start, BLK), :] == segq_ref[:, i * BLK : (i + 1) * BLK]
            bias_ref[...] = jnp.where((k_pos <= q_pos) & same, 0.0, masked_score)
            step(kb, True)

        return carry

    lax.fori_loop(0, count, visit, 0)


ACC = HEAD_DIM + 16


def attend_body(
    place_ref, seg_ref, segk_ref, segq_ref, q_ref, k_ref, vt_ref, *refs, first, last
):
    if first:
        acc_ref, top_ref, bias_ref = refs
    elif last:
        acc_in, top_in, out_ref, total_ref, bias_ref, acc_ref, top_ref = refs
    if first:
        acc_ref[...] = jnp.zeros_like(acc_ref)
        top_ref[...] = jnp.full_like(top_ref, masked_score)
    else:
        acc_ref[...] = acc_in[...]
        top_ref[...] = top_in[...]
    ones = jnp.ones((16, BLK), bf16)
    for i in range(2):
        cols = slice(i * BLK, (i + 1) * BLK)

        def step(kb, masked):
            k_rows = pl.ds(pl.multiple_of(kb * BLK, BLK), BLK)
            for pair in range(HEADS // 2):
                lanes = slice(pair * LANES, (pair + 1) * LANES)
                k_pair = k_ref[k_rows, lanes]
                q_pair = q_ref[cols, lanes]
                for odd in range(2):
                    h = 2 * pair + odd
                    s = dot(k_pair, head_lanes(q_pair, odd), nt_dims) * score_factor
                    if masked:
                        s = s + bias_ref[...]
                    old = top_ref[h : h + 1, cols]
                    new = jnp.maximum(old, jnp.max(s, axis=0, keepdims=True))
                    p = jnp.exp2(s - new).astype(bf16)
                    v_part = jnp.concatenate(
                        [vt_ref[h * HEAD_DIM : (h + 1) * HEAD_DIM, k_rows], ones], axis=0
                    )
                    part = dot(v_part, p)
                    acc_ref[h, :, cols] = acc_ref[h, :, cols] * jnp.exp2(old - new) + part
                    top_ref[h : h + 1, cols] = new

        for_blocks(place_ref, seg_ref, segk_ref, segq_ref, bias_ref, i, step)
    if last:
        for h in range(HEADS):
            total = acc_ref[h, HEAD_DIM : HEAD_DIM + 1, :]
            out_ref[h * HEAD_DIM : (h + 1) * HEAD_DIM, :] = acc_ref[h, :HEAD_DIM, :] / total
            total_ref[h : h + 1, :] = top_ref[h : h + 1, :] + jnp.log2(total)


smem = pl.BlockSpec(memory_space=pltpu.SMEM)
vmem = pl.BlockSpec(memory_space=pltpu.VMEM)


def attend(place, seg, segk, segq, q, k, vt, state=None):
    count = q.shape[0]
    first = state is None
    acc_shape = jax.ShapeDtypeStruct((HEADS, ACC, count), f32)
    row_shape = jax.ShapeDtypeStruct((16, count), f32)
    scratch = [pltpu.VMEM((BLK, BLK), f32)]
    if first:
        outs = (acc_shape, row_shape)
    else:
        outs = (jax.ShapeDtypeStruct((D, count), f32), row_shape)
        scratch += [pltpu.VMEM((HEADS, ACC, count), f32), pltpu.VMEM((16, count), f32)]
    extra = () if first else state
    return pl.pallas_call(
        partial(attend_body, first=first, last=not first),
        in_specs=[smem, smem] + [vmem] * (5 + len(extra)),
        out_specs=(vmem, vmem),
        out_shape=outs,
        scratch_shapes=scratch,
        compiler_params=params_of(),
    )(place, seg, segk, segq, q, k, vt, *extra)


def attend_back_body(
    place_ref,
    seg_ref,
    segk_ref,
    segq_ref,
    q_ref,
    k_ref,
    kt_ref,
    v_ref,
    do_ref,
    total_ref,
    delta_ref,
    dqt_in,
    dqt_ref,
    dk_ref,
    dv_ref,
    bias_ref,
    dk_acc,
    dv_acc,
):
    dqt_ref[...] = dqt_in[...]
    dk_acc[...] = jnp.zeros_like(dk_acc)
    dv_acc[...] = jnp.zeros_like(dv_acc)
    for i in range(2):
        cols = slice(i * BLK, (i + 1) * BLK)

        def step(kb, masked):
            k_rows = pl.ds(pl.multiple_of(kb * BLK, BLK), BLK)
            for pair in range(HEADS // 2):
                lanes = slice(pair * LANES, (pair + 1) * LANES)
                k_pair = k_ref[k_rows, lanes]
                v_pair = v_ref[k_rows, lanes]
                q_pair = q_ref[cols, lanes]
                do_pair = do_ref[cols, lanes]
                dk = jnp.zeros((BLK, LANES), f32)
                dv = jnp.zeros((BLK, LANES), f32)
                for odd in range(2):
                    h = 2 * pair + odd
                    head = slice(h * HEAD_DIM, (h + 1) * HEAD_DIM)
                    q_head = head_lanes(q_pair, odd)
                    do_head = head_lanes(do_pair, odd)
                    s = dot(k_pair, q_head, nt_dims) * score_factor
                    if masked:
                        s = s + bias_ref[...]
                    p = jnp.exp2(s - total_ref[h : h + 1, cols])
                    da = dot(v_pair, do_head, nt_dims)
                    ds = (p * (da - delta_ref[h : h + 1, cols])).astype(bf16)
                    dv = dv + dot(p.astype(bf16), do_head)
                    dk = dk + dot(ds, q_head)
                    dqt_ref[head, cols] += dot(kt_ref[head, k_rows], ds)
                dk_acc[k_rows, lanes] += dk
                dv_acc[k_rows, lanes] += dv

        for_blocks(place_ref, seg_ref, segk_ref, segq_ref, bias_ref, i, step)
    dk_ref[...] = (dk_acc[...] * (1.0 / HEAD_DIM)).astype(bf16)
    dv_ref[...] = dv_acc[...].astype(bf16)


def attend_back(place, seg, segk, segq, q, k, kt, v, do, total, delta, dqt):
    keys = k.shape[0]
    return pl.pallas_call(
        attend_back_body,
        in_specs=[smem, smem] + [vmem] * 10,
        out_specs=(vmem, vmem, vmem),
        out_shape=(
            jax.ShapeDtypeStruct(dqt.shape, f32),
            jax.ShapeDtypeStruct((keys, D), bf16),
            jax.ShapeDtypeStruct((keys, D), bf16),
        ),
        scratch_shapes=[
            pltpu.VMEM((BLK, BLK), f32),
            pltpu.VMEM((keys, D), f32),
            pltpu.VMEM((keys, D), f32),
        ],
        compiler_params=params_of(),
    )(place, seg, segk, segq, q, k, kt, v, do, total, delta, dqt)


def rounded(value):
    return lax.reduce_precision(value, 8, 7).astype(bf16)


def norm_parts(values):
    center = values - jnp.mean(values, axis=-1, keepdims=True)
    spread = jnp.mean(center * center, axis=-1, keepdims=True)
    rstd = lax.rsqrt(spread + norm_epsilon)
    return center * rstd, rstd


def norm_back(unit, rstd, gain, grad):
    scaled = grad * gain
    return rstd * (
        scaled
        - jnp.mean(scaled, axis=-1, keepdims=True)
        - unit * jnp.mean(scaled * unit, axis=-1, keepdims=True)
    )


def bit_pairs(size, bit, sender=lambda place: True):
    return [(n, n ^ bit) for n in range(size) if sender(n)]


def swap(value, axis, bit):
    return lax.ppermute(value, axis, bit_pairs(lax.axis_size(axis), bit))


def halves(value, axis, which):
    size = value.shape[axis] // 2
    own = lax.dynamic_slice_in_dim(value, which * size, size, axis)
    other = lax.dynamic_slice_in_dim(value, (1 - which) * size, size, axis)
    return own, other


def add(a, b):
    return rounded(a.astype(f32) + b.astype(f32))


def core_window(shard_rows):
    return (shard_rows + 15) // 16 * 16


def reduce_plane(piece, shard_rows):
    core = lax.axis_index("seq") % 2
    x = lax.axis_index("seq") // 2
    y = lax.axis_index("dp") % 2
    window = core_window(shard_rows)
    blocks = piece.reshape(2, 2, 2 * shard_rows, LANES)
    first, second = blocks[:, :, :window], blocks[:, :, 2 * shard_rows - window :]
    own = jnp.where(core == 0, first, second)
    other = jnp.where(core == 0, second, first)
    blocks = add(own, swap(other, "seq", 1))
    cut = window // 32 * 16
    one, two = blocks[:, :, :cut], blocks[:, :, cut:]
    own_one, other_one = halves(one, 1, x)
    own_two, other_two = halves(two, 0, y)
    got_one, got_two = swap(other_one, "seq", 2), swap(other_two, "dp", 1)
    one, two = add(own_one, got_one), add(own_two, got_two)
    own_one, other_one = halves(one, 0, y)
    own_two, other_two = halves(two, 1, x)
    got_one, got_two = swap(other_one, "dp", 1), swap(other_two, "seq", 2)
    one, two = add(own_one, got_one), add(own_two, got_two)
    return jnp.concatenate([one, two], axis=2).reshape(window, LANES)


def reduce_up(part, plane):
    size = lax.axis_size("dp")
    bit = 1
    while bit < size // 2:

        def sender(n):
            z = n // 2
            return (z ^ plane) & bit != 0 and (z ^ plane) & (bit - 1) == 0

        part = add(part, lax.ppermute(part, "dp", bit_pairs(size, 2 * bit, sender)))
        bit *= 2
    return part


def vector(params, row, rows=6):
    return params[row : row + rows].reshape(1, rows * LANES)


def shards(tokens, cotangent, loss_mask, segments, params, first_moment, second_moment):
    block = tokens.shape[0]
    seq_index = lax.axis_index("seq")
    core = seq_index % 2
    x = seq_index // 2
    shard_rows = first_moment.shape[0]
    total_rows = params.shape[0]
    chip = 2 * block

    def chip_rows(value):
        other = swap(value, "seq", 1)
        return jnp.concatenate(
            [jnp.where(core == 0, value, other), jnp.where(core == 0, other, value)]
        )

    def pick(value):
        return jnp.concatenate(
            [
                lax.dynamic_slice_in_dim(value, core * BLK, BLK, 0),
                lax.dynamic_slice_in_dim(value, (3 - core) * BLK, BLK, 0),
            ]
        )

    def unpick(value):
        low, high = value[:BLK], value[BLK:]
        got = swap(jnp.where(core == 0, high, low), "seq", 1)
        return jnp.where(
            core == 0, jnp.concatenate([low, got]), jnp.concatenate([high, got])
        )

    own_tokens = tokens.reshape(block, D)
    near_low = chip_rows(own_tokens)
    far_low = chip_rows(swap(own_tokens, "seq", 2))
    grad_out = cotangent.reshape(block, D).astype(f32) * loss_mask.astype(f32)
    grad_low = (grad_out).astype(bf16)
    grad_out = pick(chip_rows(grad_low)).astype(f32)

    w_qkv = unpack_matrix(params, ROW_QKV, D, 3 * D, 64)
    w_out = unpack_matrix(params, ROW_WO, D, D, 128)
    w_up = unpack_matrix(params, ROW_FC, D, FF, 64)
    w_down = unpack_matrix(params, ROW_PR, FF, D, 256)
    gain_one, shift_one = vector(params, ROW_G1), vector(params, ROW_S1)
    bias_query, bias_value = vector(params, ROW_BQ), vector(params, ROW_BV)
    bias_out = vector(params, ROW_BO)
    gain_two, shift_two = vector(params, ROW_G2), vector(params, ROW_S2)
    bias_up = vector(params, ROW_BFC, 24)
    bias_down = vector(params, ROW_BPR)

    seg_row = segments.reshape(1, -1)
    seg_col = segments.reshape(-1, 1)
    q_place = x * chip + jnp.stack([core * BLK, (3 - core) * BLK])
    near_place = jnp.concatenate(
        [q_place, jnp.stack([x * chip, core + 1, 4 - core])]
    ).astype(jnp.int32)
    far_place = jnp.concatenate([q_place, jnp.stack([x * 0, 4 * x, 4 * x])]).astype(jnp.int32)
    segq = jnp.concatenate(
        [lax.dynamic_slice_in_dim(seg_row, q_place[n], BLK, 1) for n in range(2)], axis=1
    )

    unit_near, rstd_near = norm_parts(near_low.astype(f32))
    near_n = rounded(unit_near * gain_one + shift_one)
    unit_far, rstd_far = norm_parts(far_low.astype(f32))
    far_n = rounded(unit_far * gain_one + shift_one)
    query_n = pick(near_n)
    wq, wk, wv = w_qkv[:, :D], w_qkv[:, D : 2 * D], w_qkv[:, 2 * D :]
    queries = rounded(dot(query_n, wq) + bias_query)

    def keys_values(normed):
        keys = rounded(dot(normed, wk))
        values = rounded(dot(normed, wv) + bias_value)
        return keys, values

    near_k, near_v = keys_values(near_n)
    far_k, far_v = keys_values(far_n)
    state = attend(near_place, seg_row, seg_col, segq, queries, near_k, near_v.T)
    out_t, total = attend(
        far_place, seg_row, seg_col, segq, queries, far_k, far_v.T, state
    )
    attn_low = rounded(out_t.T)
    resid_one = pick(near_low).astype(f32) + branch_scale * (dot(attn_low, w_out) + bias_out)
    unit_two, rstd_two = norm_parts(resid_one)
    two_n = rounded(unit_two * gain_two + shift_two)
    up_proj = dot(two_n, w_up) + bias_up
    active, gelu_back = jax.vjp(partial(jax.nn.gelu, approximate=True), up_proj)
    active_low = rounded(active)
    block_output = unpick(
        rounded(resid_one + branch_scale * (dot(active_low, w_down) + bias_down))
    )

    d_mlp = rounded(branch_scale * grad_out)
    d_up = rounded(gelu_back(dot(d_mlp, w_down, nt_dims))[0])
    part_down = weight_grad(active_low, d_mlp, ROW_PR, total_rows, 256)
    part_up = weight_grad(two_n, d_up, ROW_FC, down16(ROW_PR))
    d_two = dot(d_up, w_up, nt_dims)
    d_resid = grad_out + norm_back(unit_two, rstd_two, gain_two, d_two)
    d_attn = rounded(branch_scale * d_resid)
    part_out = weight_grad(attn_low, d_attn, ROW_WO, down16(ROW_FC))
    d_heads = rounded(dot(d_attn, w_out, nt_dims))
    d_heads_t = rounded(dot(w_out, d_attn, nt_dims))

    delta = jnp.sum(
        (d_heads_t.astype(f32) * out_t).reshape(HEADS, HEAD_DIM, block), axis=1
    )
    delta = jnp.concatenate([delta, jnp.zeros((4, block), f32)])
    no_grad = jnp.zeros((D, block), f32)
    dq_t, far_dk, far_dv = attend_back(
        far_place, seg_row, seg_col, segq, queries, far_k, far_k.T, far_v, d_heads, total,
        delta, no_grad,
    )
    dq_t, near_dk, near_dv = attend_back(
        near_place, seg_row, seg_col, segq, queries, near_k, near_k.T, near_v, d_heads, total,
        delta, dq_t,
    )
    d_query = rounded((dq_t * (1.0 / HEAD_DIM)).T)
    zero_block = jnp.zeros((BLK, D), bf16)
    low, high = d_query[:BLK], d_query[BLK:]
    near_dq = jnp.where(
        core == 0,
        jnp.concatenate([low, zero_block, zero_block, high]),
        jnp.concatenate([zero_block, low, high, zero_block]),
    )
    near_dp = jnp.concatenate([near_dq, near_dk, near_dv], axis=1)
    far_dp = jnp.concatenate([jnp.zeros((chip, D), bf16), far_dk, far_dv], axis=1)
    all_n = jnp.concatenate([near_n, far_n])
    all_dp = jnp.concatenate([near_dp, far_dp])
    part_qkv = weight_grad(all_n, all_dp, ROW_QKV, down16(ROW_WO))
    d_near = dot(near_dp, w_qkv, nt_dims)
    d_far = dot(far_dp, w_qkv, nt_dims)
    d_bias_query = jnp.sum(d_query.astype(f32), axis=0)
    d_bias_value = jnp.sum(near_dv.astype(f32), axis=0) + jnp.sum(far_dv.astype(f32), axis=0)
    d_gain_one = jnp.sum(d_near * unit_near, axis=0) + jnp.sum(d_far * unit_far, axis=0)
    d_shift_one = jnp.sum(d_near, axis=0) + jnp.sum(d_far, axis=0)

    far_in = norm_back(unit_far, rstd_far, gain_one, d_far)
    near_in = norm_back(unit_near, rstd_near, gain_one, d_near)
    own, other = halves(far_in, 0, core)
    far_sum = own + swap(rounded(other), "seq", 1).astype(f32)
    from_far = swap(rounded(far_sum), "seq", 2)
    from_far = jnp.where(x == 0, from_far, jnp.zeros_like(from_far))
    zero_wide = jnp.zeros((BLK, D), f32)
    low, high = d_resid[:BLK], d_resid[BLK:]
    near_in = near_in + jnp.where(
        core == 0,
        jnp.concatenate([low, zero_wide, zero_wide, high]),
        jnp.concatenate([zero_wide, low, high, zero_wide]),
    )
    own, other = halves(near_in, 0, core)
    input_grad = rounded(own + swap(rounded(other), "seq", 1).astype(f32) + from_far.astype(f32))

    column_sums = [
        d_gain_one,
        d_shift_one,
        d_bias_query,
        d_bias_value,
        jnp.sum(d_attn.astype(f32), axis=0),
        jnp.sum(d_two * unit_two, axis=0),
        jnp.sum(d_two, axis=0),
        jnp.sum(d_up.astype(f32), axis=0),
        jnp.sum(d_mlp.astype(f32), axis=0),
    ]
    runs = [(ROW_G1, 12), (ROW_BQ, 12), (ROW_BO, 18), (ROW_BFC, 24), (ROW_BPR, 6)]
    vectors = lax.psum(jnp.concatenate(column_sums).reshape(-1, LANES), ("dp", "seq"))

    windows = [part_qkv, part_out, part_up, part_down]
    starts = [0, down16(ROW_WO), down16(ROW_FC), down16(ROW_PR)]
    plane_rows = 8 * shard_rows
    own_plane = lax.axis_index("dp") // 2
    window = core_window(shard_rows)
    summed = jnp.zeros((window, LANES), bf16)
    for plane in reversed(range(total_rows // plane_rows)):
        begin, end = plane * plane_rows, (plane + 1) * plane_rows
        pieces = [
            rows[max(begin - start, 0) : end - start]
            for rows, start in zip(windows, starts)
            if start < end and start + rows.shape[0] > begin
        ]
        piece = jnp.concatenate(pieces) if len(pieces) > 1 else pieces[0]
        part = reduce_up(reduce_plane(piece, shard_rows), plane)
        summed = jnp.where(own_plane == plane, part, summed)

    summed = summed.astype(f32)
    summed = jnp.where(core == 0, summed[:shard_rows], summed[window - shard_rows :])
    device_count = lax.axis_size(("dp", "seq"))
    first_row = lax.axis_index(("dp", "seq")) * shard_rows
    margin = 24
    spread = jnp.zeros((shard_rows + 2 * margin, LANES), f32)
    at = 0
    for row, count in runs:
        place = jnp.clip(row - first_row + margin, 0, shard_rows + margin)
        spread = lax.dynamic_update_slice(spread, vectors[at : at + count], (place, 0))
        at += count
    grads_mean = (summed + spread[margin : margin + shard_rows]) / device_count
    bias_down_grad = vectors[-6:].reshape(-1) / device_count
    own_params = lax.dynamic_slice_in_dim(params, first_row, shard_rows, 0)
    new_first = first_decay * first_moment + (1.0 - first_decay) * grads_mean
    new_second = second_decay * second_moment + (1.0 - second_decay) * grads_mean * grads_mean
    fix_one = 1.0 - first_decay**STEP
    fix_two = 1.0 - second_decay**STEP
    update = new_first / fix_one / (jnp.sqrt(new_second / fix_two) + adam_epsilon)
    row = first_row + lax.broadcasted_iota(jnp.int32, (shard_rows, LANES), 0)
    in_matrix = jnp.zeros(row.shape, bool)
    for start, end in (
        (ROW_QKV, ROW_BQ),
        (ROW_WO, ROW_BO),
        (ROW_FC, ROW_BFC),
        (ROW_PR, ROW_BPR),
    ):
        in_matrix = in_matrix | ((row >= start) & (row < end))
    new_params = own_params - jnp.where(in_matrix, base_rate / D, base_rate) * update
    return (
        block_output.reshape(tokens.shape),
        input_grad.reshape(tokens.shape),
        new_params,
        new_first,
        new_second,
        bias_down_grad,
    )


def solution(mesh):
    return jax.shard_map(
        shards,
        mesh=mesh,
        in_specs=(
            P("seq", "dp", None),
            P("seq", "dp", None),
            P("seq", "dp"),
            P(None, "dp"),
            P(),
            P(("dp", "seq"), None),
            P(("dp", "seq"), None),
        ),
        out_specs=(
            P("seq", "dp", None),
            P("seq", "dp", None),
            P(("dp", "seq"), None),
            P(("dp", "seq"), None),
            P(("dp", "seq"), None),
            P(),
        ),
        check_vma=False,
    )
```

```python
from functools import partial
import math

import jax
import jax.numpy as jnp
from jax import lax
from jax.experimental import pallas as pl
from jax.experimental.pallas import tpu as pltpu
from jax.sharding import PartitionSpec as P

D = 768
HEADS = 12
HEAD_DIM = 64
FF = 3072
STEP = 4
LANES = 128
BLK = 256

norm_epsilon = 1e-05
branch_scale = 48.0 ** (-0.5)
first_decay = 0.9
second_decay = 0.95
adam_epsilon = 1e-08
base_rate = 0.1
masked_score = -1e30
LOG2E = 1.4426950408889634
score_factor = LOG2E / HEAD_DIM

f32 = jnp.float32
bf16 = jnp.bfloat16

ROW_G1, ROW_S1 = 0, 6
ROW_QKV = 12
ROW_BQ = ROW_QKV + D * 3 * D // LANES
ROW_BV = ROW_BQ + 6
ROW_WO = ROW_BV + 6
ROW_BO = ROW_WO + D * D // LANES
ROW_G2, ROW_S2 = ROW_BO + 6, ROW_BO + 12
ROW_FC = ROW_BO + 18
ROW_BFC = ROW_FC + D * FF // LANES
ROW_PR = ROW_BFC + FF // LANES
ROW_BPR = ROW_PR + D * FF // LANES
ROW_END = ROW_BPR + 6

VMEM = 56 * 1024 * 1024


nt_dims = (((1,), (1,)), ((), ()))
nn_dims = (((1,), (0,)), ((), ()))
tn_dims = (((0,), (0,)), ((), ()))

smem = pl.BlockSpec(memory_space=pltpu.SMEM)
vmem = pl.BlockSpec(memory_space=pltpu.VMEM)
anywhere = pl.BlockSpec(memory_space=pl.ANY)


def params_of(limit=VMEM):
    return pltpu.CompilerParams(vmem_limit_bytes=limit)


def cost(flops, moved):
    return pl.CostEstimate(flops=int(flops), bytes_accessed=int(moved), transcendentals=0)


def dot(a, b, dims=nn_dims):
    return lax.dot_general(a, b, dims, preferred_element_type=f32)


def iota(shape, axis):
    return lax.broadcasted_iota(jnp.int32, shape, axis)


def down16(row):
    return row // 16 * 16


def group_rows(blocks):
    return 16 if blocks > 8 else 32


def unpack_body(x_ref, o_ref, move, *, shift, rows, blocks, pairs):
    size = rows * blocks
    bits = rows.bit_length() - 1

    @pl.when(pl.program_id(0) == 0)
    def _():
        to, come = iota(move.shape, 0), iota(move.shape, 1)
        move[...] = (come == shift + (to & (rows - 1)) * blocks + (to >> bits)).astype(bf16)

    for n in range(pairs):
        both = jnp.concatenate(
            [x_ref[pl.ds((2 * n + side) * size, size + 16), :].astype(bf16) for side in (0, 1)],
            axis=1,
        )
        moved = dot(move[...], both).astype(bf16)
        for side in (0, 1):
            for j in range(blocks):
                o_ref[
                    (2 * n + side) * rows : (2 * n + side + 1) * rows,
                    j * LANES : (j + 1) * LANES,
                ] = moved[j * rows : (j + 1) * rows, side * LANES : (side + 1) * LANES]


def unpack_matrix(params, row, matrix_rows, columns, steps):
    blocks = columns // LANES
    rows = group_rows(blocks)
    base = row // 8 * 8
    chunk = matrix_rows // steps
    size = chunk * blocks
    return pl.pallas_call(
        partial(
            unpack_body, shift=row - base, rows=rows, blocks=blocks, pairs=chunk // rows // 2
        ),
        grid=(steps,),
        in_specs=[
            pl.BlockSpec(
                (pl.Element(size + 16), pl.Element(LANES)),
                lambda i: (pl.multiple_of(base + i * size, 8), 0),
            )
        ],
        out_specs=pl.BlockSpec((chunk, columns), lambda i: (i, 0)),
        out_shape=jax.ShapeDtypeStruct((matrix_rows, columns), bf16),
        scratch_shapes=[pltpu.VMEM((rows * blocks, rows * blocks + 16), bf16)],
        compiler_params=params_of(),
        cost_estimate=cost(2e9, 6 * matrix_rows * columns),
    )(params)


def grad_body(
    core_ref,
    *refs,
    products,
    vectors,
    rest,
    base,
    row,
    matrix_rows,
    columns,
    head,
    tail,
    planes,
    plane_rows,
    keep,
):
    refs = list(refs)
    factors = [refs.pop(0) for _ in range(2 * products)]
    vector_refs = [refs.pop(0) for _ in range(vectors)]
    rest_ref = refs.pop(0) if rest else None
    plane_refs = [(refs.pop(0), refs.pop(0)) for _ in planes]
    keep_ref = refs.pop(0) if keep else None
    window, grad, move, carry, last, sems = refs
    blocks = columns // LANES
    rows = group_rows(blocks)
    bits = rows.bit_length() - 1
    size = rows * blocks
    shift = row - base
    body_rows = matrix_rows * blocks
    tail_rows = last.shape[0]
    if rest:
        load = pltpu.make_async_copy(
            rest_ref, window.at[pl.ds(body_rows + tail_rows, rest), :], sems.at[0]
        )
        load.start()
    to, come = iota(move.shape, 0), iota(move.shape, 1)
    move[...] = (to == shift + (come & (rows - 1)) * blocks + (come >> bits)).astype(bf16)
    carry[...] = jnp.zeros_like(carry)
    last[...] = jnp.zeros_like(last)
    for place, n, start, count in head:
        carry[place : place + count, :] = vector_refs[n][start : start + count, :]
    for place, n, start, count in tail:
        last[place : place + count, :] = vector_refs[n][start : start + count, :]

    core = core_ref[0]

    def chunk(c, state):
        lanes = pl.ds(pl.multiple_of(c * LANES, LANES), LANES)
        grad[...] = dot(factors[0][:, lanes], factors[1][...], tn_dims).astype(bf16)
        if products == 2:

            @pl.when(core_ref[1] == 1)
            def _():
                wide = factors[3].shape[1]
                grad[:, columns - wide :] = (
                    dot(factors[0][:, lanes], factors[1][:, columns - wide :], tn_dims)
                    + dot(factors[2][:, lanes], factors[3][...], tn_dims)
                ).astype(bf16)

        for pair in range(LANES // rows // 2):
            both = jnp.concatenate(
                [
                    jnp.concatenate(
                        [
                            grad[
                                (2 * pair + side) * rows : (2 * pair + side + 1) * rows,
                                j * LANES : (j + 1) * LANES,
                            ]
                            for j in range(blocks)
                        ],
                        axis=0,
                    )
                    for side in (0, 1)
                ],
                axis=1,
            )
            moved = dot(move[...], both)
            for side in (0, 1):
                part = moved[:, side * LANES : (side + 1) * LANES]
                at = pl.multiple_of((c * (LANES // rows) + 2 * pair + side) * size, 16)
                window[pl.ds(at, 16), :] = (part[:16] + carry[...]).astype(bf16)
                window[pl.ds(at + 16, size - 16), :] = part[16:size].astype(bf16)
                carry[...] = part[size:]
        return state

    lax.fori_loop(0, matrix_rows // LANES, chunk, 0)
    last[pl.ds(0, 16), :] = last[pl.ds(0, 16), :] + carry[...]
    window[pl.ds(body_rows, tail_rows), :] = last[...].astype(bf16)
    if rest:
        load.wait()
    copies = []
    half = plane_rows // 4
    for plane, (own_ref, other_ref) in zip(planes, plane_refs):
        part_rows = own_ref.shape[1]
        for block in range(4):
            for ref, which in ((own_ref, core), (other_ref, 1 - core)):
                at = plane * plane_rows - base + block * half
                at = pl.multiple_of(at + which * (half - part_rows), 16)
                copies.append((window.at[pl.ds(at, part_rows), :], ref.at[block]))
    if keep:
        copies.append((window.at[pl.ds(0, keep), :], keep_ref))
    started = [
        pltpu.make_async_copy(source, target, sems.at[1 + n])
        for n, (source, target) in enumerate(copies)
    ]
    for copy in started:
        copy.start()
    for copy in started:
        copy.wait()


def weight_grad(place, products, vectors, rest, row, head, tail, shard_rows, top):
    base = down16(row)
    matrix_rows, columns = products[0][0].shape[1], products[0][1].shape[1]
    blocks = columns // LANES
    rows = group_rows(blocks)
    size = rows * blocks
    plane_rows = 8 * shard_rows
    rest_rows = 0 if rest is None else rest.shape[0]
    own_end = top - rest_rows
    tail_rows = own_end - base - matrix_rows * blocks
    first_plane = -(-base // plane_rows)
    planes = list(range(first_plane, top // plane_rows))
    keep = first_plane * plane_rows - base
    part_rows = core_window(shard_rows)
    part = jax.ShapeDtypeStruct((4, part_rows, LANES), bf16)
    out_shape = [part] * (2 * len(planes))
    if keep:
        out_shape.append(jax.ShapeDtypeStruct((keep, LANES), bf16))
    operands = [value for pair in products for value in pair] + list(vectors)
    specs = [smem] + [vmem] * len(operands)
    if rest_rows:
        operands.append(rest)
        specs.append(anywhere)
    tokens = sum(a.shape[0] for a, _ in products)
    outs = pl.pallas_call(
        partial(
            grad_body,
            products=len(products),
            vectors=len(vectors),
            rest=rest_rows,
            base=base,
            row=row,
            matrix_rows=matrix_rows,
            columns=columns,
            head=head,
            tail=tail,
            planes=planes,
            plane_rows=plane_rows,
            keep=keep,
        ),
        in_specs=specs,
        out_specs=[anywhere] * len(out_shape),
        out_shape=out_shape,
        scratch_shapes=[
            pltpu.VMEM((top - base, LANES), bf16),
            pltpu.VMEM((LANES, columns), bf16),
            pltpu.VMEM((size + 16, size), bf16),
            pltpu.VMEM((16, LANES), f32),
            pltpu.VMEM((tail_rows, LANES), f32),
            pltpu.SemaphoreType.DMA((2 + 8 * len(planes),)),
        ],
        compiler_params=params_of(),
        cost_estimate=cost(4 * tokens * matrix_rows * columns, 4 * matrix_rows * columns),
    )(place, *operands)
    pairs = {plane: (outs[2 * n], outs[2 * n + 1]) for n, plane in enumerate(planes)}
    return pairs, (outs[-1] if keep else None)


def row_mean(value):
    return jnp.sum(value, axis=-1, keepdims=True) * (1.0 / value.shape[-1])


def norm_parts(values):
    center = values - row_mean(values)
    rstd = lax.rsqrt(row_mean(center * center) + norm_epsilon)
    return center * rstd, rstd


def norm_back(unit, rstd, gain, grad):
    scaled = grad * gain
    return rstd * (scaled - row_mean(scaled) - unit * row_mean(scaled * unit))


def project_body(x_ref, gain_ref, shift_ref, bq_ref, bv_ref, w_ref, *outs, with_query):
    n_ref, k_ref, kt_ref, v_ref, vt_ref = outs[:5]
    unit, _ = norm_parts(x_ref[...].astype(f32))
    normed = (unit * gain_ref[...] + shift_ref[...]).astype(bf16)
    n_ref[...] = normed
    keys = dot(normed, w_ref[:, D : 2 * D]).astype(bf16)
    k_ref[...] = keys
    kt_ref[...] = keys.T
    values = (dot(normed, w_ref[:, 2 * D :]) + bv_ref[...]).astype(bf16)
    v_ref[...] = values
    vt_ref[...] = values.T
    if with_query:
        outs[5][...] = (dot(normed, w_ref[:, :D]) + bq_ref[...]).astype(bf16)


def project(x, gain, shift, bias_query, bias_value, w_qkv, with_query):
    count = x.shape[0]
    by_rows = pl.BlockSpec((BLK, D), lambda i: (i, 0))
    by_columns = pl.BlockSpec((D, BLK), lambda i: (0, i))
    row = pl.BlockSpec((1, D), lambda i: (0, 0))
    tall = jax.ShapeDtypeStruct((count, D), bf16)
    wide = jax.ShapeDtypeStruct((D, count), bf16)
    return pl.pallas_call(
        partial(project_body, with_query=with_query),
        grid=(count // BLK,),
        in_specs=[by_rows, row, row, row, row, pl.BlockSpec((D, 3 * D), lambda i: (0, 0))],
        out_specs=[by_rows, by_rows, by_columns, by_rows, by_columns] + [by_rows] * with_query,
        out_shape=[tall, tall, wide, tall, wide] + [tall] * with_query,
        compiler_params=params_of(),
        cost_estimate=cost(2 * count * D * (2 + with_query) * D, 12 * count * D),
    )(x, gain, shift, bias_query, bias_value, w_qkv)


def head_lanes(value, odd):
    lane = iota(value.shape, 1)
    keep = (lane >= HEAD_DIM) if odd else (lane < HEAD_DIM)
    return jnp.where(keep, value, jnp.zeros_like(value))


def visit_block(place_ref, seg_ref, segk_ref, segq_ref, bias_ref, i, k_start, valid, step):
    q_start = place_ref[i]
    q_first = seg_ref[0, q_start]
    q_last = seg_ref[0, q_start + BLK - 1]
    k_first = seg_ref[0, k_start]
    k_last = seg_ref[0, k_start + BLK - 1]
    active = valid & (k_start <= q_start) & (k_last >= q_first)
    plain = (k_first == q_last) & (k_start + BLK <= q_start)

    @pl.when(active & plain)
    def _():
        step(False)

    @pl.when(active & jnp.logical_not(plain))
    def _():
        k_pos = k_start + iota((BLK, BLK), 0)
        q_pos = q_start + iota((BLK, BLK), 1)
        segk = segk_ref[pl.ds(pl.multiple_of(k_start, BLK), BLK), :]
        same = segk == segq_ref[:, i * BLK : (i + 1) * BLK]
        bias_ref[...] = jnp.where((k_pos <= q_pos) & same, 0.0, masked_score)
        step(True)


ACC = HEAD_DIM + 16


def attend_body(
    place_ref, seg_ref, segk_ref, segq_ref, q_ref, k_ref, vt_ref, *refs, first
):
    if first:
        acc_ref, top_ref, bias_ref, s_ref = refs
        acc_ref[...] = jnp.zeros_like(acc_ref)
        top_ref[...] = jnp.full_like(top_ref, masked_score)
    else:
        acc_in, top_in, out_ref, outt_ref, total_ref, bias_ref, s_ref, acc_ref, top_ref = refs
        acc_ref[...] = acc_in[...]
        top_ref[...] = top_in[...]
    ones = jnp.ones((16, BLK), bf16)
    count = k_ref.shape[0] // BLK
    x = place_ref[3]
    base = x * (count * BLK) if first else 0 * x
    valid = (x >= 0) if first else (x == 1)
    for i in range(2):
        cols = slice(i * BLK, (i + 1) * BLK)

        def visit(n, carry):
            kb = count - 1 - n
            k_rows = pl.ds(pl.multiple_of(kb * BLK, BLK), BLK)
            q_rows = pl.ds(pl.multiple_of(place_ref[4 + i], BLK), BLK)

            def step(masked):
                tops = []
                for h in range(HEADS):
                    pair, odd = h // 2, h % 2
                    lanes = slice(pair * LANES, (pair + 1) * LANES)
                    s = dot(k_ref[k_rows, lanes], head_lanes(q_ref[q_rows, lanes], odd), nt_dims)
                    s = s * score_factor
                    if masked:
                        s = s + bias_ref[...]
                    s_ref[h] = s
                    tops.append(jnp.max(s, axis=0, keepdims=True))
                old = top_ref[:HEADS, cols]
                new = jnp.maximum(old, jnp.concatenate(tops, axis=0))
                top_ref[:HEADS, cols] = new
                scale = jnp.exp2(old - new)
                for h in range(HEADS):
                    p = jnp.exp2(s_ref[h] - new[h : h + 1]).astype(bf16)
                    v_part = jnp.concatenate(
                        [vt_ref[h * HEAD_DIM : (h + 1) * HEAD_DIM, k_rows], ones], axis=0
                    )
                    acc_ref[h, :, cols] = acc_ref[h, :, cols] * scale[h : h + 1] + dot(v_part, p)

            visit_block(
                place_ref, seg_ref, segk_ref, segq_ref, bias_ref, i, base + kb * BLK, valid, step
            )
            return carry

        lax.fori_loop(0, count, visit, 0)
    if not first:
        for h in range(HEADS):
            total = acc_ref[h, HEAD_DIM : HEAD_DIM + 1, :]
            outt_ref[h * HEAD_DIM : (h + 1) * HEAD_DIM, :] = acc_ref[h, :HEAD_DIM, :] / total
            total_ref[h : h + 1, :] = top_ref[h : h + 1, :] + jnp.log2(total)
        for i in range(2):
            cols = slice(i * BLK, (i + 1) * BLK)
            out_ref[cols, :] = outt_ref[:, cols].T.astype(bf16)


def attend(place, seg, segk, segq, q, k, vt, state=None):
    count = 2 * BLK
    first = state is None
    acc_shape = jax.ShapeDtypeStruct((HEADS, ACC, count), f32)
    row_shape = jax.ShapeDtypeStruct((16, count), f32)
    if first:
        outs = (acc_shape, row_shape)
    else:
        outs = (
            jax.ShapeDtypeStruct((count, D), bf16),
            jax.ShapeDtypeStruct((D, count), f32),
            row_shape,
        )
    extra = () if first else state
    held = [] if first else [pltpu.VMEM((HEADS, ACC, count), f32), pltpu.VMEM((16, count), f32)]
    return pl.pallas_call(
        partial(attend_body, first=first),
        in_specs=[smem, smem] + [vmem] * (5 + len(extra)),
        out_specs=(vmem,) * len(outs),
        out_shape=outs,
        scratch_shapes=[pltpu.VMEM((BLK, BLK), f32), pltpu.VMEM((HEADS, BLK, BLK), f32)] + held,
        compiler_params=params_of(),
        cost_estimate=cost(6e9, 8e6),
    )(place, seg, segk, segq, q, k, vt, *extra)


def attend_back_body(
    place_ref, seg_ref, segk_ref, segq_ref, q_ref, do_ref, total_ref, delta_ref,
    fk_ref, fkt_ref, fv_ref, nk_ref, nkt_ref, nv_ref,
    dnear_ref, dfar_ref, bias_ref, dqt_ref, dk_acc, dv_acc,
):
    dqt_ref[...] = jnp.zeros_like(dqt_ref)
    dnear_ref[...] = jnp.zeros_like(dnear_ref)
    count = nk_ref.shape[0] // BLK
    x = place_ref[3]
    chip = count * BLK

    def side(k_ref, kt_ref, v_ref, out_ref, at, base, valid):
        def visit(kb, carry):
            k_rows = pl.ds(pl.multiple_of(kb * BLK, BLK), BLK)
            dk_acc[...] = jnp.zeros_like(dk_acc)
            dv_acc[...] = jnp.zeros_like(dv_acc)
            for i in range(2):
                cols = slice(i * BLK, (i + 1) * BLK)
                q_rows = pl.ds(pl.multiple_of(place_ref[4 + i], BLK), BLK)

                def step(masked):
                    for pair in range(HEADS // 2):
                        lanes = slice(pair * LANES, (pair + 1) * LANES)
                        k_pair = k_ref[k_rows, lanes]
                        v_pair = v_ref[k_rows, lanes]
                        q_pair = q_ref[q_rows, lanes]
                        do_pair = do_ref[cols, lanes]
                        dk = jnp.zeros((BLK, LANES), f32)
                        dv = jnp.zeros((BLK, LANES), f32)
                        for odd in range(2):
                            h = 2 * pair + odd
                            head = slice(h * HEAD_DIM, (h + 1) * HEAD_DIM)
                            q_head = head_lanes(q_pair, odd)
                            do_head = head_lanes(do_pair, odd)
                            s = dot(k_pair, q_head, nt_dims) * score_factor
                            if masked:
                                s = s + bias_ref[...]
                            p = jnp.exp2(s - total_ref[h : h + 1, cols])
                            da = dot(v_pair, do_head, nt_dims)
                            ds = (p * (da - delta_ref[h : h + 1, cols])).astype(bf16)
                            dv = dv + dot(p.astype(bf16), do_head)
                            dk = dk + dot(ds, q_head)
                            dqt_ref[head, cols] += dot(kt_ref[head, k_rows], ds)
                        dk_acc[:, lanes] += dk
                        dv_acc[:, lanes] += dv

                visit_block(
                    place_ref, seg_ref, segk_ref, segq_ref, bias_ref, i, base + kb * BLK, valid,
                    step,
                )
            out_ref[k_rows, at : at + D] = (dk_acc[...] * (1.0 / HEAD_DIM)).astype(bf16)
            out_ref[k_rows, at + D : at + 2 * D] = dv_acc[...].astype(bf16)
            return carry

        lax.fori_loop(0, count, visit, 0)

    side(fk_ref, fkt_ref, fv_ref, dfar_ref, 0, 0 * x, x == 1)
    side(nk_ref, nkt_ref, nv_ref, dnear_ref, D, x * chip, x >= 0)
    for i in range(2):
        q_rows = pl.ds(pl.multiple_of(place_ref[4 + i], BLK), BLK)
        part = dqt_ref[:, i * BLK : (i + 1) * BLK] * (1.0 / HEAD_DIM)
        dnear_ref[q_rows, :D] = part.T.astype(bf16)


def attend_back(place, seg, segk, segq, q, do, total, delta, far, near):
    keys = q.shape[0]
    return pl.pallas_call(
        attend_back_body,
        in_specs=[smem, smem] + [vmem] * 12,
        out_specs=(vmem, vmem),
        out_shape=(
            jax.ShapeDtypeStruct((keys, 3 * D), bf16),
            jax.ShapeDtypeStruct((keys, 2 * D), bf16),
        ),
        scratch_shapes=[
            pltpu.VMEM((BLK, BLK), f32),
            pltpu.VMEM((D, 2 * BLK), f32),
            pltpu.VMEM((BLK, D), f32),
            pltpu.VMEM((BLK, D), f32),
        ],
        compiler_params=params_of(),
        cost_estimate=cost(25e9, 2e7),
    )(place, seg, segk, segq, q, do, total, delta, *far, *near)


GELU_A = math.sqrt(2.0 / math.pi)
GELU_B = 0.044715
FF_BLK = 512


def put_rows(ref, at, value):
    for j in range(value.shape[1] // LANES):
        ref[at + j : at + j + 1, :] = value[:, j * LANES : (j + 1) * LANES]


def column_sum(value):
    return jnp.sum(value, axis=0, keepdims=True)


def feed_body(
    place_ref, attn_ref, outt_ref, x_ref, dy_ref, wo_ref, bo_ref, g2_ref, s2_ref, wu_ref, bu_ref,
    wd_ref, bd_ref,
    act_ref, dup_ref, two_ref, dmlp_ref, dattn_ref, dresid_ref, dheads_ref, delta_ref, block_ref,
    vec_ref, dbu_ref,
    r1, unit, rstd, ym, dtwo,
):
    step = pl.program_id(0)

    @pl.when(step == 0)
    def _():
        for i in range(2):
            rows = slice(i * BLK, (i + 1) * BLK)
            place = pl.ds(pl.multiple_of(place_ref[4 + i], BLK), BLK)
            ya = dot(attn_ref[rows, :], wo_ref[...]) + bo_ref[...]
            resid = x_ref[place, :].astype(f32) + branch_scale * ya
            r1[rows, :] = resid
            one, inverse = norm_parts(resid)
            unit[rows, :] = one
            rstd[rows, :] = inverse
            two_ref[rows, :] = (one * g2_ref[...] + s2_ref[...]).astype(bf16)
            dmlp_ref[rows, :] = (branch_scale * dy_ref[place, :].astype(f32)).astype(bf16)
        ym[...] = jnp.zeros_like(ym)
        dtwo[...] = jnp.zeros_like(dtwo)

    u = dot(two_ref[...], wu_ref[...]) + bu_ref[...]
    square = u * u
    t = jnp.tanh(GELU_A * (u * (1.0 + GELU_B * square)))
    half = 0.5 * (1.0 + t)
    act = (u * half).astype(bf16)
    act_ref[...] = act
    slope = half + (0.5 * GELU_A) * u * (1.0 - t * t) * (1.0 + 3.0 * GELU_B * square)
    dup = dot(dmlp_ref[...], wd_ref[...], nt_dims) * slope
    dup = dup.astype(bf16)
    dup_ref[...] = dup
    ym[...] += dot(act, wd_ref[...])
    dtwo[...] += dot(dup, wu_ref[...], nt_dims)
    put_rows(dbu_ref, 0, column_sum(dup.astype(f32)))

    @pl.when(step == pl.num_programs(0) - 1)
    def _():
        dg = jnp.zeros((1, D), f32)
        ds = jnp.zeros((1, D), f32)
        db = jnp.zeros((1, D), f32)
        dbd = jnp.zeros((1, D), f32)
        for i in range(2):
            rows = slice(i * BLK, (i + 1) * BLK)
            place = pl.ds(pl.multiple_of(place_ref[4 + i], BLK), BLK)
            block_ref[rows, :] = (
                r1[rows, :] + branch_scale * (ym[rows, :] + bd_ref[...])
            ).astype(bf16)
            grad = dtwo[rows, :]
            one = unit[rows, :]
            dresid = dy_ref[place, :].astype(f32) + norm_back(one, rstd[rows, :], g2_ref[...], grad)
            dresid_ref[rows, :] = dresid
            dattn = (branch_scale * dresid).astype(bf16)
            dattn_ref[rows, :] = dattn
            dg = dg + column_sum(grad * one)
            ds = ds + column_sum(grad)
            db = db + column_sum(dattn.astype(f32))
            dbd = dbd + column_sum(dmlp_ref[rows, :].astype(f32))
            dheads_ref[rows, :] = dot(dattn, wo_ref[...], nt_dims).astype(bf16)
            back = dot(wo_ref[...], dattn, nt_dims).astype(bf16).astype(f32)
            both = back * outt_ref[:, rows]
            for h in range(HEADS):
                delta_ref[h : h + 1, rows] = column_sum(both[h * HEAD_DIM : (h + 1) * HEAD_DIM])
        vec_ref[...] = jnp.zeros_like(vec_ref)
        put_rows(vec_ref, 0, db)
        put_rows(vec_ref, 6, dg)
        put_rows(vec_ref, 12, ds)
        put_rows(vec_ref, 18, dbd)


def feed(place, attn, attn_t, x, dy, w_out, b_out, gain, shift, w_up, b_up, w_down, b_down):
    count = attn.shape[0]

    def whole(*shape):
        return pl.BlockSpec(shape, lambda k: (0,) * len(shape))

    wide = pl.BlockSpec((count, FF_BLK), lambda k: (0, k))
    tall = whole(count, D)
    steps = FF // FF_BLK
    lane_rows = FF_BLK // LANES
    shapes = [
        ((count, FF), bf16, wide),
        ((count, FF), bf16, wide),
        ((count, D), bf16, tall),
        ((count, D), bf16, tall),
        ((count, D), bf16, tall),
        ((count, D), f32, tall),
        ((count, D), bf16, tall),
        ((16, count), f32, whole(16, count)),
        ((count, D), bf16, tall),
        ((24, LANES), f32, whole(24, LANES)),
        (
            (steps, lane_rows, LANES),
            f32,
            pl.BlockSpec((pl.Squeezed(), lane_rows, LANES), lambda k: (k, 0, 0)),
        ),
    ]
    return pl.pallas_call(
        feed_body,
        grid=(steps,),
        in_specs=[
            smem,
            tall,
            whole(D, count),
            whole(2 * count, D),
            whole(2 * count, D),
            whole(D, D),
            whole(1, D),
            whole(1, D),
            whole(1, D),
            pl.BlockSpec((D, FF_BLK), lambda k: (0, k)),
            pl.BlockSpec((1, FF_BLK), lambda k: (0, k)),
            pl.BlockSpec((FF_BLK, D), lambda k: (k, 0)),
            whole(1, D),
        ],
        out_specs=[spec for _, _, spec in shapes],
        out_shape=[jax.ShapeDtypeStruct(shape, kind) for shape, kind, _ in shapes],
        scratch_shapes=[
            pltpu.VMEM((count, D), f32),
            pltpu.VMEM((count, D), f32),
            pltpu.VMEM((count, 1), f32),
            pltpu.VMEM((count, D), f32),
            pltpu.VMEM((count, D), f32),
        ],
        compiler_params=params_of(),
        cost_estimate=cost(12e9, 2e7),
    )(place, attn, attn_t, x, dy, w_out, b_out, gain, shift, w_up, b_up, w_down, b_down)


def input_body(place_ref, x_ref, dp_ref, w_ref, gain_ref, *refs, near):
    if near:
        dresid_ref, out_ref, vec_ref, dg, ds, dbq, dbv = refs
    else:
        out_ref, vec_ref, dg, ds, dbq, dbv = refs
    step = pl.program_id(0)

    @pl.when(step == 0)
    def _():
        for ref in (dg, ds, dbq, dbv):
            ref[...] = jnp.zeros_like(ref)

    unit, rstd = norm_parts(x_ref[...].astype(f32))
    weights = w_ref[...] if near else w_ref[:, D:]
    grad = dot(dp_ref[...], weights, nt_dims)
    dg[...] += column_sum(grad * unit)
    ds[...] += column_sum(grad)
    wide = dp_ref.shape[1]
    dbv[...] += column_sum(dp_ref[:, wide - D :].astype(f32))
    if near:
        dbq[...] += column_sum(dp_ref[:, :D].astype(f32))
    out_ref[...] = norm_back(unit, rstd, gain_ref[...], grad).astype(out_ref.dtype)
    if near:
        for i in range(2):

            @pl.when(step * BLK == place_ref[4 + i])
            def _():
                out_ref[...] += dresid_ref[i * BLK : (i + 1) * BLK, :]

    @pl.when(step == pl.num_programs(0) - 1)
    def _():
        put_rows(vec_ref, 0, dg[...])
        put_rows(vec_ref, 6, ds[...])
        put_rows(vec_ref, 12, dbq[...])
        put_rows(vec_ref, 18, dbv[...])


def input_back(place, x, dp, w_qkv, gain, dresid=None):
    near = dresid is not None
    count, wide = dp.shape
    extra = [dresid] if near else []
    return pl.pallas_call(
        partial(input_body, near=near),
        grid=(count // BLK,),
        in_specs=[
            smem,
            pl.BlockSpec((BLK, D), lambda i: (i, 0)),
            pl.BlockSpec((BLK, wide), lambda i: (i, 0)),
            pl.BlockSpec((D, 3 * D), lambda i: (0, 0)),
            pl.BlockSpec((1, D), lambda i: (0, 0)),
        ]
        + [pl.BlockSpec((2 * BLK, D), lambda i: (0, 0))] * near,
        out_specs=[
            pl.BlockSpec((BLK, D), lambda i: (i, 0)),
            pl.BlockSpec((24, LANES), lambda i: (0, 0)),
        ],
        out_shape=[
            jax.ShapeDtypeStruct((count, D), f32),
            jax.ShapeDtypeStruct((24, LANES), f32),
        ],
        scratch_shapes=[pltpu.VMEM((1, D), f32)] * 4,
        compiler_params=params_of(),
        cost_estimate=cost(2 * count * wide * D, 10 * count * D),
    )(place, x, dp, w_qkv, gain, *extra)


def rounded(value):
    return lax.reduce_precision(value, 8, 7).astype(bf16)


def bit_pairs(size, bit, sender=lambda place: True):
    return [(n, n ^ bit) for n in range(size) if sender(n)]


def swap(value, axis, bit):
    return lax.ppermute(value, axis, bit_pairs(lax.axis_size(axis), bit))


def halves(value, axis, which):
    size = value.shape[axis] // 2
    own = lax.dynamic_slice_in_dim(value, which * size, size, axis)
    other = lax.dynamic_slice_in_dim(value, (1 - which) * size, size, axis)
    return own, other


def add(a, b):
    return rounded(a.astype(f32) + b.astype(f32))


def core_window(shard_rows):
    return (shard_rows + 15) // 16 * 16


def reduce_plane(own, other):
    x = lax.axis_index("seq") // 2
    y = lax.axis_index("dp") % 2
    window = own.shape[1]
    blocks = add(own, swap(other, "seq", 1)).reshape(2, 2, window, LANES)
    cut = window // 32 * 16
    one, two = blocks[:, :, :cut], blocks[:, :, cut:]
    own_one, other_one = halves(one, 1, x)
    own_two, other_two = halves(two, 0, y)
    got_one, got_two = swap(other_one, "seq", 2), swap(other_two, "dp", 1)
    one, two = add(own_one, got_one), add(own_two, got_two)
    own_one, other_one = halves(one, 0, y)
    own_two, other_two = halves(two, 1, x)
    got_one, got_two = swap(other_one, "dp", 1), swap(other_two, "seq", 2)
    one, two = add(own_one, got_one), add(own_two, got_two)
    return jnp.concatenate([one, two], axis=2).reshape(window, LANES)


def reduce_up(part, plane):
    size = lax.axis_size("dp")
    bit = 1
    while bit < size // 2:

        def sender(n):
            z = n // 2
            return (z ^ plane) & bit != 0 and (z ^ plane) & (bit - 1) == 0

        part = add(part, lax.ppermute(part, "dp", bit_pairs(size, 2 * bit, sender)))
        bit *= 2
    return part


def vector(params, row, rows=6):
    return params[row : row + rows].reshape(1, rows * LANES)


def total_of(value):
    for axis in ("seq", "dp"):
        bit = 1
        while bit < lax.axis_size(axis):
            value = value + swap(value, axis, bit)
            bit *= 2
    return value


def shards(tokens, cotangent, loss_mask, segments, params, first_moment, second_moment):
    block = tokens.shape[0]
    seq_index = lax.axis_index("seq")
    core = seq_index % 2
    x = seq_index // 2
    shard_rows = first_moment.shape[0]
    total_rows = params.shape[0]
    chip = 2 * block
    device_count = lax.axis_size(("dp", "seq"))

    def chip_rows(value):
        other = swap(value, "seq", 1)
        return jnp.concatenate(
            [jnp.where(core == 0, value, other), jnp.where(core == 0, other, value)]
        )

    def unpick(value):
        low, high = value[:BLK], value[BLK:]
        got = swap(jnp.where(core == 0, high, low), "seq", 1)
        return jnp.where(
            core == 0, jnp.concatenate([low, got]), jnp.concatenate([high, got])
        )

    own_tokens = tokens.reshape(block, D)
    near_x = chip_rows(own_tokens)
    far_x = chip_rows(swap(own_tokens, "seq", 2))
    grad_low = cotangent.reshape(block, D) * loss_mask.astype(bf16)
    near_dy = chip_rows(grad_low)
    bias_sum = jnp.sum(rounded(branch_scale * grad_low.astype(f32)).astype(f32), axis=0)
    bias_down_grad = total_of(bias_sum.reshape(-1, LANES)).reshape(-1) / device_count

    w_qkv = unpack_matrix(params, ROW_QKV, D, 3 * D, 4)
    w_out = unpack_matrix(params, ROW_WO, D, D, 2)
    w_up = unpack_matrix(params, ROW_FC, D, FF, 4)
    w_down = unpack_matrix(params, ROW_PR, FF, D, 4)
    gain_one, shift_one = vector(params, ROW_G1), vector(params, ROW_S1)
    bias_query, bias_value = vector(params, ROW_BQ), vector(params, ROW_BV)
    bias_out = vector(params, ROW_BO)
    gain_two, shift_two = vector(params, ROW_G2), vector(params, ROW_S2)
    bias_up = vector(params, ROW_BFC, 24)
    bias_down = vector(params, ROW_BPR)

    seg_row = segments.reshape(1, -1)
    seg_col = segments.reshape(-1, 1)
    near_rows = [core * BLK, (3 - core) * BLK]
    q_place = [x * chip + row for row in near_rows]
    place = jnp.stack(q_place + [core, x] + near_rows).astype(jnp.int32)
    segq = jnp.concatenate(
        [lax.dynamic_slice_in_dim(seg_row, start, BLK, 1) for start in q_place], axis=1
    )
    masks = (place, seg_row, seg_col, segq)

    near_n, near_k, near_kt, near_v, near_vt, queries = project(
        near_x, gain_one, shift_one, bias_query, bias_value, w_qkv, True
    )
    state = attend(*masks, queries, near_k, near_vt)
    far_n, far_k, far_kt, far_v, far_vt = project(
        far_x, gain_one, shift_one, bias_query, bias_value, w_qkv, False
    )
    attn, attn_t, total = attend(*masks, queries, far_k, far_vt, state)
    (
        active, d_up, two_n, d_mlp, d_attn, d_resid, d_heads, delta, block_low, vec, d_bias_up
    ) = feed(
        place, attn, attn_t, near_x, near_dy, w_out, bias_out, gain_two, shift_two, w_up, bias_up,
        w_down, bias_down,
    )
    block_output = unpick(block_low)
    up_rows = d_bias_up.reshape(24, LANES)

    core_x = jnp.stack([core, x]).astype(jnp.int32)
    planes = {}

    def grads(products, vectors, rest, row, head, tail, top):
        done, left = weight_grad(
            core_x, products, vectors, rest, row, head, tail, shard_rows, top
        )
        planes.update(done)
        return left, down16(row) + (0 if left is None else left.shape[0])

    left, top = grads(
        [(active, d_mlp)], [up_rows, vec], None, ROW_PR, [(0, 0, 22, 2)], [(2, 1, 18, 6)],
        total_rows,
    )
    left, top = grads(
        [(two_n, d_up)], [up_rows, vec], left, ROW_FC, [(0, 1, 8, 10)], [(10, 0, 0, 22)], top
    )
    left, top = grads([(attn, d_attn)], [vec], left, ROW_WO, [], [(8, 0, 0, 8)], top)

    d_near, d_far = attend_back(
        *masks, queries, d_heads, total, delta, (far_k, far_kt, far_v), (near_k, near_kt, near_v)
    )
    far_in, far_vec = input_back(place, far_x, d_far, w_qkv, gain_one)
    near_in, near_vec = input_back(place, near_x, d_near, w_qkv, gain_one, d_resid)
    one_vec = near_vec + far_vec
    if left is not None:
        extra = jnp.concatenate([one_vec[16:], jnp.zeros((left.shape[0] - 8, LANES), f32)])
        left = rounded(left.astype(f32) + extra)
    grads(
        [(near_n, d_near), (far_n, d_far)], [one_vec], left, ROW_QKV, [(0, 0, 0, 12)],
        [(12, 0, 12, 4)], top,
    )

    own, other = halves(far_in, 0, core)
    far_sum = own + swap(rounded(other), "seq", 1).astype(f32)
    from_far = swap(rounded(far_sum), "seq", 2).astype(f32)
    own, other = halves(near_in, 0, core)
    input_grad = own + swap(rounded(other), "seq", 1).astype(f32)
    input_grad = rounded(jnp.where(x == 0, input_grad + from_far, input_grad))

    own_plane = lax.axis_index("dp") // 2
    window = core_window(shard_rows)
    summed = jnp.zeros((window, LANES), bf16)
    for plane in sorted(planes, reverse=True):
        part = reduce_up(reduce_plane(*planes[plane]), plane)
        summed = jnp.where(own_plane == plane, part, summed)
    summed = summed.astype(f32)
    summed = jnp.where(core == 0, summed[:shard_rows], summed[window - shard_rows :])

    first_row = lax.axis_index(("dp", "seq")) * shard_rows
    grads_mean = summed / device_count
    own_params = lax.dynamic_slice_in_dim(params, first_row, shard_rows, 0)
    new_first = first_decay * first_moment + (1.0 - first_decay) * grads_mean
    new_second = second_decay * second_moment + (1.0 - second_decay) * grads_mean * grads_mean
    fix_one = 1.0 - first_decay**STEP
    fix_two = 1.0 - second_decay**STEP
    update = new_first / fix_one / (jnp.sqrt(new_second / fix_two) + adam_epsilon)
    row = first_row + iota((shard_rows, LANES), 0)
    in_matrix = jnp.zeros(row.shape, bool)
    for start, end in (
        (ROW_QKV, ROW_BQ),
        (ROW_WO, ROW_BO),
        (ROW_FC, ROW_BFC),
        (ROW_PR, ROW_BPR),
    ):
        in_matrix = in_matrix | ((row >= start) & (row < end))
    new_params = own_params - jnp.where(in_matrix, base_rate / D, base_rate) * update
    return (
        block_output.reshape(tokens.shape),
        input_grad.reshape(tokens.shape),
        new_params,
        new_first,
        new_second,
        bias_down_grad,
    )


def solution(mesh):
    return jax.shard_map(
        shards,
        mesh=mesh,
        in_specs=(
            P("seq", "dp", None),
            P("seq", "dp", None),
            P("seq", "dp"),
            P(None, "dp"),
            P(),
            P(("dp", "seq"), None),
            P(("dp", "seq"), None),
        ),
        out_specs=(
            P("seq", "dp", None),
            P("seq", "dp", None),
            P(("dp", "seq"), None),
            P(("dp", "seq"), None),
            P(("dp", "seq"), None),
            P(),
        ),
        check_vma=False,
    )
```

```python
from functools import partial
import math

import jax
import jax.numpy as jnp
from jax import lax
from jax.experimental import pallas as pl
from jax.experimental.pallas import tpu as pltpu
from jax.sharding import PartitionSpec as P

D = 768
HEADS = 12
HEAD_DIM = 64
FF = 3072
STEP = 4
LANES = 128
BLK = 256

norm_epsilon = 1e-05
branch_scale = 48.0 ** (-0.5)
first_decay = 0.9
second_decay = 0.95
adam_epsilon = 1e-08
base_rate = 0.1
masked_score = -1e30
LOG2E = 1.4426950408889634
score_factor = LOG2E / HEAD_DIM

f32 = jnp.float32
bf16 = jnp.bfloat16

ROW_G1, ROW_S1 = 0, 6
ROW_QKV = 12
ROW_BQ = ROW_QKV + D * 3 * D // LANES
ROW_BV = ROW_BQ + 6
ROW_WO = ROW_BV + 6
ROW_BO = ROW_WO + D * D // LANES
ROW_G2, ROW_S2 = ROW_BO + 6, ROW_BO + 12
ROW_FC = ROW_BO + 18
ROW_BFC = ROW_FC + D * FF // LANES
ROW_PR = ROW_BFC + FF // LANES
ROW_BPR = ROW_PR + D * FF // LANES
ROW_END = ROW_BPR + 6

VMEM = 56 * 1024 * 1024


nt_dims = (((1,), (1,)), ((), ()))
nn_dims = (((1,), (0,)), ((), ()))
tn_dims = (((0,), (0,)), ((), ()))

smem = pl.BlockSpec(memory_space=pltpu.SMEM)
vmem = pl.BlockSpec(memory_space=pltpu.VMEM)
anywhere = pl.BlockSpec(memory_space=pl.ANY)


def params_of(limit=VMEM):
    return pltpu.CompilerParams(vmem_limit_bytes=limit)


def cost(flops, moved):
    return pl.CostEstimate(flops=int(flops), bytes_accessed=int(moved), transcendentals=0)


def dot(a, b, dims=nn_dims):
    return lax.dot_general(a, b, dims, preferred_element_type=f32)


def iota(shape, axis):
    return lax.broadcasted_iota(jnp.int32, shape, axis)


def kernel_call(body, operands, in_specs, after=(), **options):
    count = len(operands)

    def without(*refs):
        body(*refs[:count], *refs[count + len(after) :])

    return pl.pallas_call(without, in_specs=in_specs + [anywhere] * len(after), **options)(
        *operands, *after
    )


def down16(row):
    return row // 16 * 16


def group_rows(blocks):
    return 8 if blocks > 8 else 32


def side_by_side(value, other):
    return jnp.concatenate([value, other], axis=1)


def unpack_body(x_ref, o_ref, move, *, shift, rows, blocks, pairs):
    size = rows * blocks
    bits = rows.bit_length() - 1

    @pl.when(pl.program_id(0) == 0)
    def _():
        to, come = iota(move.shape, 0), iota(move.shape, 1)
        move[...] = (come == shift + (to & (rows - 1)) * blocks + (to >> bits)).astype(bf16)

    for n in range(pairs):
        both = side_by_side(
            *[x_ref[pl.ds((2 * n + side) * size, size + 16), :].astype(bf16) for side in (0, 1)]
        )
        moved = dot(move[...], both)
        for j in range(blocks):
            part = moved[j * rows : (j + 1) * rows]
            part = jnp.concatenate([part[:, :LANES], part[:, LANES:]], axis=0).astype(bf16)
            o_ref[2 * n * rows : 2 * (n + 1) * rows, j * LANES : (j + 1) * LANES] = part


def unpack_matrix(params, row, matrix_rows, columns, steps):
    blocks = columns // LANES
    rows = group_rows(blocks)
    base = row // 8 * 8
    chunk = matrix_rows // steps
    size = chunk * blocks
    return pl.pallas_call(
        partial(
            unpack_body, shift=row - base, rows=rows, blocks=blocks, pairs=chunk // rows // 2
        ),
        grid=(steps,),
        in_specs=[
            pl.BlockSpec(
                (pl.Element(size + 16), pl.Element(LANES)),
                lambda i: (pl.multiple_of(base + i * size, 8), 0),
            )
        ],
        out_specs=pl.BlockSpec((chunk, columns), lambda i: (i, 0)),
        out_shape=jax.ShapeDtypeStruct((matrix_rows, columns), bf16),
        scratch_shapes=[pltpu.VMEM((rows * blocks, rows * blocks + 16), bf16)],
        compiler_params=params_of(),
        cost_estimate=cost(2e9, 6 * matrix_rows * columns),
    )(params)


def grad_body(
    core_ref,
    *refs,
    products,
    vectors,
    rest,
    base,
    row,
    matrix_rows,
    columns,
    head,
    tail,
    planes,
    plane_rows,
    keep,
):
    refs = list(refs)
    factors = [refs.pop(0) for _ in range(2 * products)]
    vector_refs = [refs.pop(0) for _ in range(vectors)]
    rest_ref = refs.pop(0) if rest else None
    plane_refs = [(refs.pop(0), refs.pop(0)) for _ in planes]
    keep_ref = refs.pop(0) if keep else None
    window, grad, move, carry, last, sems = refs
    blocks = columns // LANES
    rows = group_rows(blocks)
    bits = rows.bit_length() - 1
    size = rows * blocks
    shift = row - base
    body_rows = matrix_rows * blocks
    tail_rows = last.shape[0]
    if rest:
        load = pltpu.make_async_copy(
            rest_ref, window.at[pl.ds(body_rows + tail_rows, rest), :], sems.at[0]
        )
        load.start()
    to, come = iota(move.shape, 0), iota(move.shape, 1)
    move[...] = (to == shift + (come & (rows - 1)) * blocks + (come >> bits)).astype(bf16)
    carry[...] = jnp.zeros_like(carry)
    last[...] = jnp.zeros_like(last)
    for place, n, start, count in head:
        carry[place : place + count, :] = vector_refs[n][start : start + count, :]
    for place, n, start, count in tail:
        last[place : place + count, :] = vector_refs[n][start : start + count, :]

    core = core_ref[0]
    wide_rows = grad.shape[0]

    def multiply(c, state):
        lanes = pl.ds(pl.multiple_of(c * wide_rows, wide_rows), wide_rows)
        grad[...] = dot(factors[0][:, lanes], factors[1][...], tn_dims)
        if products == 2:

            @pl.when(core_ref[1] == 1)
            def _():
                wide = factors[3].shape[1]
                grad[:, columns - wide :] += dot(factors[2][:, lanes], factors[3][...], tn_dims)

        left = carry[...]
        for pair in range(wide_rows // rows // 2):
            both = side_by_side(
                *[
                    jnp.concatenate(
                        [
                            grad[at : at + rows, j * LANES : (j + 1) * LANES]
                            for j in range(blocks)
                        ],
                        axis=0,
                    ).astype(bf16)
                    for at in (2 * pair * rows, (2 * pair + 1) * rows)
                ]
            )
            moved = dot(move[...], both)
            for side in (0, 1):
                part = moved[:, side * LANES : (side + 1) * LANES]
                at = pl.multiple_of((c * (wide_rows // rows) + 2 * pair + side) * size, 16)
                window[pl.ds(at, 16), :] = (part[:16] + left).astype(bf16)
                window[pl.ds(at + 16, size - 16), :] = part[16:size].astype(bf16)
                left = part[size:]
        carry[...] = left
        return state

    lax.fori_loop(0, matrix_rows // wide_rows, multiply, 0)
    last[pl.ds(0, 16), :] = last[pl.ds(0, 16), :] + carry[...]
    window[pl.ds(body_rows, tail_rows), :] = last[...].astype(bf16)
    if rest:
        load.wait()
    copies = []
    half = plane_rows // 4
    for plane, (own_ref, other_ref) in zip(planes, plane_refs):
        part_rows = own_ref.shape[1]
        for block in range(4):
            for ref, which in ((own_ref, core), (other_ref, 1 - core)):
                at = plane * plane_rows - base + block * half
                at = pl.multiple_of(at + which * (half - part_rows), 16)
                copies.append((window.at[pl.ds(at, part_rows), :], ref.at[block]))
    if keep:
        copies.append((window.at[pl.ds(0, keep), :], keep_ref))
    started = [
        pltpu.make_async_copy(source, target, sems.at[1 + n])
        for n, (source, target) in enumerate(copies)
    ]
    for copy in started:
        copy.start()
    for copy in started:
        copy.wait()


def weight_grad(place, products, vectors, rest, row, head, tail, shard_rows, top, after):
    base = down16(row)
    matrix_rows, columns = products[0][0].shape[1], products[0][1].shape[1]
    blocks = columns // LANES
    rows = group_rows(blocks)
    size = rows * blocks
    plane_rows = 8 * shard_rows
    rest_rows = 0 if rest is None else rest.shape[0]
    own_end = top - rest_rows
    tail_rows = own_end - base - matrix_rows * blocks
    first_plane = -(-base // plane_rows)
    planes = list(range(first_plane, top // plane_rows))
    keep = first_plane * plane_rows - base
    part_rows = core_window(shard_rows)
    part = jax.ShapeDtypeStruct((4, part_rows, LANES), bf16)
    out_shape = [part] * (2 * len(planes))
    if keep:
        out_shape.append(jax.ShapeDtypeStruct((keep, LANES), bf16))
    operands = [value for pair in products for value in pair] + list(vectors)
    specs = [smem] + [vmem] * len(operands)
    if rest_rows:
        operands.append(rest)
        specs.append(anywhere)
    tokens = sum(a.shape[0] for a, _ in products)
    outs = kernel_call(
        partial(
            grad_body,
            products=len(products),
            vectors=len(vectors),
            rest=rest_rows,
            base=base,
            row=row,
            matrix_rows=matrix_rows,
            columns=columns,
            head=head,
            tail=tail,
            planes=planes,
            plane_rows=plane_rows,
            keep=keep,
        ),
        [place] + operands,
        specs,
        after,
        out_specs=[anywhere] * len(out_shape),
        out_shape=out_shape,
        scratch_shapes=[
            pltpu.VMEM((top - base, LANES), bf16),
            pltpu.VMEM((256 if columns < 3 * D or columns == FF else 128, columns), f32),
            pltpu.VMEM((size + 16, size), bf16),
            pltpu.VMEM((16, LANES), f32),
            pltpu.VMEM((tail_rows, LANES), f32),
            pltpu.SemaphoreType.DMA((2 + 8 * len(planes),)),
        ],
        compiler_params=params_of(),
        cost_estimate=cost(4 * tokens * matrix_rows * columns, 4 * matrix_rows * columns),
    )
    pairs = {plane: (outs[2 * n], outs[2 * n + 1]) for n, plane in enumerate(planes)}
    return pairs, (outs[-1] if keep else None)


def row_mean(value):
    return jnp.sum(value, axis=-1, keepdims=True) * (1.0 / value.shape[-1])


def norm_parts(values):
    center = values - row_mean(values)
    rstd = lax.rsqrt(row_mean(center * center) + norm_epsilon)
    return center * rstd, rstd


def norm_back(unit, rstd, gain, grad):
    scaled = grad * gain
    return rstd * (scaled - row_mean(scaled) - unit * row_mean(scaled * unit))


def project_body(x_ref, gain_ref, shift_ref, bq_ref, bv_ref, w_ref, *outs, with_query):
    n_ref, k_ref, kt_ref, v_ref, vt_ref = outs[:5]
    unit, _ = norm_parts(x_ref[...].astype(f32))
    normed = (unit * gain_ref[...] + shift_ref[...]).astype(bf16)
    n_ref[...] = normed
    keys = dot(normed, w_ref[:, D : 2 * D]).astype(bf16)
    k_ref[...] = keys
    kt_ref[...] = keys.T
    values = (dot(normed, w_ref[:, 2 * D :]) + bv_ref[...]).astype(bf16)
    v_ref[...] = values
    vt_ref[...] = values.T
    if with_query:
        outs[5][...] = (dot(normed, w_ref[:, :D]) + bq_ref[...]).astype(bf16)


def project(x, gain, shift, bias_query, bias_value, w_qkv, with_query):
    count = x.shape[0]
    by_rows = pl.BlockSpec((BLK, D), lambda i: (i, 0))
    by_columns = pl.BlockSpec((D, BLK), lambda i: (0, i))
    row = pl.BlockSpec((1, D), lambda i: (0, 0))
    tall = jax.ShapeDtypeStruct((count, D), bf16)
    wide = jax.ShapeDtypeStruct((D, count), bf16)
    return pl.pallas_call(
        partial(project_body, with_query=with_query),
        grid=(count // BLK,),
        in_specs=[by_rows, row, row, row, row, pl.BlockSpec((D, 3 * D), lambda i: (0, 0))],
        out_specs=[by_rows, by_rows, by_columns, by_rows, by_columns] + [by_rows] * with_query,
        out_shape=[tall, tall, wide, tall, wide] + [tall] * with_query,
        compiler_params=params_of(),
        cost_estimate=cost(2 * count * D * (2 + with_query) * D, 12 * count * D),
    )(x, gain, shift, bias_query, bias_value, w_qkv)


def head_lanes(value, odd):
    lane = iota(value.shape, 1)
    keep = (lane >= HEAD_DIM) if odd else (lane < HEAD_DIM)
    return jnp.where(keep, value, jnp.zeros_like(value))


def visit_block(place_ref, seg_ref, segk_ref, segq_ref, bias_ref, i, k_start, valid, step):
    q_start = place_ref[i]
    q_first = seg_ref[0, q_start]
    q_last = seg_ref[0, q_start + BLK - 1]
    k_first = seg_ref[0, k_start]
    k_last = seg_ref[0, k_start + BLK - 1]
    active = valid & (k_start <= q_start) & (k_last >= q_first)
    plain = (k_first == q_last) & (k_start + BLK <= q_start)

    @pl.when(active & plain)
    def _():
        step(False)

    @pl.when(active & jnp.logical_not(plain))
    def _():
        k_pos = k_start + iota((BLK, BLK), 0)
        q_pos = q_start + iota((BLK, BLK), 1)
        segk = segk_ref[pl.ds(pl.multiple_of(k_start, BLK), BLK), :]
        same = segk == segq_ref[:, i * BLK : (i + 1) * BLK]
        bias_ref[...] = jnp.where((k_pos <= q_pos) & same, 0.0, masked_score)
        step(True)


ACC = HEAD_DIM + 16


def attend_body(
    place_ref, seg_ref, segk_ref, segq_ref, q_ref, k_ref, vt_ref, *refs, first
):
    if first:
        acc_ref, top_ref, bias_ref, s_ref = refs
        acc_ref[...] = jnp.zeros_like(acc_ref)
        top_ref[...] = jnp.full_like(top_ref, masked_score)
    else:
        acc_in, top_in, out_ref, outt_ref, total_ref, bias_ref, s_ref, acc_ref, top_ref = refs
        acc_ref[...] = acc_in[...]
        top_ref[...] = top_in[...]
    ones = jnp.ones((16, BLK), bf16)
    count = k_ref.shape[0] // BLK
    x = place_ref[3]
    base = x * (count * BLK) if first else 0 * x
    valid = (x >= 0) if first else (x == 1)
    for i in range(2):
        cols = slice(i * BLK, (i + 1) * BLK)

        def visit(n, carry):
            kb = count - 1 - n
            k_rows = pl.ds(pl.multiple_of(kb * BLK, BLK), BLK)
            q_rows = pl.ds(pl.multiple_of(place_ref[4 + i], BLK), BLK)

            def step(masked):
                tops = []
                for h in range(HEADS):
                    pair, odd = h // 2, h % 2
                    lanes = slice(pair * LANES, (pair + 1) * LANES)
                    s = dot(k_ref[k_rows, lanes], head_lanes(q_ref[q_rows, lanes], odd), nt_dims)
                    s = s * score_factor
                    if masked:
                        s = s + bias_ref[...]
                    s_ref[h] = s
                    tops.append(jnp.max(s, axis=0, keepdims=True))
                old = top_ref[:HEADS, cols]
                new = jnp.maximum(old, jnp.concatenate(tops, axis=0))
                top_ref[:HEADS, cols] = new
                scale = jnp.exp2(old - new)
                for h in range(HEADS):
                    p = jnp.exp2(s_ref[h] - new[h : h + 1]).astype(bf16)
                    v_part = jnp.concatenate(
                        [vt_ref[h * HEAD_DIM : (h + 1) * HEAD_DIM, k_rows], ones], axis=0
                    )
                    acc_ref[h, :, cols] = acc_ref[h, :, cols] * scale[h : h + 1] + dot(v_part, p)

            visit_block(
                place_ref, seg_ref, segk_ref, segq_ref, bias_ref, i, base + kb * BLK, valid, step
            )
            return carry

        lax.fori_loop(0, count, visit, 0)
    if not first:
        for h in range(HEADS):
            total = acc_ref[h, HEAD_DIM : HEAD_DIM + 1, :]
            outt_ref[h * HEAD_DIM : (h + 1) * HEAD_DIM, :] = acc_ref[h, :HEAD_DIM, :] / total
            total_ref[h : h + 1, :] = top_ref[h : h + 1, :] + jnp.log2(total)
        for i in range(2):
            cols = slice(i * BLK, (i + 1) * BLK)
            out_ref[cols, :] = outt_ref[:, cols].T.astype(bf16)


def attend(place, seg, segk, segq, q, k, vt, state=None):
    count = 2 * BLK
    first = state is None
    acc_shape = jax.ShapeDtypeStruct((HEADS, ACC, count), f32)
    row_shape = jax.ShapeDtypeStruct((16, count), f32)
    if first:
        outs = (acc_shape, row_shape)
    else:
        outs = (
            jax.ShapeDtypeStruct((count, D), bf16),
            jax.ShapeDtypeStruct((D, count), f32),
            row_shape,
        )
    extra = () if first else state
    held = [] if first else [pltpu.VMEM((HEADS, ACC, count), f32), pltpu.VMEM((16, count), f32)]
    return pl.pallas_call(
        partial(attend_body, first=first),
        in_specs=[smem, smem] + [vmem] * (5 + len(extra)),
        out_specs=(vmem,) * len(outs),
        out_shape=outs,
        scratch_shapes=[pltpu.VMEM((BLK, BLK), f32), pltpu.VMEM((HEADS, BLK, BLK), f32)] + held,
        compiler_params=params_of(),
        cost_estimate=cost(6e9, 8e6),
    )(place, seg, segk, segq, q, k, vt, *extra)


def attend_back_body(
    place_ref, seg_ref, segk_ref, segq_ref, q_ref, do_ref, total_ref, delta_ref, k_ref, kt_ref,
    v_ref, *refs, near
):
    if near:
        dqt_in, out_ref, bias_ref, dk_acc, dv_acc, dqt_ref = refs
        dqt_ref[...] = dqt_in[...]
    else:
        out_ref, dqt_ref, bias_ref, dk_acc, dv_acc = refs
        dqt_ref[...] = jnp.zeros_like(dqt_ref)
    count = k_ref.shape[0] // BLK
    x = place_ref[3]
    base = x * (count * BLK) if near else 0 * x
    valid = (x >= 0) if near else (x == 1)
    at = D if near else 0

    def visit(kb, carry):
        k_rows = pl.ds(pl.multiple_of(kb * BLK, BLK), BLK)
        dk_acc[...] = jnp.zeros_like(dk_acc)
        dv_acc[...] = jnp.zeros_like(dv_acc)
        for i in range(2):
            cols = slice(i * BLK, (i + 1) * BLK)
            q_rows = pl.ds(pl.multiple_of(place_ref[4 + i], BLK), BLK)

            def step(masked):
                for pair in range(HEADS // 2):
                    lanes = slice(pair * LANES, (pair + 1) * LANES)
                    k_pair = k_ref[k_rows, lanes]
                    v_pair = v_ref[k_rows, lanes]
                    q_pair = q_ref[q_rows, lanes]
                    do_pair = do_ref[cols, lanes]
                    dk = dk_acc[:, lanes]
                    dv = dv_acc[:, lanes]
                    for odd in range(2):
                        h = 2 * pair + odd
                        head = slice(h * HEAD_DIM, (h + 1) * HEAD_DIM)
                        q_head = head_lanes(q_pair, odd)
                        do_head = head_lanes(do_pair, odd)
                        s = dot(k_pair, q_head, nt_dims) * score_factor
                        if masked:
                            s = s + bias_ref[...]
                        p = jnp.exp2(s - total_ref[h : h + 1, cols])
                        da = dot(v_pair, do_head, nt_dims)
                        ds = (p * (da - delta_ref[h : h + 1, cols])).astype(bf16)
                        dv = dv + dot(p.astype(bf16), do_head)
                        dk = dk + dot(ds, q_head)
                        dqt_ref[head, cols] += dot(kt_ref[head, k_rows], ds)
                    dk_acc[:, lanes] = dk
                    dv_acc[:, lanes] = dv

            visit_block(
                place_ref, seg_ref, segk_ref, segq_ref, bias_ref, i, base + kb * BLK, valid, step
            )
        out_ref[k_rows, at : at + D] = (dk_acc[...] * (1.0 / HEAD_DIM)).astype(bf16)
        out_ref[k_rows, at + D : at + 2 * D] = dv_acc[...].astype(bf16)
        if near:
            out_ref[k_rows, :D] = jnp.zeros((BLK, D), bf16)
        return carry

    lax.fori_loop(0, count, visit, 0)
    if near:
        for i in range(2):
            q_rows = pl.ds(pl.multiple_of(place_ref[4 + i], BLK), BLK)
            part = dqt_ref[:, i * BLK : (i + 1) * BLK] * (1.0 / HEAD_DIM)
            out_ref[q_rows, :D] = part.T.astype(bf16)


def attend_back(place, seg, segk, segq, q, do, total, delta, keys, dqt, after):
    near = dqt is not None
    rows = q.shape[0]
    sums = jax.ShapeDtypeStruct((D, 2 * BLK), f32)
    blocks = [pltpu.VMEM((BLK, BLK), f32), pltpu.VMEM((BLK, D), f32), pltpu.VMEM((BLK, D), f32)]
    operands = [place, seg, segk, segq, q, do, total, delta, *keys] + ([dqt] if near else [])
    outs = kernel_call(
        partial(attend_back_body, near=near),
        operands,
        [smem, smem] + [vmem] * (len(operands) - 2),
        after,
        out_specs=[vmem] * (2 - near),
        out_shape=[jax.ShapeDtypeStruct((rows, (2 + near) * D), bf16)] + ([] if near else [sums]),
        scratch_shapes=blocks + ([pltpu.VMEM((D, 2 * BLK), f32)] if near else []),
        compiler_params=params_of(),
        cost_estimate=cost(15e9, 2e7),
    )
    return outs[0] if near else outs


GELU_A = math.sqrt(2.0 / math.pi)
GELU_B = 0.044715
FF_BLK = 512


def put_rows(ref, at, value):
    for j in range(value.shape[1] // LANES):
        ref[at + j : at + j + 1, :] = value[:, j * LANES : (j + 1) * LANES]


def column_sum(value):
    return jnp.sum(value, axis=0, keepdims=True)


def feed_body(
    place_ref, attn_ref, outt_ref, x_ref, dy_ref, wo_ref, bo_ref, g2_ref, s2_ref, wu_ref, bu_ref,
    wd_ref, bd_ref,
    act_ref, dup_ref, two_ref, dmlp_ref, dattn_ref, dresid_ref, dheads_ref, delta_ref, block_ref,
    vec_ref, dbu_ref,
    r1, unit, rstd, ym, dtwo,
):
    step = pl.program_id(0)

    @pl.when(step == 0)
    def _():
        for i in range(2):
            rows = slice(i * BLK, (i + 1) * BLK)
            place = pl.ds(pl.multiple_of(place_ref[4 + i], BLK), BLK)
            ya = dot(attn_ref[rows, :], wo_ref[...]) + bo_ref[...]
            resid = x_ref[place, :].astype(f32) + branch_scale * ya
            r1[rows, :] = resid
            one, inverse = norm_parts(resid)
            unit[rows, :] = one
            rstd[rows, :] = inverse
            two_ref[rows, :] = (one * g2_ref[...] + s2_ref[...]).astype(bf16)
            dmlp_ref[rows, :] = (branch_scale * dy_ref[place, :].astype(f32)).astype(bf16)
        ym[...] = jnp.zeros_like(ym)
        dtwo[...] = jnp.zeros_like(dtwo)

    u = dot(two_ref[...], wu_ref[...]) + bu_ref[...]
    square = u * u
    t = jnp.tanh(GELU_A * (u * (1.0 + GELU_B * square)))
    half = 0.5 * (1.0 + t)
    act = (u * half).astype(bf16)
    act_ref[...] = act
    slope = half + (0.5 * GELU_A) * u * (1.0 - t * t) * (1.0 + 3.0 * GELU_B * square)
    dup = dot(dmlp_ref[...], wd_ref[...], nt_dims) * slope
    dup = dup.astype(bf16)
    dup_ref[...] = dup
    ym[...] += dot(act, wd_ref[...])
    dtwo[...] += dot(dup, wu_ref[...], nt_dims)
    put_rows(dbu_ref, 0, column_sum(dup.astype(f32)))

    @pl.when(step == pl.num_programs(0) - 1)
    def _():
        dg = jnp.zeros((1, D), f32)
        ds = jnp.zeros((1, D), f32)
        db = jnp.zeros((1, D), f32)
        dbd = jnp.zeros((1, D), f32)
        for i in range(2):
            rows = slice(i * BLK, (i + 1) * BLK)
            place = pl.ds(pl.multiple_of(place_ref[4 + i], BLK), BLK)
            block_ref[rows, :] = (
                r1[rows, :] + branch_scale * (ym[rows, :] + bd_ref[...])
            ).astype(bf16)
            grad = dtwo[rows, :]
            one = unit[rows, :]
            dresid = dy_ref[place, :].astype(f32) + norm_back(one, rstd[rows, :], g2_ref[...], grad)
            dresid_ref[rows, :] = dresid
            dattn = (branch_scale * dresid).astype(bf16)
            dattn_ref[rows, :] = dattn
            dg = dg + column_sum(grad * one)
            ds = ds + column_sum(grad)
            db = db + column_sum(dattn.astype(f32))
            dbd = dbd + column_sum(dmlp_ref[rows, :].astype(f32))
            dheads_ref[rows, :] = dot(dattn, wo_ref[...], nt_dims).astype(bf16)
            back = dot(wo_ref[...], dattn, nt_dims).astype(bf16).astype(f32)
            both = back * outt_ref[:, rows]
            for h in range(HEADS):
                delta_ref[h : h + 1, rows] = column_sum(both[h * HEAD_DIM : (h + 1) * HEAD_DIM])
        vec_ref[...] = jnp.zeros_like(vec_ref)
        put_rows(vec_ref, 0, db)
        put_rows(vec_ref, 6, dg)
        put_rows(vec_ref, 12, ds)
        put_rows(vec_ref, 18, dbd)


def feed(place, attn, attn_t, x, dy, w_out, b_out, gain, shift, w_up, b_up, w_down, b_down):
    count = attn.shape[0]

    def whole(*shape):
        return pl.BlockSpec(shape, lambda k: (0,) * len(shape))

    wide = pl.BlockSpec((count, FF_BLK), lambda k: (0, k))
    tall = whole(count, D)
    steps = FF // FF_BLK
    lane_rows = FF_BLK // LANES
    shapes = [
        ((count, FF), bf16, wide),
        ((count, FF), bf16, wide),
        ((count, D), bf16, tall),
        ((count, D), bf16, tall),
        ((count, D), bf16, tall),
        ((count, D), f32, tall),
        ((count, D), bf16, tall),
        ((16, count), f32, whole(16, count)),
        ((count, D), bf16, tall),
        ((24, LANES), f32, whole(24, LANES)),
        (
            (steps, lane_rows, LANES),
            f32,
            pl.BlockSpec((pl.Squeezed(), lane_rows, LANES), lambda k: (k, 0, 0)),
        ),
    ]
    return pl.pallas_call(
        feed_body,
        grid=(steps,),
        in_specs=[
            smem,
            tall,
            whole(D, count),
            whole(2 * count, D),
            whole(2 * count, D),
            whole(D, D),
            whole(1, D),
            whole(1, D),
            whole(1, D),
            pl.BlockSpec((D, FF_BLK), lambda k: (0, k)),
            pl.BlockSpec((1, FF_BLK), lambda k: (0, k)),
            pl.BlockSpec((FF_BLK, D), lambda k: (k, 0)),
            whole(1, D),
        ],
        out_specs=[spec for _, _, spec in shapes],
        out_shape=[jax.ShapeDtypeStruct(shape, kind) for shape, kind, _ in shapes],
        scratch_shapes=[
            pltpu.VMEM((count, D), f32),
            pltpu.VMEM((count, D), f32),
            pltpu.VMEM((count, 1), f32),
            pltpu.VMEM((count, D), f32),
            pltpu.VMEM((count, D), f32),
        ],
        compiler_params=params_of(),
        cost_estimate=cost(12e9, 2e7),
    )(place, attn, attn_t, x, dy, w_out, b_out, gain, shift, w_up, b_up, w_down, b_down)


def input_body(place_ref, x_ref, dp_ref, w_ref, gain_ref, *refs, near):
    if near:
        dresid_ref, out_ref, vec_ref, dg, ds, dbq, dbv = refs
    else:
        out_ref, vec_ref, dg, ds, dbq, dbv = refs
    step = pl.program_id(0)

    @pl.when(step == 0)
    def _():
        for ref in (dg, ds, dbq, dbv):
            ref[...] = jnp.zeros_like(ref)

    unit, rstd = norm_parts(x_ref[...].astype(f32))
    weights = w_ref[...] if near else w_ref[:, D:]
    grad = dot(dp_ref[...], weights, nt_dims)
    dg[...] += column_sum(grad * unit)
    ds[...] += column_sum(grad)
    wide = dp_ref.shape[1]
    dbv[...] += column_sum(dp_ref[:, wide - D :].astype(f32))
    if near:
        dbq[...] += column_sum(dp_ref[:, :D].astype(f32))
    out_ref[...] = norm_back(unit, rstd, gain_ref[...], grad).astype(out_ref.dtype)
    if near:
        for i in range(2):

            @pl.when(step * BLK == place_ref[4 + i])
            def _():
                out_ref[...] += dresid_ref[i * BLK : (i + 1) * BLK, :]

    @pl.when(step == pl.num_programs(0) - 1)
    def _():
        put_rows(vec_ref, 0, dg[...])
        put_rows(vec_ref, 6, ds[...])
        put_rows(vec_ref, 12, dbq[...])
        put_rows(vec_ref, 18, dbv[...])


def input_back(place, x, dp, w_qkv, gain, dresid, after):
    near = dresid is not None
    count, wide = dp.shape
    return kernel_call(
        partial(input_body, near=near),
        [place, x, dp, w_qkv, gain] + [dresid] * near,
        [
            smem,
            pl.BlockSpec((BLK, D), lambda i: (i, 0)),
            pl.BlockSpec((BLK, wide), lambda i: (i, 0)),
            pl.BlockSpec((D, 3 * D), lambda i: (0, 0)),
            pl.BlockSpec((1, D), lambda i: (0, 0)),
        ]
        + [pl.BlockSpec((2 * BLK, D), lambda i: (0, 0))] * near,
        after,
        grid=(count // BLK,),
        out_specs=[
            pl.BlockSpec((BLK, D), lambda i: (i, 0)),
            pl.BlockSpec((24, LANES), lambda i: (0, 0)),
        ],
        out_shape=[
            jax.ShapeDtypeStruct((count, D), f32),
            jax.ShapeDtypeStruct((24, LANES), f32),
        ],
        scratch_shapes=[pltpu.VMEM((1, D), f32)] * 4,
        compiler_params=params_of(),
        cost_estimate=cost(2 * count * wide * D, 10 * count * D),
    )


def rounded(value):
    return lax.reduce_precision(value, 8, 7).astype(bf16)


def bit_pairs(size, bit, sender=lambda place: True):
    return [(n, n ^ bit) for n in range(size) if sender(n)]


def swap(value, axis, bit):
    return lax.ppermute(value, axis, bit_pairs(lax.axis_size(axis), bit))


def halves(value, axis, which):
    size = value.shape[axis] // 2
    own = lax.dynamic_slice_in_dim(value, which * size, size, axis)
    other = lax.dynamic_slice_in_dim(value, (1 - which) * size, size, axis)
    return own, other


def add(a, b):
    return rounded(a.astype(f32) + b.astype(f32))


def core_window(shard_rows):
    return (shard_rows + 15) // 16 * 16


def toward(plane, size):
    if size == 4:
        return [
            [[(1, 0), (3, 2)], [(2, 0)]],
            [[(0, 1), (3, 2)], [(2, 1)]],
            [[(0, 1), (3, 2)], [(1, 2)]],
            [[(0, 1), (2, 3)], [(1, 3)]],
        ][plane]
    steps = []
    bit = 1
    while bit < size:
        away = [z for z in range(size) if (z ^ plane) & bit and not (z ^ plane) & (bit - 1)]
        steps.append([(z, z ^ bit) for z in away])
        bit *= 2
    return steps


def tie(value, token):
    return value if token is None else lax.optimization_barrier((value, token))[0]


def reduce_plane(parts, plane, own, other):
    x = lax.axis_index("seq") // 2
    y = lax.axis_index("dp") % 2
    window = own.shape[1]
    got = swap(other, "seq", 1)
    token = yield [other], [got]
    blocks = add(own, tie(got, token)).reshape(2, 2, window, LANES)
    cut = window // 32 * 16
    one, two = blocks[:, :, :cut], blocks[:, :, cut:]
    own_one, other_one = halves(one, 1, x)
    own_two, other_two = halves(two, 0, y)
    got_one, got_two = swap(other_one, "seq", 2), swap(other_two, "dp", 1)
    token = yield [other_one, other_two], [got_one, got_two]
    one, two = add(own_one, tie(got_one, token)), add(own_two, tie(got_two, token))
    own_one, other_one = halves(one, 0, y)
    own_two, other_two = halves(two, 1, x)
    got_one, got_two = swap(other_one, "dp", 1), swap(other_two, "seq", 2)
    token = yield [other_one, other_two], [got_one, got_two]
    one, two = add(own_one, tie(got_one, token)), add(own_two, tie(got_two, token))
    part = jnp.concatenate([one, two], axis=2).reshape(window, LANES)
    for step in toward(plane, lax.axis_size("dp") // 2):
        pairs = [(2 * a + side, 2 * b + side) for a, b in step for side in (0, 1)]
        got = lax.ppermute(part, "dp", pairs)
        token = yield [part], [got]
        part = add(part, tie(got, token))
    parts[plane] = part


def set_out(flows):
    return move_on(flows, None)


def move_on(flows, token):
    sent, got = [], []
    for flow in flows:
        try:
            out, into = flow.send(token)
        except StopIteration:
            continue
        sent += out
        got += into
    return sent, got


def vector(params, row, rows=6):
    return params[row : row + rows].reshape(1, rows * LANES)


def top_of(value):
    return None if value is None else value[:8]


def total_of(value):
    for axis in ("seq", "dp"):
        bit = 1
        while bit < lax.axis_size(axis):
            value = value + swap(value, axis, bit)
            bit *= 2
    return value


def shards(tokens, cotangent, loss_mask, segments, params, first_moment, second_moment):
    block = tokens.shape[0]
    seq_index = lax.axis_index("seq")
    core = seq_index % 2
    x = seq_index // 2
    shard_rows = first_moment.shape[0]
    total_rows = params.shape[0]
    chip = 2 * block
    device_count = lax.axis_size(("dp", "seq"))

    def chip_rows(value):
        other = swap(value, "seq", 1)
        return jnp.concatenate(
            [jnp.where(core == 0, value, other), jnp.where(core == 0, other, value)]
        )

    def unpick(value):
        low, high = value[:BLK], value[BLK:]
        got = swap(jnp.where(core == 0, high, low), "seq", 1)
        return jnp.where(
            core == 0, jnp.concatenate([low, got]), jnp.concatenate([high, got])
        )

    own_tokens = tokens.reshape(block, D)
    near_x = chip_rows(own_tokens)
    far_x = chip_rows(swap(own_tokens, "seq", 2))
    grad_low = cotangent.reshape(block, D) * loss_mask.astype(bf16)
    near_dy = chip_rows(grad_low)

    w_qkv = unpack_matrix(params, ROW_QKV, D, 3 * D, 4)
    w_out = unpack_matrix(params, ROW_WO, D, D, 2)
    w_up = unpack_matrix(params, ROW_FC, D, FF, 4)
    w_down = unpack_matrix(params, ROW_PR, FF, D, 4)
    gain_one, shift_one = vector(params, ROW_G1), vector(params, ROW_S1)
    bias_query, bias_value = vector(params, ROW_BQ), vector(params, ROW_BV)
    bias_out = vector(params, ROW_BO)
    gain_two, shift_two = vector(params, ROW_G2), vector(params, ROW_S2)
    bias_up = vector(params, ROW_BFC, 24)
    bias_down = vector(params, ROW_BPR)

    seg_row = segments.reshape(1, -1)
    seg_col = segments.reshape(-1, 1)
    near_rows = [core * BLK, (3 - core) * BLK]
    q_place = [x * chip + row for row in near_rows]
    place = jnp.stack(q_place + [core, x] + near_rows).astype(jnp.int32)
    segq = jnp.concatenate(
        [lax.dynamic_slice_in_dim(seg_row, start, BLK, 1) for start in q_place], axis=1
    )
    masks = (place, seg_row, seg_col, segq)

    near_n, near_k, near_kt, near_v, near_vt, queries = project(
        near_x, gain_one, shift_one, bias_query, bias_value, w_qkv, True
    )
    state = attend(*masks, queries, near_k, near_vt)
    far_n, far_k, far_kt, far_v, far_vt = project(
        far_x, gain_one, shift_one, bias_query, bias_value, w_qkv, False
    )
    attn, attn_t, total = attend(*masks, queries, far_k, far_vt, state)
    (
        active, d_up, two_n, d_mlp, d_attn, d_resid, d_heads, delta, block_low, vec, d_bias_up
    ) = feed(
        place, attn, attn_t, near_x, near_dy, w_out, bias_out, gain_two, shift_two, w_up, bias_up,
        w_down, bias_down,
    )
    block_output = unpick(block_low)
    up_rows = d_bias_up.reshape(24, LANES)

    core_x = jnp.stack([core, x]).astype(jnp.int32)
    parts = {}

    def grads(products, vectors, rest, row, head, tail, top, after):
        done, left = weight_grad(
            core_x, products, vectors, rest, row, head, tail, shard_rows, top, after
        )
        flows = [reduce_plane(parts, plane, *pair) for plane, pair in done.items()]
        return flows, left, down16(row) + (0 if left is None else left.shape[0])

    flow_down, left, top = grads(
        [(active, d_mlp)], [up_rows, vec], None, ROW_PR, [(0, 0, 22, 2)], [(2, 1, 18, 6)],
        total_rows, [],
    )
    set_out(flow_down)
    flow_up, left, top = grads(
        [(two_n, d_up)], [up_rows, vec], left, ROW_FC, [(0, 1, 8, 10)], [(10, 0, 0, 22)], top, []
    )
    sent_down, down = move_on(flow_down, top_of(left))
    sent_up, up = set_out(flow_up)
    flow_out, left, top = grads(
        [(attn, d_attn)], [vec], left, ROW_WO, [], [(8, 0, 0, 8)], top, sent_down + sent_up
    )
    sent_out, out = set_out(flow_out)

    given = (*masks, queries, d_heads, total, delta)
    sent_up, up = move_on(flow_up, None)
    d_far, dq_t = attend_back(*given, (far_k, far_kt, far_v), None, sent_out + sent_up)
    sent_down, down_next = move_on(flow_down, dq_t)
    sent_out, out_next = move_on(flow_out, dq_t)
    d_near = attend_back(
        *given, (near_k, near_kt, near_v), dq_t, down + out + sent_down + sent_out
    )
    sent_down, down = move_on(flow_down, d_near)
    sent_up, up_next = move_on(flow_up, d_near)
    flow_qkv, _, _ = grads(
        [(near_n, d_near), (far_n, d_far)], [], left, ROW_QKV, [], [], top,
        down_next + up + sent_down + sent_up,
    )
    sent_qkv, qkv = set_out(flow_qkv)
    sent_out, out = move_on(flow_out, sent_qkv)
    far_in, far_vec = input_back(
        place, far_x, d_far, w_qkv, gain_one, None, out_next + sent_qkv + sent_out
    )
    sent_down, down = move_on(flow_down, far_vec)
    sent_up, up = move_on(flow_up, far_vec)
    sent_qkv, qkv = move_on(flow_qkv, far_vec)
    near_in, near_vec = input_back(
        place, near_x, d_near, w_qkv, gain_one, d_resid, sent_qkv + sent_down + sent_up
    )
    sent_qkv, _ = move_on(flow_qkv, near_vec)
    vectors = total_of(tie(jnp.concatenate([near_vec + far_vec, vec[18:24]]), sent_qkv))
    bias_down_grad = vectors[24:].reshape(-1) / device_count
    far_in, near_in, _ = lax.optimization_barrier((far_in, near_in, sent_qkv))

    own, other = halves(far_in, 0, core)
    far_sum = own + swap(rounded(other), "seq", 1).astype(f32)
    from_far = swap(rounded(far_sum), "seq", 2).astype(f32)
    own, other = halves(near_in, 0, core)
    input_grad = own + swap(rounded(other), "seq", 1).astype(f32)
    input_grad = rounded(jnp.where(x == 0, input_grad + from_far, input_grad))

    own_plane = lax.axis_index("dp") // 2
    window = core_window(shard_rows)
    summed = jnp.zeros((window, LANES), bf16)
    flows = flow_down + flow_up + flow_out + flow_qkv
    while move_on(flows, None)[0]:
        pass
    for plane, part in parts.items():
        summed = jnp.where(own_plane == plane, part, summed)
    summed = summed.astype(f32)
    summed = jnp.where(core == 0, summed[:shard_rows], summed[window - shard_rows :])

    first_row = lax.axis_index(("dp", "seq")) * shard_rows
    margin = 16
    spread = jnp.zeros((shard_rows + 2 * margin, LANES), f32)
    for at, row in ((0, ROW_G1), (12, ROW_BQ)):
        start = jnp.clip(row - first_row + margin, 0, shard_rows + margin)
        spread = lax.dynamic_update_slice(spread, vectors[at : at + 12], (start, 0))
    grads_mean = (summed + spread[margin : margin + shard_rows]) / device_count
    own_params = lax.dynamic_slice_in_dim(params, first_row, shard_rows, 0)
    new_first = first_decay * first_moment + (1.0 - first_decay) * grads_mean
    new_second = second_decay * second_moment + (1.0 - second_decay) * grads_mean * grads_mean
    fix_one = 1.0 - first_decay**STEP
    fix_two = 1.0 - second_decay**STEP
    update = new_first / fix_one / (jnp.sqrt(new_second / fix_two) + adam_epsilon)
    row = first_row + iota((shard_rows, LANES), 0)
    in_matrix = jnp.zeros(row.shape, bool)
    for start, end in (
        (ROW_QKV, ROW_BQ),
        (ROW_WO, ROW_BO),
        (ROW_FC, ROW_BFC),
        (ROW_PR, ROW_BPR),
    ):
        in_matrix = in_matrix | ((row >= start) & (row < end))
    new_params = own_params - jnp.where(in_matrix, base_rate / D, base_rate) * update
    return (
        block_output.reshape(tokens.shape),
        input_grad.reshape(tokens.shape),
        new_params,
        new_first,
        new_second,
        bias_down_grad,
    )


def solution(mesh):
    return jax.shard_map(
        shards,
        mesh=mesh,
        in_specs=(
            P("seq", "dp", None),
            P("seq", "dp", None),
            P("seq", "dp"),
            P(None, "dp"),
            P(),
            P(("dp", "seq"), None),
            P(("dp", "seq"), None),
        ),
        out_specs=(
            P("seq", "dp", None),
            P("seq", "dp", None),
            P(("dp", "seq"), None),
            P(("dp", "seq"), None),
            P(("dp", "seq"), None),
            P(),
        ),
        check_vma=False,
    )
```

```python
from functools import partial
import math

import jax
import jax.numpy as jnp
from jax import lax
from jax.experimental import pallas as pl
from jax.experimental.pallas import tpu as pltpu
from jax.sharding import PartitionSpec as P

D = 768
HEADS = 12
HEAD_DIM = 64
FF = 3072
STEP = 4
LANES = 128
BLK = 256

norm_epsilon = 1e-05
branch_scale = 48.0 ** (-0.5)
first_decay = 0.9
second_decay = 0.95
adam_epsilon = 1e-08
base_rate = 0.1
masked_score = -1e30
LOG2E = 1.4426950408889634
score_factor = LOG2E / HEAD_DIM

f32 = jnp.float32
bf16 = jnp.bfloat16

ROW_G1, ROW_S1 = 0, 6
ROW_QKV = 12
ROW_BQ = ROW_QKV + D * 3 * D // LANES
ROW_BV = ROW_BQ + 6
ROW_WO = ROW_BV + 6
ROW_BO = ROW_WO + D * D // LANES
ROW_G2, ROW_S2 = ROW_BO + 6, ROW_BO + 12
ROW_FC = ROW_BO + 18
ROW_BFC = ROW_FC + D * FF // LANES
ROW_PR = ROW_BFC + FF // LANES
ROW_BPR = ROW_PR + D * FF // LANES
ROW_END = ROW_BPR + 6

VMEM = 56 * 1024 * 1024


nt_dims = (((1,), (1,)), ((), ()))
nn_dims = (((1,), (0,)), ((), ()))
tn_dims = (((0,), (0,)), ((), ()))

smem = pl.BlockSpec(memory_space=pltpu.SMEM)
vmem = pl.BlockSpec(memory_space=pltpu.VMEM)
anywhere = pl.BlockSpec(memory_space=pl.ANY)


def params_of(mebibytes):
    return pltpu.CompilerParams(vmem_limit_bytes=mebibytes << 20)


def cost(flops, moved):
    return pl.CostEstimate(flops=int(flops), bytes_accessed=int(moved), transcendentals=0)


def few_rows(count):
    return pl.BlockSpec((count, LANES), lambda *_: (0, 0))


def row_of(ref, start, rows=6):
    return jnp.concatenate([ref[start + j : start + j + 1, :] for j in range(rows)], axis=1)


def column_of(row):
    return jnp.broadcast_to(row, (8, row.shape[1])).T[:, :1]


def dot(a, b, dims=nn_dims):
    return lax.dot_general(a, b, dims, preferred_element_type=f32)


def iota(shape, axis):
    return lax.broadcasted_iota(jnp.int32, shape, axis)


def kernel_call(body, operands, in_specs, after=(), **options):
    count = len(operands)

    def without(*refs):
        body(*refs[:count], *refs[count + len(after) :])

    return pl.pallas_call(without, in_specs=in_specs + [anywhere] * len(after), **options)(
        *operands, *after
    )


def down16(row):
    return row // 16 * 16


def group_rows(blocks):
    return 8 if blocks > 8 else 32


def side_by_side(value, other):
    return jnp.concatenate([value, other], axis=1)


def unpack_body(x_ref, o_ref, move, *, shift, rows, blocks, pairs):
    size = rows * blocks
    bits = rows.bit_length() - 1

    @pl.when(pl.program_id(0) == 0)
    def _():
        to, come = iota(move.shape, 0), iota(move.shape, 1)
        move[...] = (come == shift + (to & (rows - 1)) * blocks + (to >> bits)).astype(bf16)

    for n in range(pairs):
        both = side_by_side(
            *[x_ref[pl.ds((2 * n + side) * size, size + 16), :].astype(bf16) for side in (0, 1)]
        )
        moved = dot(move[...], both)
        for j in range(blocks):
            part = moved[j * rows : (j + 1) * rows]
            part = jnp.concatenate([part[:, :LANES], part[:, LANES:]], axis=0).astype(bf16)
            o_ref[2 * n * rows : 2 * (n + 1) * rows, j * LANES : (j + 1) * LANES] = part


def take_body(*refs):
    count = len(refs) // 2
    for x_ref, o_ref in zip(refs[:count], refs[count:]):
        o_ref[...] = x_ref[...]


def take_rows(params, runs):
    runs = [(first // 8 * 8, count) for first, count in runs]

    def window(first, count):
        return pl.BlockSpec((pl.Element(count), pl.Element(LANES)), lambda i: (first, 0))

    return pl.pallas_call(
        take_body,
        grid=(1,),
        in_specs=[window(first, count) for first, count in runs],
        out_specs=[pl.BlockSpec((count, LANES), lambda i: (0, 0)) for _, count in runs],
        out_shape=[jax.ShapeDtypeStruct((count, LANES), f32) for _, count in runs],
        compiler_params=params_of(48),
    )(*[params] * len(runs))


def unpack_matrix(params, row, matrix_rows, columns, steps):
    blocks = columns // LANES
    rows = group_rows(blocks)
    base = row // 8 * 8
    chunk = matrix_rows // steps
    size = chunk * blocks
    return pl.pallas_call(
        partial(
            unpack_body, shift=row - base, rows=rows, blocks=blocks, pairs=chunk // rows // 2
        ),
        grid=(steps,),
        in_specs=[
            pl.BlockSpec(
                (pl.Element(size + 16), pl.Element(LANES)),
                lambda i: (pl.multiple_of(base + i * size, 8), 0),
            )
        ],
        out_specs=pl.BlockSpec((chunk, columns), lambda i: (i, 0)),
        out_shape=jax.ShapeDtypeStruct((matrix_rows, columns), bf16),
        scratch_shapes=[pltpu.VMEM((rows * blocks, rows * blocks + 16), bf16)],
        compiler_params=params_of(38),
        cost_estimate=cost(8e9, 6 * matrix_rows * columns),
    )(params)


def grad_body(
    core_ref,
    *refs,
    products,
    vectors,
    below,
    rest,
    base,
    row,
    matrix_rows,
    columns,
    head,
    tail,
    planes,
    plane_rows,
    keep,
):
    refs = list(refs)
    factors = [refs.pop(0) for _ in range(2 * len(products))]
    vector_refs = [refs.pop(0) for _ in range(vectors)]
    below_ref = refs.pop(0) if below else None
    rest_ref = refs.pop(0) if rest else None
    own_ref, other_ref = (refs.pop(0), refs.pop(0)) if planes else (None, None)
    keep_ref = refs.pop(0) if keep else None
    window, grad, move, carry, last = refs
    blocks = columns // LANES
    rows = group_rows(blocks)
    bits = rows.bit_length() - 1
    size = rows * blocks
    shift = row - base
    body_rows = matrix_rows * blocks
    tail_rows = last.shape[0]
    if below:
        window[pl.ds(0, below), :] = below_ref[...]
    if rest:
        window[pl.ds(below + body_rows + tail_rows, rest), :] = rest_ref[...]
    to, come = iota(move.shape, 0), iota(move.shape, 1)
    move[...] = (to == shift + (come & (rows - 1)) * blocks + (come >> bits)).astype(bf16)
    carry[...] = jnp.zeros_like(carry)
    last[...] = jnp.zeros_like(last)
    for place, n, start, count in head:
        carry[place : place + count, :] = vector_refs[n][start : start + count, :]
    for place, n, start, count in tail:
        last[place : place + count, :] = vector_refs[n][start : start + count, :]

    core = core_ref[0]
    wide_rows = grad.shape[0]

    def multiply(c, state):
        lanes = pl.ds(pl.multiple_of(c * wide_rows, wide_rows), wide_rows)
        for n, (at, far) in enumerate(products):
            a_ref, b_ref = factors[2 * n], factors[2 * n + 1]
            span = slice(at, at + b_ref.shape[1])
            if far:

                @pl.when(core_ref[1] == 1)
                def _():
                    grad[:, span] += dot(a_ref[:, lanes], b_ref[...], tn_dims)

            else:
                grad[:, span] = dot(a_ref[:, lanes], b_ref[...], tn_dims)

        left = carry[...]
        for pair in range(wide_rows // rows // 2):
            both = side_by_side(
                *[
                    jnp.concatenate(
                        [
                            grad[at : at + rows, j * LANES : (j + 1) * LANES]
                            for j in range(blocks)
                        ],
                        axis=0,
                    ).astype(bf16)
                    for at in (2 * pair * rows, (2 * pair + 1) * rows)
                ]
            )
            moved = dot(move[...], both)
            for side in (0, 1):
                part = moved[:, side * LANES : (side + 1) * LANES]
                at = (c * (wide_rows // rows) + 2 * pair + side) * size + below
                at = pl.multiple_of(at, 16)
                window[pl.ds(at, 16), :] = (part[:16] + left).astype(bf16)
                window[pl.ds(at + 16, size - 16), :] = part[16:size].astype(bf16)
                left = part[size:]
        carry[...] = left
        return state

    lax.fori_loop(0, matrix_rows // wide_rows, multiply, 0)
    last[pl.ds(0, 16), :] = last[pl.ds(0, 16), :] + carry[...]
    window[pl.ds(below + body_rows, tail_rows), :] = last[...].astype(bf16)
    half = plane_rows // 4
    for n, plane in enumerate(planes):
        part_rows = own_ref.shape[1]
        for block in range(4):
            for ref, which in ((own_ref, core), (other_ref, 1 - core)):
                at = plane * plane_rows - (base - below) + block * half
                at = pl.multiple_of(at + which * (half - part_rows), 16)
                ref[4 * n + block] = window[pl.ds(at, part_rows), :]
    if keep:
        keep_ref[...] = window[pl.ds(0, keep), :]


def weight_grad(
    place, products, vectors, below, rest, row, head, tail, shard_rows, top, after, work,
    whole=True,
):
    base = down16(row)
    matrix_rows = products[0][0].shape[1]
    columns = max(at + b.shape[1] for _, b, at, _ in products)
    blocks = columns // LANES
    rows = group_rows(blocks)
    size = rows * blocks
    plane_rows = 8 * shard_rows
    below_rows = 0 if below is None else below.shape[0]
    rest_rows = 0 if rest is None else rest.shape[0]
    first_row = base - below_rows
    tail_rows = top - rest_rows - base - matrix_rows * blocks
    first_plane = -(-first_row // plane_rows)
    planes = list(range(first_plane, top // plane_rows)) if whole else []
    keep = first_plane * plane_rows - first_row if whole else top - first_row
    part = jax.ShapeDtypeStruct((4 * len(planes), core_window(shard_rows), LANES), bf16)
    out_shape = [part, part] if planes else []
    if keep:
        out_shape.append(jax.ShapeDtypeStruct((keep, LANES), bf16))
    operands = [value for pair in products for value in pair[:2]] + list(vectors)
    operands += [value for value in (below, rest) if value is not None]
    outs = kernel_call(
        partial(
            grad_body,
            products=[pair[2:] for pair in products],
            vectors=len(vectors),
            below=below_rows,
            rest=rest_rows,
            base=base,
            row=row,
            matrix_rows=matrix_rows,
            columns=columns,
            head=head,
            tail=tail,
            planes=planes,
            plane_rows=plane_rows,
            keep=keep,
        ),
        [place] + operands,
        [smem] + [vmem] * len(operands),
        after,
        out_specs=[vmem] * len(out_shape),
        out_shape=out_shape,
        scratch_shapes=[
            pltpu.VMEM((top - first_row, LANES), bf16),
            pltpu.VMEM((256 if columns < 3 * D or columns == FF else 128, columns), f32),
            pltpu.VMEM((size + 16, size), bf16),
            pltpu.VMEM((16, LANES), f32),
            pltpu.VMEM((tail_rows, LANES), f32),
        ],
        compiler_params=params_of(16),
        cost_estimate=cost(work, 4 * matrix_rows * columns),
    )
    return planes, tuple(outs[:2]) if planes else None, outs[-1] if keep else None


def row_mean(value):
    return jnp.sum(value, axis=-1, keepdims=True) * (1.0 / value.shape[-1])


def norm_parts(values):
    center = values - row_mean(values)
    rstd = lax.rsqrt(row_mean(center * center) + norm_epsilon)
    return center * rstd, rstd


def norm_back(unit, rstd, gain, grad):
    scaled = grad * gain
    return rstd * (scaled - row_mean(scaled) - unit * row_mean(scaled * unit))


def project_body(place_ref, own_ref, got_ref, norm_ref, bias_ref, w_ref, *outs, with_query):
    n_ref, k_ref, kt_ref, v_ref, vt_ref = outs[:5]
    mine = pl.program_id(0) // 2 == place_ref[2]
    x = jnp.where(mine, own_ref[...], got_ref[...])
    unit, _ = norm_parts(x.astype(f32))
    normed = (unit * row_of(norm_ref, 0) + row_of(norm_ref, 6)).astype(bf16)
    n_ref[...] = normed
    keys = dot(normed, w_ref[:, D : 2 * D]).astype(bf16)
    k_ref[...] = keys
    kt_ref[...] = keys.T
    bias = ROW_BQ % 8
    values = (dot(normed, w_ref[:, 2 * D :]) + row_of(bias_ref, bias + 6)).astype(bf16)
    v_ref[...] = values
    vt_ref[...] = values.T
    if with_query:
        outs[5][...] = (dot(normed, w_ref[:, :D]) + row_of(bias_ref, bias)).astype(bf16)


def project(place, own, got, norm_rows, bias_rows, w_qkv, with_query):
    count = 2 * own.shape[0]
    half = own.shape[0] // BLK
    by_rows = pl.BlockSpec((BLK, D), lambda i: (i, 0))
    by_halves = pl.BlockSpec((BLK, D), lambda i: (i % half, 0))
    by_columns = pl.BlockSpec((D, BLK), lambda i: (0, i))
    tall = jax.ShapeDtypeStruct((count, D), bf16)
    wide = jax.ShapeDtypeStruct((D, count), bf16)
    return pl.pallas_call(
        partial(project_body, with_query=with_query),
        grid=(count // BLK,),
        in_specs=[
            smem,
            by_halves,
            by_halves,
            few_rows(16),
            few_rows(16),
            pl.BlockSpec((D, 3 * D), lambda i: (0, 0)),
        ],
        out_specs=[by_rows, by_rows, by_columns, by_rows, by_columns]
        + [by_rows] * with_query,
        out_shape=[tall, tall, wide, tall, wide] + [tall] * with_query,
        compiler_params=params_of(12),
        cost_estimate=cost(2 * count * D * (2 + with_query) * D, 12 * count * D),
    )(place, own, got, norm_rows, bias_rows, w_qkv)


def head_lanes(value, odd):
    lane = iota(value.shape, 1)
    keep = (lane >= HEAD_DIM) if odd else (lane < HEAD_DIM)
    return jnp.where(keep, value, jnp.zeros_like(value))


def visit_block(place_ref, seg_ref, segs_ref, bias_ref, i, k_start, valid, step):
    q_start = place_ref[i]
    q_first = seg_ref[0, q_start]
    q_last = seg_ref[0, q_start + BLK - 1]
    k_first = seg_ref[0, k_start]
    k_last = seg_ref[0, k_start + BLK - 1]
    active = valid & (k_start <= q_start) & (k_last >= q_first)
    plain = (k_first == q_last) & (k_start + BLK <= q_start)

    @pl.when(active & plain)
    def _():
        step(False)

    @pl.when(active & jnp.logical_not(plain))
    def _():
        k_pos = k_start + iota((BLK, BLK), 0)
        q_pos = q_start + iota((BLK, BLK), 1)
        segk = column_of(segs_ref[:, pl.ds(pl.multiple_of(k_start, BLK), BLK)])
        same = segk == segs_ref[:, pl.ds(pl.multiple_of(q_start, BLK), BLK)]
        bias_ref[...] = jnp.where((k_pos <= q_pos) & same, 0.0, masked_score)
        step(True)


ACC = HEAD_DIM + 16


def attend_body(
    place_ref, seg_ref, segs_ref, q_ref, k_ref, vt_ref, *refs, first
):
    if first:
        acc_ref, top_ref, bias_ref, s_ref = refs
        acc_ref[...] = jnp.zeros_like(acc_ref)
        top_ref[...] = jnp.full_like(top_ref, masked_score)
    else:
        acc_in, top_in, out_ref, outt_ref, total_ref, bias_ref, s_ref, acc_ref, top_ref = refs
        acc_ref[...] = acc_in[...]
        top_ref[...] = top_in[...]
    ones = jnp.ones((16, BLK), bf16)
    count = k_ref.shape[0] // BLK
    x = place_ref[3]
    base = x * (count * BLK) if first else 0 * x
    valid = (x >= 0) if first else (x == 1)
    for i in range(2):
        cols = slice(i * BLK, (i + 1) * BLK)

        def visit(n, carry):
            kb = count - 1 - n
            k_rows = pl.ds(pl.multiple_of(kb * BLK, BLK), BLK)
            q_rows = pl.ds(pl.multiple_of(place_ref[4 + i], BLK), BLK)

            def step(masked):
                tops = []
                for h in range(HEADS):
                    pair, odd = h // 2, h % 2
                    lanes = slice(pair * LANES, (pair + 1) * LANES)
                    s = dot(k_ref[k_rows, lanes], head_lanes(q_ref[q_rows, lanes], odd), nt_dims)
                    s = s * score_factor
                    if masked:
                        s = s + bias_ref[...]
                    s_ref[h] = s
                    tops.append(jnp.max(s, axis=0, keepdims=True))
                old = top_ref[:HEADS, cols]
                new = jnp.maximum(old, jnp.concatenate(tops, axis=0))
                top_ref[:HEADS, cols] = new
                scale = jnp.exp2(old - new)
                for h in range(HEADS):
                    p = jnp.exp2(s_ref[h] - new[h : h + 1]).astype(bf16)
                    v_part = jnp.concatenate(
                        [vt_ref[h * HEAD_DIM : (h + 1) * HEAD_DIM, k_rows], ones], axis=0
                    )
                    acc_ref[h, :, cols] = acc_ref[h, :, cols] * scale[h : h + 1] + dot(v_part, p)

            visit_block(
                place_ref, seg_ref, segs_ref, bias_ref, i, base + kb * BLK, valid, step
            )
            return carry

        lax.fori_loop(0, count, visit, 0)
    if not first:
        for h in range(HEADS):
            total = acc_ref[h, HEAD_DIM : HEAD_DIM + 1, :]
            outt_ref[h * HEAD_DIM : (h + 1) * HEAD_DIM, :] = acc_ref[h, :HEAD_DIM, :] / total
            total_ref[h : h + 1, :] = top_ref[h : h + 1, :] + jnp.log2(total)
        for i in range(2):
            cols = slice(i * BLK, (i + 1) * BLK)
            out_ref[cols, :] = outt_ref[:, cols].T.astype(bf16)


def attend(place, seg, segs, q, k, vt, state=None):
    count = 2 * BLK
    first = state is None
    acc_shape = jax.ShapeDtypeStruct((HEADS, ACC, count), f32)
    row_shape = jax.ShapeDtypeStruct((16, count), f32)
    if first:
        outs = (acc_shape, row_shape)
    else:
        outs = (
            jax.ShapeDtypeStruct((count, D), bf16),
            jax.ShapeDtypeStruct((D, count), f32),
            row_shape,
        )
    extra = () if first else state
    held = [] if first else [pltpu.VMEM((HEADS, ACC, count), f32), pltpu.VMEM((16, count), f32)]
    return pl.pallas_call(
        partial(attend_body, first=first),
        in_specs=[smem, smem] + [vmem] * (4 + len(extra)),
        out_specs=(vmem,) * len(outs),
        out_shape=outs,
        scratch_shapes=[pltpu.VMEM((BLK, BLK), f32), pltpu.VMEM((HEADS, BLK, BLK), f32)] + held,
        compiler_params=params_of(14),
        cost_estimate=cost(15e9, 8e6),
    )(place, seg, segs, q, k, vt, *extra)


def two_heads(value):
    return jnp.concatenate([head_lanes(value, 0), head_lanes(value, 1)], axis=0)


def attend_back_body(
    place_ref, seg_ref, segs_ref, q_ref, do_ref, total_ref, delta_ref, k_ref, kt_ref,
    v_ref, *refs, near
):
    if near:
        out_ref, dqt_ref, bias_ref, dk_acc, dv_acc, q_two, do_two, s_ref, da_ref = refs
        dqt_ref[...] = jnp.zeros_like(dqt_ref)
    else:
        dqt_in, out_ref, dq_ref, bias_ref, dk_acc, dv_acc, q_two, do_two, s_ref, da_ref, dqt_ref = (
            refs
        )
        dqt_ref[...] = dqt_in[...]
        dq_ref[...] = jnp.zeros_like(dq_ref)
    count = k_ref.shape[0] // BLK
    x = place_ref[3]
    base = x * (count * BLK) if near else 0 * x
    valid = (x >= 0) if near else (x == 1)
    pairs = HEADS // 2

    @pl.when(valid)
    def _():
        for i in range(2):
            q_rows = pl.ds(pl.multiple_of(place_ref[4 + i], BLK), BLK)
            for pair in range(pairs):
                lanes = slice(pair * LANES, (pair + 1) * LANES)
                q_two[i, pair] = two_heads(q_ref[q_rows, lanes])
                do_two[i, pair] = two_heads(do_ref[i * BLK : (i + 1) * BLK, lanes])

    def visit(kb, carry):
        k_rows = pl.ds(pl.multiple_of(kb * BLK, BLK), BLK)
        dk_acc[...] = jnp.zeros_like(dk_acc)
        dv_acc[...] = jnp.zeros_like(dv_acc)
        for i in range(2):
            cols = slice(i * BLK, (i + 1) * BLK)

            def step(masked):
                def row_two(ref, pair):
                    return jnp.concatenate(
                        [ref[2 * pair : 2 * pair + 1, cols], ref[2 * pair + 1 : 2 * pair + 2, cols]],
                        axis=1,
                    )

                def scores(pair):
                    lanes = slice(pair * LANES, (pair + 1) * LANES)
                    s_ref[pair % 2] = dot(k_ref[k_rows, lanes], q_two[i, pair], nt_dims)
                    da_ref[pair % 2] = dot(v_ref[k_rows, lanes], do_two[i, pair], nt_dims)

                scores(0)
                for pair in range(pairs):
                    if pair + 1 < pairs:
                        scores(pair + 1)
                    lanes = slice(pair * LANES, (pair + 1) * LANES)
                    s = s_ref[pair % 2] * score_factor
                    if masked:
                        s = s + jnp.concatenate([bias_ref[...], bias_ref[...]], axis=1)
                    p = jnp.exp2(s - row_two(total_ref, pair))
                    ds = (p * (da_ref[pair % 2] - row_two(delta_ref, pair))).astype(bf16)
                    dv_acc[:, lanes] += dot(p.astype(bf16), do_two[i, pair])
                    dk_acc[:, lanes] += dot(ds, q_two[i, pair])
                    for odd in range(2):
                        h = 2 * pair + odd
                        head = slice(h * HEAD_DIM, (h + 1) * HEAD_DIM)
                        dqt_ref[head, cols] += dot(
                            kt_ref[head, k_rows], ds[:, odd * BLK : (odd + 1) * BLK]
                        )

            visit_block(
                place_ref, seg_ref, segs_ref, bias_ref, i, base + kb * BLK, valid, step
            )
        out_ref[k_rows, :D] = (dk_acc[...] * (1.0 / HEAD_DIM)).astype(bf16)
        out_ref[k_rows, D:] = dv_acc[...].astype(bf16)
        return carry

    lax.fori_loop(0, count, visit, 0)
    if not near:
        for i in range(2):
            q_rows = pl.ds(pl.multiple_of(place_ref[4 + i], BLK), BLK)
            part = dqt_ref[:, i * BLK : (i + 1) * BLK] * (1.0 / HEAD_DIM)
            dq_ref[q_rows, :] = part.T.astype(bf16)


def attend_back(place, seg, segs, q, do, total, delta, keys, dqt, after):
    near = dqt is None
    rows = q.shape[0]
    two = pltpu.VMEM((2, HEADS // 2, 2 * BLK, LANES), bf16)
    wide = pltpu.VMEM((2, BLK, 2 * BLK), f32)
    sums_of = pltpu.VMEM((BLK, D), f32)
    blocks = [pltpu.VMEM((BLK, BLK), f32), sums_of, sums_of, two, two, wide, wide]
    sums = jax.ShapeDtypeStruct((D, 2 * BLK), f32)
    operands = [place, seg, segs, q, do, total, delta, *keys] + ([] if near else [dqt])
    return kernel_call(
        partial(attend_back_body, near=near),
        operands,
        [smem, smem] + [vmem] * (len(operands) - 2),
        after,
        out_specs=[vmem] * 2,
        out_shape=[
            jax.ShapeDtypeStruct((rows, 2 * D), bf16),
            sums if near else jax.ShapeDtypeStruct((rows, D), bf16),
        ],
        scratch_shapes=blocks + ([] if near else [pltpu.VMEM((D, 2 * BLK), f32)]),
        compiler_params=params_of(16),
        cost_estimate=cost(30e9, 1e7),
    )


GELU_A = math.sqrt(2.0 / math.pi)
GELU_B = 0.044715
FF_BLK = 512
FF_PART = 256


def put_rows(ref, at, value):
    for j in range(value.shape[1] // LANES):
        ref[at + j : at + j + 1, :] = value[:, j * LANES : (j + 1) * LANES]


def column_sum(value):
    return jnp.sum(value, axis=0, keepdims=True)


def feed_body(
    place_ref, attn_ref, outt_ref, xo_ref, xg_ref, dyo_ref, dyg_ref, wo_ref, two_vec, wu_ref,
    bu_ref, wd_ref, bd_ref,
    act_ref, dup_ref, two_ref, dmlp_ref, dattn_ref, dresid_ref, dheads_ref, delta_ref, block_ref,
    vec_ref, dbu_ref,
    r1, unit, rstd, ym, dtwo,
):
    step = pl.program_id(0)
    core = place_ref[2]

    def picked(own_ref, got_ref, i):
        return jnp.where(core == i, own_ref[:BLK, :], got_ref[BLK:, :])

    @pl.when(step == 0)
    def _():
        for i in range(2):
            rows = slice(i * BLK, (i + 1) * BLK)
            ya = dot(attn_ref[rows, :], wo_ref[...]) + row_of(two_vec, 0)
            resid = picked(xo_ref, xg_ref, i).astype(f32) + branch_scale * ya
            r1[rows, :] = resid
            one, inverse = norm_parts(resid)
            unit[rows, :] = one
            rstd[rows, :] = inverse
            two_ref[rows, :] = (one * row_of(two_vec, 6) + row_of(two_vec, 12)).astype(bf16)
            dy = picked(dyo_ref, dyg_ref, i).astype(f32)
            dmlp_ref[rows, :] = (branch_scale * dy).astype(bf16)
        ym[...] = jnp.zeros_like(ym)
        dtwo[...] = jnp.zeros_like(dtwo)

    two, dmlp = two_ref[...], dmlp_ref[...]
    parts = [slice(n, n + FF_PART) for n in range(0, FF_BLK, FF_PART)]

    lane_rows = FF_BLK // LANES
    bias = bu_ref[pl.ds(ROW_BFC % 8 + step * lane_rows, lane_rows), :]
    bias = jnp.concatenate([bias[j : j + 1, :] for j in range(lane_rows)], axis=1)

    def ahead(part):
        return dot(two, wu_ref[:, part]) + bias[:, part], dot(dmlp, wd_ref[part, :], nt_dims)

    ready = ahead(parts[0])
    for n, part in enumerate(parts):
        u, dact = ready
        if n + 1 < len(parts):
            ready = ahead(parts[n + 1])
        square = u * u
        t = jnp.tanh(u * (GELU_A + (GELU_A * GELU_B) * square))
        half = 0.5 + 0.5 * t
        act = (u * half).astype(bf16)
        act_ref[:, part] = act
        slope = half + u * (half * (1.0 - t)) * (GELU_A + (3.0 * GELU_A * GELU_B) * square)
        dup = dact * slope
        dup_low = dup.astype(bf16)
        dup_ref[:, part] = dup_low
        put_rows(dbu_ref, part.start // LANES, column_sum(dup_low.astype(f32)))
    ym[...] += dot(act_ref[...], wd_ref[...])
    dtwo[...] += dot(dup_ref[...], wu_ref[...], nt_dims)

    @pl.when(step == pl.num_programs(0) - 1)
    def _():
        dg = jnp.zeros((1, D), f32)
        ds = jnp.zeros((1, D), f32)
        db = jnp.zeros((1, D), f32)
        dbd = jnp.zeros((1, D), f32)
        for i in range(2):
            rows = slice(i * BLK, (i + 1) * BLK)
            down = ym[rows, :] + row_of(bd_ref, ROW_BPR % 8)
            block_ref[rows, :] = (r1[rows, :] + branch_scale * down).astype(bf16)
            grad = dtwo[rows, :]
            one = unit[rows, :]
            dy = picked(dyo_ref, dyg_ref, i).astype(f32)
            dresid = dy + norm_back(one, rstd[rows, :], row_of(two_vec, 6), grad)
            dresid_ref[rows, :] = dresid
            dattn = (branch_scale * dresid).astype(bf16)
            dattn_ref[rows, :] = dattn
            dg = dg + column_sum(grad * one)
            ds = ds + column_sum(grad)
            db = db + column_sum(dattn.astype(f32))
            dbd = dbd + column_sum(dmlp_ref[rows, :].astype(f32))
            dheads_ref[rows, :] = dot(dattn, wo_ref[...], nt_dims).astype(bf16)
            back = dot(wo_ref[...], dattn, nt_dims).astype(bf16).astype(f32)
            both = back * outt_ref[:, rows]
            for h in range(HEADS):
                delta_ref[h : h + 1, rows] = column_sum(both[h * HEAD_DIM : (h + 1) * HEAD_DIM])
        vec_ref[...] = jnp.zeros_like(vec_ref)
        put_rows(vec_ref, 0, db)
        put_rows(vec_ref, 6, dg)
        put_rows(vec_ref, 12, ds)
        put_rows(vec_ref, 18, dbd)


def feed(place, attn, attn_t, x_own, x_got, dy_own, dy_got, rows, w_out, w_up, w_down):
    count = attn.shape[0]

    def whole(*shape):
        return pl.BlockSpec(shape, lambda k: (0,) * len(shape))

    wide = pl.BlockSpec((count, FF_BLK), lambda k: (0, k))
    tall = whole(count, D)
    steps = FF // FF_BLK
    lane_rows = FF_BLK // LANES
    shapes = [
        ((count, FF), bf16, wide),
        ((count, FF), bf16, wide),
        ((count, D), bf16, tall),
        ((count, D), bf16, tall),
        ((count, D), bf16, tall),
        ((count, D), f32, tall),
        ((count, D), bf16, tall),
        ((16, count), f32, whole(16, count)),
        ((count, D), bf16, tall),
        ((24, LANES), f32, whole(24, LANES)),
        (
            (steps, lane_rows, LANES),
            f32,
            pl.BlockSpec((pl.Squeezed(), lane_rows, LANES), lambda k: (k, 0, 0)),
        ),
    ]
    return pl.pallas_call(
        feed_body,
        grid=(steps,),
        in_specs=[
            smem,
            tall,
            whole(D, count),
            tall,
            tall,
            tall,
            tall,
            whole(D, D),
            few_rows(24),
            pl.BlockSpec((D, FF_BLK), lambda k: (0, k)),
            few_rows(32),
            pl.BlockSpec((FF_BLK, D), lambda k: (k, 0)),
            few_rows(8),
        ],
        out_specs=[spec for _, _, spec in shapes],
        out_shape=[jax.ShapeDtypeStruct(shape, kind) for shape, kind, _ in shapes],
        scratch_shapes=[
            pltpu.VMEM((count, D), f32),
            pltpu.VMEM((count, D), f32),
            pltpu.VMEM((count, 1), f32),
            pltpu.VMEM((count, D), f32),
            pltpu.VMEM((count, D), f32),
        ],
        compiler_params=params_of(20),
        cost_estimate=cost(40e9, 2e7),
    )(
        place, attn, attn_t, x_own, x_got, dy_own, dy_got, w_out, rows[0], w_up, rows[1], w_down,
        rows[2],
    )


def input_body(place_ref, own_ref, got_ref, dp_ref, w_ref, gain_ref, *refs, near):
    if near:
        dq_ref, dresid_ref, out_ref, vec_ref, dg, ds, dbq, dbv = refs
    else:
        out_ref, vec_ref, dg, ds, dbq, dbv = refs
    step = pl.program_id(0)

    @pl.when(step == 0)
    def _():
        for ref in (dg, ds, dbq, dbv):
            ref[...] = jnp.zeros_like(ref)

    mine = step // 2 == place_ref[2]
    x = jnp.where(mine, own_ref[...], got_ref[...])
    unit, rstd = norm_parts(x.astype(f32))
    gain = row_of(gain_ref, 0)
    grad = dot(dp_ref[...], w_ref[:, D:], nt_dims)
    if near:
        grad = grad + dot(dq_ref[...], w_ref[:, :D], nt_dims)
    dg[...] += column_sum(grad * unit)
    ds[...] += column_sum(grad)
    dbv[...] += column_sum(dp_ref[:, D:].astype(f32))
    if near:
        dbq[...] += column_sum(dq_ref[...].astype(f32))
    out_ref[...] = norm_back(unit, rstd, gain, grad)
    if near:
        for i in range(2):

            @pl.when(step * BLK == place_ref[4 + i])
            def _():
                out_ref[...] += dresid_ref[i * BLK : (i + 1) * BLK, :]

    @pl.when(step == pl.num_programs(0) - 1)
    def _():
        put_rows(vec_ref, 0, dg[...])
        put_rows(vec_ref, 6, ds[...])
        put_rows(vec_ref, 12, dbq[...])
        put_rows(vec_ref, 18, dbv[...])


def input_back(place, own, got, dp, w_qkv, norm_rows, near_parts, after):
    near = len(near_parts) > 0
    count, wide = dp.shape
    return kernel_call(
        partial(input_body, near=near),
        [place, own, got, dp, w_qkv, norm_rows] + near_parts,
        [
            smem,
            pl.BlockSpec((BLK, D), lambda i: (i % 2, 0)),
            pl.BlockSpec((BLK, D), lambda i: (i % 2, 0)),
            pl.BlockSpec((BLK, wide), lambda i: (i, 0)),
            pl.BlockSpec((D, 3 * D), lambda i: (0, 0)),
            few_rows(16),
        ]
        + [pl.BlockSpec((BLK, D), lambda i: (i, 0)), pl.BlockSpec((2 * BLK, D), lambda i: (0, 0))]
        * near,
        after,
        grid=(count // BLK,),
        out_specs=[
            pl.BlockSpec((BLK, D), lambda i: (i, 0)),
            pl.BlockSpec((24, LANES), lambda i: (0, 0)),
        ],
        out_shape=[
            jax.ShapeDtypeStruct((count, D), f32),
            jax.ShapeDtypeStruct((24, LANES), f32),
        ],
        scratch_shapes=[pltpu.VMEM((1, D), f32)] * 4,
        compiler_params=params_of(10),
        cost_estimate=cost(2 * count * wide * D, 10 * count * D),
    )


def rounded(value):
    return lax.reduce_precision(value, 8, 7).astype(bf16)


def bit_pairs(size, bit, sender=lambda place: True):
    return [(n, n ^ bit) for n in range(size) if sender(n)]


def swap(value, axis, bit):
    return lax.ppermute(value, axis, bit_pairs(lax.axis_size(axis), bit))


def halves(value, axis, which):
    size = value.shape[axis] // 2
    own = lax.dynamic_slice_in_dim(value, which * size, size, axis)
    other = lax.dynamic_slice_in_dim(value, (1 - which) * size, size, axis)
    return own, other


def total(*values):
    return rounded(sum(value.astype(f32) for value in values))


def core_window(shard_rows):
    return (shard_rows + 15) // 16 * 16


def toward(plane, size):
    if size == 4:
        return [
            [[(1, 0), (3, 2)], [(2, 0)]],
            [[(0, 1), (3, 2)], [(2, 1)]],
            [[(0, 1), (3, 2)], [(1, 2)]],
            [[(0, 1), (2, 3)], [(1, 3)]],
        ][plane]
    steps = []
    bit = 1
    while bit < size:
        away = [z for z in range(size) if (z ^ plane) & bit and not (z ^ plane) & (bit - 1)]
        steps.append([(z, z ^ bit) for z in away])
        bit *= 2
    return steps


def tie(value, token):
    return value if token is None else lax.optimization_barrier((value, token))[0]


def between_planes(value, step):
    pairs = [(2 * a + side, 2 * b + side) for a, b in step for side in (0, 1)]
    return lax.ppermute(value, "dp", pairs)


def plane_call(body, place, operands, shapes, after=()):
    operands = [place] + operands
    shapes = [jax.ShapeDtypeStruct(shape, bf16) for shape in shapes]
    return kernel_call(
        body,
        operands,
        [smem] + [vmem] * (len(operands) - 1),
        after,
        out_specs=[vmem] * len(shapes),
        out_shape=shapes,
        compiler_params=params_of(24),
        cost_estimate=cost(1e9, 1e6),
    )


def plus(a, b):
    return (a.astype(f32) + b.astype(f32)).astype(bf16)


def split_first(place_ref, own_ref, got_ref, one_ref, sent_one_ref, two_ref, sent_two_ref):
    x, y = place_ref[0], place_ref[1]
    cut = one_ref.shape[2]
    for n in range(one_ref.shape[0]):
        for side in (0, 1):
            for out, block in (
                (one_ref, 2 * side + x),
                (sent_one_ref, 2 * side + 1 - x),
            ):
                block = 4 * n + block
                out[n, side] = plus(own_ref[block, :cut, :], got_ref[block, :cut, :])
            for out, block in (
                (two_ref, 2 * y + side),
                (sent_two_ref, 2 * (1 - y) + side),
            ):
                block = 4 * n + block
                out[n, side] = plus(own_ref[block, cut:, :], got_ref[block, cut:, :])


def split_second(
    place_ref, one_ref, got_one_ref, two_ref, got_two_ref,
    one_out, sent_one_ref, two_out, sent_two_ref,
):
    x, y = place_ref[0], place_ref[1]
    for n in range(one_out.shape[0]):
        for out, left, right, at in (
            (one_out, one_ref, got_one_ref, y),
            (sent_one_ref, one_ref, got_one_ref, 1 - y),
            (two_out, two_ref, got_two_ref, x),
            (sent_two_ref, two_ref, got_two_ref, 1 - x),
        ):
            out[n] = plus(left[n, at], right[n, at])


def join_parts(place_ref, one_ref, got_one_ref, two_ref, got_two_ref, *outs):
    cut = one_ref.shape[1]
    swapped = place_ref[2] >= 2
    for n in range(one_ref.shape[0]):
        upper = plus(one_ref[n], got_one_ref[n])
        lower = plus(two_ref[n], got_two_ref[n])
        if len(outs) == 1:
            outs[0][n, :cut, :] = upper
            outs[0][n, cut:, :] = lower
        else:
            for keep, out in ((n == 0, outs[0]), (n == 1, outs[1])):

                @pl.when(swapped != keep)
                def _():
                    out[:cut, :] = upper
                    out[cut:, :] = lower


def reduce_planes(parts, planes, own, other):
    x = lax.axis_index("seq") // 2
    y = lax.axis_index("dp") % 2
    z = lax.axis_index("dp") // 2
    place = jnp.stack([x, y, z]).astype(jnp.int32)
    count, window = len(planes), own.shape[1]
    cut = window // 32 * 16
    got = swap(other, "seq", 1)
    token = yield [other], [got]
    upper, lower = (count, 2, cut, LANES), (count, 2, window - cut, LANES)
    one, sent_one, two, sent_two = plane_call(
        split_first, place, [own, tie(got, token)], [upper, upper, lower, lower]
    )
    got_one, got_two = swap(sent_one, "seq", 2), swap(sent_two, "dp", 1)
    token = yield [sent_one, sent_two], [got_one, got_two]
    upper, lower = (count, cut, LANES), (count, window - cut, LANES)
    one, sent_one, two, sent_two = plane_call(
        split_second, place, [one, tie(got_one, token), two, tie(got_two, token)],
        [upper, upper, lower, lower],
    )
    got_one, got_two = swap(sent_one, "dp", 1), swap(sent_two, "seq", 2)
    token = yield [sent_one, sent_two], [got_one, got_two]
    last = [one, tie(got_one, token), two, tie(got_two, token)]
    size = lax.axis_size("dp") // 2
    if size == 4 and planes == [1, 2]:
        mine, more = plane_call(join_parts, place, last, [(window, LANES)] * 2)
        got = [
            between_planes(mine, [(0, 1), (3, 2)]),
            between_planes(more, [(1, 2), (2, 1)]),
            between_planes(more, [(0, 2), (3, 1)]),
        ]
        token = yield [mine, more], got
        part = total(mine, *[tie(value, token) for value in got])
        parts[1] = parts[2] = part
        return
    (part,) = plane_call(join_parts, place, last, [(count, window, LANES)])
    rest = [part[n] for n in range(count)]
    for n in range(len(toward(planes[0], size))):
        got = [
            between_planes(value, toward(plane, size)[n]) for value, plane in zip(rest, planes)
        ]
        token = yield rest, got
        rest = [total(value, tie(more, token)) for value, more in zip(rest, got)]
    parts.update(zip(planes, rest))


def set_out(flows):
    return move_on(flows, None)


def move_on(flows, token):
    sent, got = [], []
    for flow in flows:
        try:
            out, into = flow.send(token)
        except StopIteration:
            continue
        sent += out
        got += into
    return sent, got


def adam_body(
    place_ref, grad_ref, vector_ref, params_ref, first_ref, second_ref, out_ref, new_first_ref,
    new_second_ref, total,
    *, devices,
):
    core, first_row = place_ref[0], place_ref[1]
    rows = first_ref.shape[0]
    shift = grad_ref.shape[0] - rows
    grads = grad_ref[...].astype(f32)
    total[...] = jnp.where(core == 0, grads[:rows], grads[shift:])
    for at, row in ((0, ROW_G1), (12, ROW_BQ)):
        for n in range(12):
            place = row + n - first_row

            @pl.when((place >= 0) & (place < rows))
            def _():
                total[pl.ds(place, 1), :] += vector_ref[at + n : at + n + 1, :]

    mean = total[...] * (1.0 / devices)
    first = first_decay * first_ref[...] + (1.0 - first_decay) * mean
    second = second_decay * second_ref[...] + (1.0 - second_decay) * mean * mean
    new_first_ref[...] = first
    new_second_ref[...] = second
    fix_one = 1.0 - first_decay**STEP
    fix_two = 1.0 - second_decay**STEP
    update = first / fix_one / (jnp.sqrt(second / fix_two) + adam_epsilon)
    row = first_row + iota((rows, LANES), 0)
    in_matrix = row < 0
    for low, high in (
        (ROW_QKV, ROW_BQ),
        (ROW_WO, ROW_BO),
        (ROW_FC, ROW_BFC),
        (ROW_PR, ROW_BPR),
    ):
        in_matrix = in_matrix | ((row >= low) & (row < high))
    out_ref[...] = params_ref[...] - jnp.where(in_matrix, base_rate / D, base_rate) * update


def adam(place, grads, vectors, params, first, second, devices):
    shape = jax.ShapeDtypeStruct(first.shape, f32)
    return pl.pallas_call(
        partial(adam_body, devices=devices),
        in_specs=[smem] + [vmem] * 5,
        out_specs=[vmem] * 3,
        out_shape=[shape] * 3,
        scratch_shapes=[pltpu.VMEM(first.shape, f32)],
        compiler_params=params_of(8),
        cost_estimate=cost(1e6, 6e6),
    )(place, grads, vectors, params, first, second)


def total_of(result, value):
    dp, seq = lax.axis_size("dp"), lax.axis_size("seq")

    def exchange(value, other_dp, other_seq):
        pairs = [
            (a * seq + b, (a ^ other_dp) * seq + (b ^ other_seq))
            for a in range(dp)
            for b in range(seq)
        ]
        return lax.ppermute(value, ("dp", "seq"), pairs)

    got = [exchange(value, a, b) for a in range(2) for b in range(seq) if a + b > 0]
    token = yield [value], got
    value = sum([tie(more, token) for more in got], value)
    got = [exchange(value, 2 * a, 0) for a in range(1, dp // 2)]
    token = yield [value], got
    result.append(sum([tie(more, token) for more in got], value))


def shards(tokens, cotangent, loss_mask, segments, params, first_moment, second_moment):
    block = tokens.shape[0]
    seq_index = lax.axis_index("seq")
    core = seq_index % 2
    x = seq_index // 2
    shard_rows = first_moment.shape[0]
    total_rows = params.shape[0]
    chip = 2 * block
    device_count = lax.axis_size(("dp", "seq"))

    def unpick(value):
        low, high = value[:BLK], value[BLK:]
        got = swap(jnp.where(core == 0, high, low), "seq", 1)
        return jnp.where(
            core == 0, jnp.concatenate([low, got]), jnp.concatenate([high, got])
        )

    own_x = tokens.reshape(block, D)
    got_x = swap(own_x, "seq", 1)
    far_own = swap(own_x, "seq", 2)
    far_got = swap(far_own, "seq", 1)
    own_dy = cotangent.reshape(block, D) * loss_mask.astype(bf16)
    got_dy = swap(own_dy, "seq", 1)

    w_qkv = unpack_matrix(params, ROW_QKV, D, 3 * D, 4)
    w_out = unpack_matrix(params, ROW_WO, D, D, 2)
    w_up = unpack_matrix(params, ROW_FC, D, FF, 4)
    w_down = unpack_matrix(params, ROW_PR, FF, D, 4)

    norm_rows, bias_rows, *feed_rows = take_rows(
        params, [(ROW_G1, 16), (ROW_BQ, 16), (ROW_BO, 24), (ROW_BFC, 32), (ROW_BPR, 8)]
    )
    seg_row = segments.reshape(1, -1)
    near_rows = [core * BLK, (3 - core) * BLK]
    q_place = [x * chip + row for row in near_rows]
    place = jnp.stack(q_place + [core, x] + near_rows).astype(jnp.int32)
    masks = (place, seg_row, seg_row.astype(f32))

    near_n, near_k, near_kt, near_v, near_vt, queries = project(
        place, own_x, got_x, norm_rows, bias_rows, w_qkv, True
    )
    state = attend(*masks, queries, near_k, near_vt)
    far_n, far_k, far_kt, far_v, far_vt = project(
        place, far_own, far_got, norm_rows, bias_rows, w_qkv, False
    )
    attn, attn_t, log_sum = attend(*masks, queries, far_k, far_vt, state)
    (
        active, d_up, two_n, d_mlp, d_attn, d_resid, d_heads, delta, block_low, vec, d_bias_up
    ) = feed(
        place, attn, attn_t, own_x, got_x, own_dy, got_dy, feed_rows, w_out, w_up, w_down
    )
    up_rows = d_bias_up.reshape(24, LANES)

    core_x = jnp.stack([core, x]).astype(jnp.int32)
    parts = {}

    def grads(*given, **options):
        planes, halves_of, left = weight_grad(core_x, *given, **options)
        flows = [reduce_planes(parts, planes, *halves_of)] if planes else []
        return flows, left

    plane_rows = 8 * shard_rows
    down, left = grads(
        [(active, d_mlp, 0, False)], [up_rows, vec], None, None, ROW_PR, [(0, 0, 22, 2)],
        [(2, 1, 18, 6)], shard_rows, total_rows, [], 15e9,
    )
    _, core_down = set_out(down)
    _, out_rows = grads(
        [(attn, d_attn, 0, False)], [vec], None, None, ROW_WO, [], [(8, 0, 0, 8)], shard_rows,
        down16(ROW_FC), [], 4e9, whole=False,
    )
    up, left = grads(
        [(two_n, d_up, 0, False)], [up_rows, vec], out_rows, left, ROW_FC, [(0, 1, 8, 10)],
        [(10, 0, 0, 22)], shard_rows, -(-down16(ROW_PR) // plane_rows) * plane_rows, [], 10e9,
    )
    sent_up, core_up = set_out(up)
    sent_down, one_down = move_on(down, None)

    given = (*masks, queries, d_heads, log_sum, delta)
    d_near, dq_t = attend_back(
        *given, (near_k, near_kt, near_v), None, core_down + sent_up + sent_down
    )
    sent_up, one_up = move_on(up, dq_t)
    sent_down, two_down = move_on(down, dq_t)
    d_far, dq = attend_back(
        *given, (far_k, far_kt, far_v), dq_t, core_up + one_down + sent_up + sent_down
    )
    sent_up, two_up = move_on(up, d_far)
    qkv, _ = grads(
        [(near_n, dq, 0, False), (near_n, d_near, D, False), (far_n, d_far, D, True)], [], None,
        left, ROW_QKV, [], [], shard_rows, -(-down16(ROW_WO) // plane_rows) * plane_rows,
        one_up + two_down + sent_up, 15e9,
    )
    _, core_qkv = set_out(qkv)
    sent_up, _ = move_on(up, None)
    sent_qkv, _ = move_on(qkv, None)
    far_in, far_vec = input_back(
        place, far_own, far_got, d_far, w_qkv, norm_rows, [], sent_up + sent_qkv
    )
    near_in, near_vec = input_back(
        place, own_x, got_x, d_near, w_qkv, norm_rows, [dq, d_resid], [far_vec]
    )
    sent_down, _ = move_on(down, near_vec)
    sent_qkv, _ = move_on(qkv, near_vec)
    vectors = []
    sums = [total_of(vectors, tie(jnp.concatenate([near_vec + far_vec, vec[18:24]]), sent_qkv))]
    far_in, near_in, block_low, _ = lax.optimization_barrier(
        (far_in, near_in, block_low, sent_qkv)
    )
    set_out(sums)
    sent_qkv, _ = move_on(qkv, None)
    move_on(down, sent_qkv)
    sent_qkv, _ = move_on(qkv, None)
    move_on(sums, sent_qkv)
    while move_on(qkv + up + down + sums, None)[0]:
        pass
    vectors = vectors[0]
    bias_down_grad = vectors[24:].reshape(-1) / device_count
    block_output = unpick(block_low)

    own, other = halves(far_in, 0, core)
    far_sum = own + swap(rounded(other), "seq", 1).astype(f32)
    from_far = swap(rounded(far_sum), "seq", 2).astype(f32)
    own, other = halves(near_in, 0, core)
    input_grad = own + swap(rounded(other), "seq", 1).astype(f32)
    input_grad = rounded(jnp.where(x == 0, input_grad + from_far, input_grad))

    own_plane = lax.axis_index("dp") // 2
    summed = jnp.zeros((core_window(shard_rows), LANES), bf16)
    for plane in sorted(parts, reverse=True):
        summed = jnp.where(own_plane == plane, parts[plane], summed)
    first_row = lax.axis_index(("dp", "seq")) * shard_rows
    own_params = lax.dynamic_slice_in_dim(params, first_row, shard_rows, 0)
    new_params, new_first, new_second = adam(
        jnp.stack([core, first_row]).astype(jnp.int32), summed, vectors, own_params, first_moment,
        second_moment, device_count,
    )
    return (
        block_output.reshape(tokens.shape),
        input_grad.reshape(tokens.shape),
        new_params,
        new_first,
        new_second,
        bias_down_grad,
    )


def solution(mesh):
    return jax.shard_map(
        shards,
        mesh=mesh,
        in_specs=(
            P("seq", "dp", None),
            P("seq", "dp", None),
            P("seq", "dp"),
            P(None, "dp"),
            P(),
            P(("dp", "seq"), None),
            P(("dp", "seq"), None),
        ),
        out_specs=(
            P("seq", "dp", None),
            P("seq", "dp", None),
            P(("dp", "seq"), None),
            P(("dp", "seq"), None),
            P(("dp", "seq"), None),
            P(),
        ),
        check_vma=False,
    )
```

```python
from functools import partial
import math

import jax
import jax.numpy as jnp
from jax import lax
from jax.experimental import pallas as pl
from jax.experimental.pallas import tpu as pltpu
from jax.sharding import PartitionSpec as P

D = 768
HEADS = 12
HEAD_DIM = 64
FF = 3072
STEP = 4
LANES = 128
BLK = 256

norm_epsilon = 1e-05
branch_scale = 48.0 ** (-0.5)
first_decay = 0.9
second_decay = 0.95
adam_epsilon = 1e-08
base_rate = 0.1
masked_score = -1e30
LOG2E = 1.4426950408889634
score_factor = LOG2E / HEAD_DIM

f32 = jnp.float32
bf16 = jnp.bfloat16

ROW_G1, ROW_S1 = 0, 6
ROW_QKV = 12
ROW_BQ = ROW_QKV + D * 3 * D // LANES
ROW_BV = ROW_BQ + 6
ROW_WO = ROW_BV + 6
ROW_BO = ROW_WO + D * D // LANES
ROW_G2, ROW_S2 = ROW_BO + 6, ROW_BO + 12
ROW_FC = ROW_BO + 18
ROW_BFC = ROW_FC + D * FF // LANES
ROW_PR = ROW_BFC + FF // LANES
ROW_BPR = ROW_PR + D * FF // LANES
ROW_END = ROW_BPR + 6

VMEM = 56 * 1024 * 1024


nt_dims = (((1,), (1,)), ((), ()))
nn_dims = (((1,), (0,)), ((), ()))
tn_dims = (((0,), (0,)), ((), ()))

smem = pl.BlockSpec(memory_space=pltpu.SMEM)
vmem = pl.BlockSpec(memory_space=pltpu.VMEM)
anywhere = pl.BlockSpec(memory_space=pl.ANY)


def params_of(mebibytes):
    return pltpu.CompilerParams(vmem_limit_bytes=mebibytes << 20)


def cost(flops, moved):
    return pl.CostEstimate(flops=int(flops), bytes_accessed=int(moved), transcendentals=0)


def few_rows(count):
    return pl.BlockSpec((count, LANES), lambda *_: (0, 0))


def row_of(ref, start, rows=6):
    return jnp.concatenate([ref[start + j : start + j + 1, :] for j in range(rows)], axis=1)


def column_of(row):
    return jnp.broadcast_to(row, (8, row.shape[1])).T[:, :1]


def dot(a, b, dims=nn_dims):
    return lax.dot_general(a, b, dims, preferred_element_type=f32)


def iota(shape, axis):
    return lax.broadcasted_iota(jnp.int32, shape, axis)


def kernel_call(body, operands, in_specs, after=(), **options):
    count = len(operands)

    def without(*refs):
        body(*refs[:count], *refs[count + len(after) :])

    return pl.pallas_call(without, in_specs=in_specs + [anywhere] * len(after), **options)(
        *operands, *after
    )


def down16(row):
    return row // 16 * 16


def group_rows(blocks):
    return 8 if blocks > 8 else 32


def side_by_side(value, other):
    return jnp.concatenate([value, other], axis=1)


def unpack_body(x_ref, o_ref, move, *, shift, rows, blocks, pairs):
    size = rows * blocks
    bits = rows.bit_length() - 1

    @pl.when(pl.program_id(0) == 0)
    def _():
        to, come = iota(move.shape, 0), iota(move.shape, 1)
        move[...] = (come == shift + (to & (rows - 1)) * blocks + (to >> bits)).astype(bf16)

    for n in range(pairs):
        both = side_by_side(
            *[x_ref[pl.ds((2 * n + side) * size, size + 16), :].astype(bf16) for side in (0, 1)]
        )
        moved = dot(move[...], both)
        for j in range(blocks):
            part = moved[j * rows : (j + 1) * rows]
            part = jnp.concatenate([part[:, :LANES], part[:, LANES:]], axis=0).astype(bf16)
            o_ref[2 * n * rows : 2 * (n + 1) * rows, j * LANES : (j + 1) * LANES] = part


def take_body(*refs):
    count = len(refs) // 2
    for x_ref, o_ref in zip(refs[:count], refs[count:]):
        o_ref[...] = x_ref[...]


def take_rows(params, runs):
    runs = [(first // 8 * 8, count) for first, count in runs]

    def window(first, count):
        return pl.BlockSpec((pl.Element(count), pl.Element(LANES)), lambda i: (first, 0))

    return pl.pallas_call(
        take_body,
        grid=(1,),
        in_specs=[window(first, count) for first, count in runs],
        out_specs=[pl.BlockSpec((count, LANES), lambda i: (0, 0)) for _, count in runs],
        out_shape=[jax.ShapeDtypeStruct((count, LANES), f32) for _, count in runs],
        compiler_params=params_of(48),
    )(*[params] * len(runs))


def unpack_matrix(params, row, matrix_rows, columns, steps):
    blocks = columns // LANES
    rows = group_rows(blocks)
    base = row // 8 * 8
    chunk = matrix_rows // steps
    size = chunk * blocks
    return pl.pallas_call(
        partial(
            unpack_body, shift=row - base, rows=rows, blocks=blocks, pairs=chunk // rows // 2
        ),
        grid=(steps,),
        in_specs=[
            pl.BlockSpec(
                (pl.Element(size + 16), pl.Element(LANES)),
                lambda i: (pl.multiple_of(base + i * size, 8), 0),
            )
        ],
        out_specs=pl.BlockSpec((chunk, columns), lambda i: (i, 0)),
        out_shape=jax.ShapeDtypeStruct((matrix_rows, columns), bf16),
        scratch_shapes=[pltpu.VMEM((rows * blocks, rows * blocks + 16), bf16)],
        compiler_params=params_of(38),
        cost_estimate=cost(8e9, 6 * matrix_rows * columns),
    )(params)


def grad_body(
    core_ref,
    *refs,
    products,
    vectors,
    below,
    rest,
    base,
    row,
    matrix_rows,
    columns,
    head,
    tail,
    planes,
    plane_rows,
    keep,
):
    refs = list(refs)
    factors = [refs.pop(0) for _ in range(2 * len(products))]
    vector_refs = [refs.pop(0) for _ in range(vectors)]
    below_ref = refs.pop(0) if below else None
    rest_ref = refs.pop(0) if rest else None
    own_ref, other_ref = (refs.pop(0), refs.pop(0)) if planes else (None, None)
    keep_ref = refs.pop(0) if keep else None
    window, grad, move, carry, last = refs
    blocks = columns // LANES
    rows = group_rows(blocks)
    bits = rows.bit_length() - 1
    size = rows * blocks
    shift = row - base
    body_rows = matrix_rows * blocks
    tail_rows = last.shape[0]
    if below:
        window[pl.ds(0, below), :] = below_ref[...]
    if rest:
        window[pl.ds(below + body_rows + tail_rows, rest), :] = rest_ref[...]
    to, come = iota(move.shape, 0), iota(move.shape, 1)
    move[...] = (to == shift + (come & (rows - 1)) * blocks + (come >> bits)).astype(bf16)
    carry[...] = jnp.zeros_like(carry)
    last[...] = jnp.zeros_like(last)
    for place, n, start, count in head:
        carry[place : place + count, :] = vector_refs[n][start : start + count, :]
    for place, n, start, count in tail:
        last[place : place + count, :] = vector_refs[n][start : start + count, :]

    core = core_ref[0]
    wide_rows = grad.shape[0]

    def multiply(c, state):
        lanes = pl.ds(pl.multiple_of(c * wide_rows, wide_rows), wide_rows)
        for n, (at, far) in enumerate(products):
            a_ref, b_ref = factors[2 * n], factors[2 * n + 1]
            span = slice(at, at + b_ref.shape[1])
            if far:

                @pl.when(core_ref[1] == 1)
                def _():
                    grad[:, span] += dot(a_ref[:, lanes], b_ref[...], tn_dims)

            else:
                grad[:, span] = dot(a_ref[:, lanes], b_ref[...], tn_dims)

        left = carry[...]
        for pair in range(wide_rows // rows // 2):
            both = side_by_side(
                *[
                    jnp.concatenate(
                        [
                            grad[at : at + rows, j * LANES : (j + 1) * LANES]
                            for j in range(blocks)
                        ],
                        axis=0,
                    ).astype(bf16)
                    for at in (2 * pair * rows, (2 * pair + 1) * rows)
                ]
            )
            moved = dot(move[...], both)
            for side in (0, 1):
                part = moved[:, side * LANES : (side + 1) * LANES]
                at = (c * (wide_rows // rows) + 2 * pair + side) * size + below
                at = pl.multiple_of(at, 16)
                window[pl.ds(at, 16), :] = (part[:16] + left).astype(bf16)
                window[pl.ds(at + 16, size - 16), :] = part[16:size].astype(bf16)
                left = part[size:]
        carry[...] = left
        return state

    lax.fori_loop(0, matrix_rows // wide_rows, multiply, 0)
    last[pl.ds(0, 16), :] = last[pl.ds(0, 16), :] + carry[...]
    window[pl.ds(below + body_rows, tail_rows), :] = last[...].astype(bf16)
    half = plane_rows // 4
    for n, plane in enumerate(planes):
        part_rows = own_ref.shape[1]
        for block in range(4):
            for ref, which in ((own_ref, core), (other_ref, 1 - core)):
                at = plane * plane_rows - (base - below) + block * half
                at = pl.multiple_of(at + which * (half - part_rows), 16)
                ref[4 * n + block] = window[pl.ds(at, part_rows), :]
    if keep:
        keep_ref[...] = window[pl.ds(0, keep), :]


def weight_grad(
    place, products, vectors, below, rest, row, head, tail, shard_rows, top, after, work,
    whole=True,
):
    base = down16(row)
    matrix_rows = products[0][0].shape[1]
    columns = max(at + b.shape[1] for _, b, at, _ in products)
    blocks = columns // LANES
    rows = group_rows(blocks)
    size = rows * blocks
    plane_rows = 8 * shard_rows
    below_rows = 0 if below is None else below.shape[0]
    rest_rows = 0 if rest is None else rest.shape[0]
    first_row = base - below_rows
    tail_rows = top - rest_rows - base - matrix_rows * blocks
    first_plane = -(-first_row // plane_rows)
    planes = list(range(first_plane, top // plane_rows)) if whole else []
    keep = first_plane * plane_rows - first_row if whole else top - first_row
    part = jax.ShapeDtypeStruct((4 * len(planes), core_window(shard_rows), LANES), bf16)
    out_shape = [part, part] if planes else []
    if keep:
        out_shape.append(jax.ShapeDtypeStruct((keep, LANES), bf16))
    operands = [value for pair in products for value in pair[:2]] + list(vectors)
    operands += [value for value in (below, rest) if value is not None]
    outs = kernel_call(
        partial(
            grad_body,
            products=[pair[2:] for pair in products],
            vectors=len(vectors),
            below=below_rows,
            rest=rest_rows,
            base=base,
            row=row,
            matrix_rows=matrix_rows,
            columns=columns,
            head=head,
            tail=tail,
            planes=planes,
            plane_rows=plane_rows,
            keep=keep,
        ),
        [place] + operands,
        [smem] + [vmem] * len(operands),
        after,
        out_specs=[vmem] * len(out_shape),
        out_shape=out_shape,
        scratch_shapes=[
            pltpu.VMEM((top - first_row, LANES), bf16),
            pltpu.VMEM((256 if columns < 3 * D or columns == FF else 128, columns), f32),
            pltpu.VMEM((size + 16, size), bf16),
            pltpu.VMEM((16, LANES), f32),
            pltpu.VMEM((tail_rows, LANES), f32),
        ],
        compiler_params=params_of(16),
        cost_estimate=cost(work, 4 * matrix_rows * columns),
    )
    return planes, tuple(outs[:2]) if planes else None, outs[-1] if keep else None


def row_mean(value):
    return jnp.sum(value, axis=-1, keepdims=True) * (1.0 / value.shape[-1])


def norm_parts(values):
    center = values - row_mean(values)
    rstd = lax.rsqrt(row_mean(center * center) + norm_epsilon)
    return center * rstd, rstd


def norm_back(unit, rstd, gain, grad):
    scaled = grad * gain
    return rstd * (scaled - row_mean(scaled) - unit * row_mean(scaled * unit))


def project_body(place_ref, own_ref, got_ref, norm_ref, bias_ref, w_ref, *outs, with_query):
    n_ref, k_ref, kt_ref, v_ref, vt_ref = outs[:5]
    mine = pl.program_id(0) // 2 == place_ref[2]
    x = jnp.where(mine, own_ref[...], got_ref[...])
    unit, _ = norm_parts(x.astype(f32))
    normed = (unit * row_of(norm_ref, 0) + row_of(norm_ref, 6)).astype(bf16)
    n_ref[...] = normed
    keys = dot(normed, w_ref[:, D : 2 * D]).astype(bf16)
    k_ref[...] = keys
    kt_ref[...] = keys.T
    bias = ROW_BQ % 8
    values = (dot(normed, w_ref[:, 2 * D :]) + row_of(bias_ref, bias + 6)).astype(bf16)
    v_ref[...] = values
    vt_ref[...] = values.T
    if with_query:
        outs[5][...] = (dot(normed, w_ref[:, :D]) + row_of(bias_ref, bias)).astype(bf16)


def project(place, own, got, norm_rows, bias_rows, w_qkv, with_query, after):
    count = 2 * own.shape[0]
    half = own.shape[0] // BLK
    by_rows = pl.BlockSpec((BLK, D), lambda i: (i, 0))
    by_halves = pl.BlockSpec((BLK, D), lambda i: (i % half, 0))
    by_columns = pl.BlockSpec((D, BLK), lambda i: (0, i))
    tall = jax.ShapeDtypeStruct((count, D), bf16)
    wide = jax.ShapeDtypeStruct((D, count), bf16)
    return kernel_call(
        partial(project_body, with_query=with_query),
        [place, own, got, norm_rows, bias_rows, w_qkv],
        [
            smem,
            by_halves,
            by_halves,
            few_rows(16),
            few_rows(16),
            pl.BlockSpec((D, 3 * D), lambda i: (0, 0)),
        ],
        after,
        grid=(count // BLK,),
        out_specs=[by_rows, by_rows, by_columns, by_rows, by_columns]
        + [by_rows] * with_query,
        out_shape=[tall, tall, wide, tall, wide] + [tall] * with_query,
        compiler_params=params_of(12),
        cost_estimate=cost(2 * count * D * (2 + with_query) * D, 12 * count * D),
    )


def head_lanes(value, odd):
    lane = iota(value.shape, 1)
    keep = (lane >= HEAD_DIM) if odd else (lane < HEAD_DIM)
    return jnp.where(keep, value, jnp.zeros_like(value))


def visit_block(place_ref, seg_ref, segs_ref, bias_ref, i, k_start, valid, step):
    q_start = place_ref[i]
    q_first = seg_ref[0, q_start]
    q_last = seg_ref[0, q_start + BLK - 1]
    k_first = seg_ref[0, k_start]
    k_last = seg_ref[0, k_start + BLK - 1]
    active = valid & (k_start <= q_start) & (k_last >= q_first)
    plain = (k_first == q_last) & (k_start + BLK <= q_start)

    @pl.when(active & plain)
    def _():
        step(False)

    @pl.when(active & jnp.logical_not(plain))
    def _():
        k_pos = k_start + iota((BLK, BLK), 0)
        q_pos = q_start + iota((BLK, BLK), 1)
        segk = column_of(segs_ref[:, pl.ds(pl.multiple_of(k_start, BLK), BLK)])
        same = segk == segs_ref[:, pl.ds(pl.multiple_of(q_start, BLK), BLK)]
        bias_ref[...] = jnp.where((k_pos <= q_pos) & same, 0.0, masked_score)
        step(True)


ACC = HEAD_DIM + 16


def attend_body(
    place_ref, seg_ref, segs_ref, q_ref, k_ref, vt_ref, *refs, first
):
    if first:
        acc_ref, top_ref, bias_ref, s_ref = refs
        acc_ref[...] = jnp.zeros_like(acc_ref)
        top_ref[...] = jnp.full_like(top_ref, masked_score)
    else:
        acc_in, top_in, out_ref, outt_ref, total_ref, bias_ref, s_ref, acc_ref, top_ref = refs
        acc_ref[...] = acc_in[...]
        top_ref[...] = top_in[...]
    ones = jnp.ones((16, BLK), bf16)
    count = k_ref.shape[0] // BLK
    x = place_ref[3]
    base = x * (count * BLK) if first else 0 * x
    valid = (x >= 0) if first else (x == 1)
    for i in range(2):
        cols = slice(i * BLK, (i + 1) * BLK)

        def visit(n, carry):
            kb = count - 1 - n
            k_rows = pl.ds(pl.multiple_of(kb * BLK, BLK), BLK)
            q_rows = pl.ds(pl.multiple_of(place_ref[4 + i], BLK), BLK)

            def step(masked):
                tops = []
                for h in range(HEADS):
                    pair, odd = h // 2, h % 2
                    lanes = slice(pair * LANES, (pair + 1) * LANES)
                    s = dot(k_ref[k_rows, lanes], head_lanes(q_ref[q_rows, lanes], odd), nt_dims)
                    s = s * score_factor
                    if masked:
                        s = s + bias_ref[...]
                    s_ref[h] = s
                    tops.append(jnp.max(s, axis=0, keepdims=True))
                old = top_ref[:HEADS, cols]
                new = jnp.maximum(old, jnp.concatenate(tops, axis=0))
                top_ref[:HEADS, cols] = new
                scale = jnp.exp2(old - new)
                for h in range(HEADS):
                    p = jnp.exp2(s_ref[h] - new[h : h + 1]).astype(bf16)
                    v_part = jnp.concatenate(
                        [vt_ref[h * HEAD_DIM : (h + 1) * HEAD_DIM, k_rows], ones], axis=0
                    )
                    acc_ref[h, :, cols] = acc_ref[h, :, cols] * scale[h : h + 1] + dot(v_part, p)

            visit_block(
                place_ref, seg_ref, segs_ref, bias_ref, i, base + kb * BLK, valid, step
            )
            return carry

        lax.fori_loop(0, count, visit, 0)
    if not first:
        for h in range(HEADS):
            total = acc_ref[h, HEAD_DIM : HEAD_DIM + 1, :]
            outt_ref[h * HEAD_DIM : (h + 1) * HEAD_DIM, :] = acc_ref[h, :HEAD_DIM, :] / total
            total_ref[h : h + 1, :] = top_ref[h : h + 1, :] + jnp.log2(total)
        for i in range(2):
            cols = slice(i * BLK, (i + 1) * BLK)
            out_ref[cols, :] = outt_ref[:, cols].T.astype(bf16)


def attend(place, seg, segs, q, k, vt, state, after):
    count = 2 * BLK
    first = state is None
    acc_shape = jax.ShapeDtypeStruct((HEADS, ACC, count), f32)
    row_shape = jax.ShapeDtypeStruct((16, count), f32)
    if first:
        outs = (acc_shape, row_shape)
    else:
        outs = (
            jax.ShapeDtypeStruct((count, D), bf16),
            jax.ShapeDtypeStruct((D, count), f32),
            row_shape,
        )
    extra = () if first else state
    held = [] if first else [pltpu.VMEM((HEADS, ACC, count), f32), pltpu.VMEM((16, count), f32)]
    return kernel_call(
        partial(attend_body, first=first),
        [place, seg, segs, q, k, vt, *extra],
        [smem, smem] + [vmem] * (4 + len(extra)),
        after,
        out_specs=(vmem,) * len(outs),
        out_shape=outs,
        scratch_shapes=[pltpu.VMEM((BLK, BLK), f32), pltpu.VMEM((HEADS, BLK, BLK), f32)] + held,
        compiler_params=params_of(14),
        cost_estimate=cost(15e9, 8e6),
    )


def two_heads(value):
    return jnp.concatenate([head_lanes(value, 0), head_lanes(value, 1)], axis=0)


def attend_back_body(
    place_ref, seg_ref, segs_ref, q_ref, do_ref, total_ref, delta_ref, k_ref, kt_ref,
    v_ref, *refs, near
):
    if near:
        out_ref, dqt_ref, bias_ref, dk_acc, dv_acc, q_two, do_two, s_ref, da_ref = refs
        dqt_ref[...] = jnp.zeros_like(dqt_ref)
    else:
        dqt_in, out_ref, dq_ref, bias_ref, dk_acc, dv_acc, q_two, do_two, s_ref, da_ref, dqt_ref = (
            refs
        )
        dqt_ref[...] = dqt_in[...]
        dq_ref[...] = jnp.zeros_like(dq_ref)
    count = k_ref.shape[0] // BLK
    x = place_ref[3]
    base = x * (count * BLK) if near else 0 * x
    valid = (x >= 0) if near else (x == 1)
    pairs = HEADS // 2

    @pl.when(valid)
    def _():
        for i in range(2):
            q_rows = pl.ds(pl.multiple_of(place_ref[4 + i], BLK), BLK)
            for pair in range(pairs):
                lanes = slice(pair * LANES, (pair + 1) * LANES)
                q_two[i, pair] = two_heads(q_ref[q_rows, lanes])
                do_two[i, pair] = two_heads(do_ref[i * BLK : (i + 1) * BLK, lanes])

    def visit(kb, carry):
        k_rows = pl.ds(pl.multiple_of(kb * BLK, BLK), BLK)
        dk_acc[...] = jnp.zeros_like(dk_acc)
        dv_acc[...] = jnp.zeros_like(dv_acc)
        for i in range(2):
            cols = slice(i * BLK, (i + 1) * BLK)

            def step(masked):
                def row_two(ref, pair):
                    return jnp.concatenate(
                        [ref[2 * pair : 2 * pair + 1, cols], ref[2 * pair + 1 : 2 * pair + 2, cols]],
                        axis=1,
                    )

                def scores(pair):
                    lanes = slice(pair * LANES, (pair + 1) * LANES)
                    s_ref[pair % 2] = dot(k_ref[k_rows, lanes], q_two[i, pair], nt_dims)
                    da_ref[pair % 2] = dot(v_ref[k_rows, lanes], do_two[i, pair], nt_dims)

                scores(0)
                for pair in range(pairs):
                    if pair + 1 < pairs:
                        scores(pair + 1)
                    lanes = slice(pair * LANES, (pair + 1) * LANES)
                    s = s_ref[pair % 2] * score_factor
                    if masked:
                        s = s + jnp.concatenate([bias_ref[...], bias_ref[...]], axis=1)
                    p = jnp.exp2(s - row_two(total_ref, pair))
                    ds = (p * (da_ref[pair % 2] - row_two(delta_ref, pair))).astype(bf16)
                    dv_acc[:, lanes] += dot(p.astype(bf16), do_two[i, pair])
                    dk_acc[:, lanes] += dot(ds, q_two[i, pair])
                    for odd in range(2):
                        h = 2 * pair + odd
                        head = slice(h * HEAD_DIM, (h + 1) * HEAD_DIM)
                        dqt_ref[head, cols] += dot(
                            kt_ref[head, k_rows], ds[:, odd * BLK : (odd + 1) * BLK]
                        )

            visit_block(
                place_ref, seg_ref, segs_ref, bias_ref, i, base + kb * BLK, valid, step
            )
        out_ref[k_rows, :D] = (dk_acc[...] * (1.0 / HEAD_DIM)).astype(bf16)
        out_ref[k_rows, D:] = dv_acc[...].astype(bf16)
        return carry

    lax.fori_loop(0, count, visit, 0)
    if not near:
        for i in range(2):
            q_rows = pl.ds(pl.multiple_of(place_ref[4 + i], BLK), BLK)
            part = dqt_ref[:, i * BLK : (i + 1) * BLK] * (1.0 / HEAD_DIM)
            dq_ref[q_rows, :] = part.T.astype(bf16)


def attend_back(place, seg, segs, q, do, total, delta, keys, dqt, after):
    near = dqt is None
    rows = q.shape[0]
    two = pltpu.VMEM((2, HEADS // 2, 2 * BLK, LANES), bf16)
    wide = pltpu.VMEM((2, BLK, 2 * BLK), f32)
    sums_of = pltpu.VMEM((BLK, D), f32)
    blocks = [pltpu.VMEM((BLK, BLK), f32), sums_of, sums_of, two, two, wide, wide]
    sums = jax.ShapeDtypeStruct((D, 2 * BLK), f32)
    operands = [place, seg, segs, q, do, total, delta, *keys] + ([] if near else [dqt])
    return kernel_call(
        partial(attend_back_body, near=near),
        operands,
        [smem, smem] + [vmem] * (len(operands) - 2),
        after,
        out_specs=[vmem] * 2,
        out_shape=[
            jax.ShapeDtypeStruct((rows, 2 * D), bf16),
            sums if near else jax.ShapeDtypeStruct((rows, D), bf16),
        ],
        scratch_shapes=blocks + ([] if near else [pltpu.VMEM((D, 2 * BLK), f32)]),
        compiler_params=params_of(16),
        cost_estimate=cost(30e9, 1e7),
    )


GELU_A = math.sqrt(2.0 / math.pi)
GELU_B = 0.044715
FF_BLK = 512
FF_PART = 256


def put_rows(ref, at, value):
    for j in range(value.shape[1] // LANES):
        ref[at + j : at + j + 1, :] = value[:, j * LANES : (j + 1) * LANES]


def column_sum(value):
    return jnp.sum(value, axis=0, keepdims=True)


def feed_body(
    place_ref, attn_ref, outt_ref, xo_ref, xg_ref, dyo_ref, dyg_ref, wo_ref, two_vec, wu_ref,
    bu_ref, wd_ref, bd_ref,
    act_ref, dup_ref, two_ref, dmlp_ref, dattn_ref, dresid_ref, dheads_ref, delta_ref, block_ref,
    vec_ref, dbu_ref,
    r1, unit, rstd, ym, dtwo,
):
    step = pl.program_id(0)
    core = place_ref[2]

    def picked(own_ref, got_ref, i):
        return jnp.where(core == i, own_ref[:BLK, :], got_ref[BLK:, :])

    @pl.when(step == 0)
    def _():
        for i in range(2):
            rows = slice(i * BLK, (i + 1) * BLK)
            ya = dot(attn_ref[rows, :], wo_ref[...]) + row_of(two_vec, 0)
            resid = picked(xo_ref, xg_ref, i).astype(f32) + branch_scale * ya
            r1[rows, :] = resid
            one, inverse = norm_parts(resid)
            unit[rows, :] = one
            rstd[rows, :] = inverse
            two_ref[rows, :] = (one * row_of(two_vec, 6) + row_of(two_vec, 12)).astype(bf16)
            dy = picked(dyo_ref, dyg_ref, i).astype(f32)
            dmlp_ref[rows, :] = (branch_scale * dy).astype(bf16)
        ym[...] = jnp.zeros_like(ym)
        dtwo[...] = jnp.zeros_like(dtwo)

    two, dmlp = two_ref[...], dmlp_ref[...]
    parts = [slice(n, n + FF_PART) for n in range(0, FF_BLK, FF_PART)]

    lane_rows = FF_BLK // LANES
    bias = bu_ref[pl.ds(ROW_BFC % 8 + step * lane_rows, lane_rows), :]
    bias = jnp.concatenate([bias[j : j + 1, :] for j in range(lane_rows)], axis=1)

    def ahead(part):
        return dot(two, wu_ref[:, part]) + bias[:, part], dot(dmlp, wd_ref[part, :], nt_dims)

    ready = ahead(parts[0])
    for n, part in enumerate(parts):
        u, dact = ready
        if n + 1 < len(parts):
            ready = ahead(parts[n + 1])
        square = u * u
        t = jnp.tanh(u * (GELU_A + (GELU_A * GELU_B) * square))
        half = 0.5 + 0.5 * t
        act = (u * half).astype(bf16)
        act_ref[:, part] = act
        slope = half + u * (half * (1.0 - t)) * (GELU_A + (3.0 * GELU_A * GELU_B) * square)
        dup = dact * slope
        dup_low = dup.astype(bf16)
        dup_ref[:, part] = dup_low
        put_rows(dbu_ref, part.start // LANES, column_sum(dup_low.astype(f32)))
    ym[...] += dot(act_ref[...], wd_ref[...])
    dtwo[...] += dot(dup_ref[...], wu_ref[...], nt_dims)

    @pl.when(step == pl.num_programs(0) - 1)
    def _():
        dg = jnp.zeros((1, D), f32)
        ds = jnp.zeros((1, D), f32)
        db = jnp.zeros((1, D), f32)
        dbd = jnp.zeros((1, D), f32)
        for i in range(2):
            rows = slice(i * BLK, (i + 1) * BLK)
            down = ym[rows, :] + row_of(bd_ref, ROW_BPR % 8)
            block_ref[rows, :] = (r1[rows, :] + branch_scale * down).astype(bf16)
            grad = dtwo[rows, :]
            one = unit[rows, :]
            dy = picked(dyo_ref, dyg_ref, i).astype(f32)
            dresid = dy + norm_back(one, rstd[rows, :], row_of(two_vec, 6), grad)
            dresid_ref[rows, :] = dresid
            dattn = (branch_scale * dresid).astype(bf16)
            dattn_ref[rows, :] = dattn
            dg = dg + column_sum(grad * one)
            ds = ds + column_sum(grad)
            db = db + column_sum(dattn.astype(f32))
            dbd = dbd + column_sum(dmlp_ref[rows, :].astype(f32))
            dheads_ref[rows, :] = dot(dattn, wo_ref[...], nt_dims).astype(bf16)
            back = dot(wo_ref[...], dattn, nt_dims).astype(bf16).astype(f32)
            both = back * outt_ref[:, rows]
            for h in range(HEADS):
                delta_ref[h : h + 1, rows] = column_sum(both[h * HEAD_DIM : (h + 1) * HEAD_DIM])
        vec_ref[...] = jnp.zeros_like(vec_ref)
        put_rows(vec_ref, 0, db)
        put_rows(vec_ref, 6, dg)
        put_rows(vec_ref, 12, ds)
        put_rows(vec_ref, 18, dbd)


def feed(place, attn, attn_t, x_own, x_got, dy_own, dy_got, rows, w_out, w_up, w_down):
    count = attn.shape[0]

    def whole(*shape):
        return pl.BlockSpec(shape, lambda k: (0,) * len(shape))

    wide = pl.BlockSpec((count, FF_BLK), lambda k: (0, k))
    tall = whole(count, D)
    steps = FF // FF_BLK
    lane_rows = FF_BLK // LANES
    shapes = [
        ((count, FF), bf16, wide),
        ((count, FF), bf16, wide),
        ((count, D), bf16, tall),
        ((count, D), bf16, tall),
        ((count, D), bf16, tall),
        ((count, D), f32, tall),
        ((count, D), bf16, tall),
        ((16, count), f32, whole(16, count)),
        ((count, D), bf16, tall),
        ((24, LANES), f32, whole(24, LANES)),
        (
            (steps, lane_rows, LANES),
            f32,
            pl.BlockSpec((pl.Squeezed(), lane_rows, LANES), lambda k: (k, 0, 0)),
        ),
    ]
    return pl.pallas_call(
        feed_body,
        grid=(steps,),
        in_specs=[
            smem,
            tall,
            whole(D, count),
            tall,
            tall,
            tall,
            tall,
            whole(D, D),
            few_rows(24),
            pl.BlockSpec((D, FF_BLK), lambda k: (0, k)),
            few_rows(32),
            pl.BlockSpec((FF_BLK, D), lambda k: (k, 0)),
            few_rows(8),
        ],
        out_specs=[spec for _, _, spec in shapes],
        out_shape=[jax.ShapeDtypeStruct(shape, kind) for shape, kind, _ in shapes],
        scratch_shapes=[
            pltpu.VMEM((count, D), f32),
            pltpu.VMEM((count, D), f32),
            pltpu.VMEM((count, 1), f32),
            pltpu.VMEM((count, D), f32),
            pltpu.VMEM((count, D), f32),
        ],
        compiler_params=params_of(20),
        cost_estimate=cost(40e9, 2e7),
    )(
        place, attn, attn_t, x_own, x_got, dy_own, dy_got, w_out, rows[0], w_up, rows[1], w_down,
        rows[2],
    )


def input_body(
    place_ref, fo_ref, fg_ref, no_ref, ng_ref, dfar_ref, dnear_ref, dq_ref, dresid_ref, w_ref,
    gain_ref, far_ref, near_ref, vec_ref, dg, ds, dbq, dbv,
):
    step = pl.program_id(0)
    count = pl.num_programs(0) // 2
    gain = row_of(gain_ref, 0)

    @pl.when(step == 0)
    def _():
        for ref in (dg, ds, dbq, dbv):
            ref[...] = jnp.zeros_like(ref)

    def back(own_ref, got_ref, dkv_ref, at, more):
        mine = at // 2 == place_ref[2]
        x = jnp.where(mine, own_ref[...], got_ref[...])
        unit, rstd = norm_parts(x.astype(f32))
        grad = dot(dkv_ref[...], w_ref[:, D:], nt_dims)
        if more:
            grad = grad + dot(dq_ref[...], w_ref[:, :D], nt_dims)
            dbq[...] += column_sum(dq_ref[...].astype(f32))
        dg[...] += column_sum(grad * unit)
        ds[...] += column_sum(grad)
        dbv[...] += column_sum(dkv_ref[:, D:].astype(f32))
        return norm_back(unit, rstd, gain, grad)

    @pl.when(step < count)
    def _():
        far_ref[...] = back(fo_ref, fg_ref, dfar_ref, step, False)

    @pl.when(step >= count)
    def _():
        at = step - count
        near_ref[...] = back(no_ref, ng_ref, dnear_ref, at, True)
        for i in range(2):

            @pl.when(at * BLK == place_ref[4 + i])
            def _():
                near_ref[...] += dresid_ref[i * BLK : (i + 1) * BLK, :]

    @pl.when(step == pl.num_programs(0) - 1)
    def _():
        put_rows(vec_ref, 0, dg[...])
        put_rows(vec_ref, 6, ds[...])
        put_rows(vec_ref, 12, dbq[...])
        put_rows(vec_ref, 18, dbv[...])


def input_back(place, far, near, d_far, d_near, dq, dresid, w_qkv, norm_rows, after):
    count = d_far.shape[0]
    steps = count // BLK

    def rows(width, index):
        return pl.BlockSpec((BLK, width), lambda i: (index(i), 0))

    def early(i):
        return jnp.minimum(i, steps - 1)

    def late(i):
        return jnp.maximum(i - steps, 0)

    return kernel_call(
        input_body,
        [place, *far, *near, d_far, d_near, dq, dresid, w_qkv, norm_rows],
        [
            smem,
            rows(D, lambda i: early(i) % 2),
            rows(D, lambda i: early(i) % 2),
            rows(D, lambda i: late(i) % 2),
            rows(D, lambda i: late(i) % 2),
            rows(2 * D, early),
            rows(2 * D, late),
            rows(D, late),
            pl.BlockSpec((2 * BLK, D), lambda i: (0, 0)),
            pl.BlockSpec((D, 3 * D), lambda i: (0, 0)),
            few_rows(16),
        ],
        after,
        grid=(2 * steps,),
        out_specs=[rows(D, early), rows(D, late), few_rows(24)],
        out_shape=[
            jax.ShapeDtypeStruct((count, D), f32),
            jax.ShapeDtypeStruct((count, D), f32),
            jax.ShapeDtypeStruct((24, LANES), f32),
        ],
        scratch_shapes=[pltpu.VMEM((1, D), f32)] * 4,
        compiler_params=params_of(12),
        cost_estimate=cost(15e9, 1e6),
    )


def rounded(value):
    return lax.reduce_precision(value, 8, 7).astype(bf16)


def bit_pairs(size, bit, sender=lambda place: True):
    return [(n, n ^ bit) for n in range(size) if sender(n)]


def swap(value, axis, bit):
    return lax.ppermute(value, axis, bit_pairs(lax.axis_size(axis), bit))


def halves(value, axis, which):
    size = value.shape[axis] // 2
    own = lax.dynamic_slice_in_dim(value, which * size, size, axis)
    other = lax.dynamic_slice_in_dim(value, (1 - which) * size, size, axis)
    return own, other


def total(*values):
    return rounded(sum(value.astype(f32) for value in values))


def core_window(shard_rows):
    return (shard_rows + 15) // 16 * 16


def toward(plane, size):
    if size == 4:
        return [
            [[(1, 0), (3, 2)], [(2, 0)]],
            [[(0, 1), (3, 2)], [(2, 1)]],
            [[(0, 1), (3, 2)], [(1, 2)]],
            [[(0, 1), (2, 3)], [(1, 3)]],
        ][plane]
    steps = []
    bit = 1
    while bit < size:
        away = [z for z in range(size) if (z ^ plane) & bit and not (z ^ plane) & (bit - 1)]
        steps.append([(z, z ^ bit) for z in away])
        bit *= 2
    return steps


def tie(value, token):
    return value if token is None else lax.optimization_barrier((value, token))[0]


def between_planes(value, step):
    pairs = [(2 * a + side, 2 * b + side) for a, b in step for side in (0, 1)]
    return lax.ppermute(value, "dp", pairs)


def plane_call(body, place, operands, shapes, after=()):
    operands = [place] + operands
    shapes = [jax.ShapeDtypeStruct(shape, bf16) for shape in shapes]
    return kernel_call(
        body,
        operands,
        [smem] + [vmem] * (len(operands) - 1),
        after,
        out_specs=[vmem] * len(shapes),
        out_shape=shapes,
        compiler_params=params_of(24),
        cost_estimate=cost(1e9, 1e6),
    )


def plus(a, b):
    return (a.astype(f32) + b.astype(f32)).astype(bf16)


def split_first(place_ref, own_ref, got_ref, one_ref, sent_one_ref, two_ref, sent_two_ref):
    x, y = place_ref[0], place_ref[1]
    cut = one_ref.shape[2]
    for n in range(one_ref.shape[0]):
        for side in (0, 1):
            for out, block in (
                (one_ref, 2 * side + x),
                (sent_one_ref, 2 * side + 1 - x),
            ):
                block = 4 * n + block
                out[n, side] = plus(own_ref[block, :cut, :], got_ref[block, :cut, :])
            for out, block in (
                (two_ref, 2 * y + side),
                (sent_two_ref, 2 * (1 - y) + side),
            ):
                block = 4 * n + block
                out[n, side] = plus(own_ref[block, cut:, :], got_ref[block, cut:, :])


def split_second(
    place_ref, one_ref, got_one_ref, two_ref, got_two_ref,
    one_out, sent_one_ref, two_out, sent_two_ref,
):
    x, y = place_ref[0], place_ref[1]
    for n in range(one_out.shape[0]):
        for out, left, right, at in (
            (one_out, one_ref, got_one_ref, y),
            (sent_one_ref, one_ref, got_one_ref, 1 - y),
            (two_out, two_ref, got_two_ref, x),
            (sent_two_ref, two_ref, got_two_ref, 1 - x),
        ):
            out[n] = plus(left[n, at], right[n, at])


def join_parts(place_ref, one_ref, got_one_ref, two_ref, got_two_ref, *outs):
    cut = one_ref.shape[1]
    swapped = place_ref[2] >= 2
    for n in range(one_ref.shape[0]):
        upper = plus(one_ref[n], got_one_ref[n])
        lower = plus(two_ref[n], got_two_ref[n])
        if len(outs) == 1:
            outs[0][n, :cut, :] = upper
            outs[0][n, cut:, :] = lower
        else:
            for keep, out in ((n == 0, outs[0]), (n == 1, outs[1])):

                @pl.when(swapped != keep)
                def _():
                    out[:cut, :] = upper
                    out[cut:, :] = lower


def reduce_planes(parts, planes, own, other):
    x = lax.axis_index("seq") // 2
    y = lax.axis_index("dp") % 2
    z = lax.axis_index("dp") // 2
    place = jnp.stack([x, y, z]).astype(jnp.int32)
    count, window = len(planes), own.shape[1]
    cut = window // 32 * 16
    got = swap(other, "seq", 1)
    token = yield [other], [got]
    upper, lower = (count, 2, cut, LANES), (count, 2, window - cut, LANES)
    one, sent_one, two, sent_two = plane_call(
        split_first, place, [own, tie(got, token)], [upper, upper, lower, lower]
    )
    got_one, got_two = swap(sent_one, "seq", 2), swap(sent_two, "dp", 1)
    token = yield [sent_one, sent_two], [got_one, got_two]
    upper, lower = (count, cut, LANES), (count, window - cut, LANES)
    one, sent_one, two, sent_two = plane_call(
        split_second, place, [one, tie(got_one, token), two, tie(got_two, token)],
        [upper, upper, lower, lower],
    )
    got_one, got_two = swap(sent_one, "dp", 1), swap(sent_two, "seq", 2)
    token = yield [sent_one, sent_two], [got_one, got_two]
    last = [one, tie(got_one, token), two, tie(got_two, token)]
    size = lax.axis_size("dp") // 2
    if size == 4 and planes == [1, 2]:
        mine, more = plane_call(join_parts, place, last, [(window, LANES)] * 2)
        got = [between_planes(mine, [(0, 1), (3, 2)]), between_planes(more, [(1, 2), (2, 1)])]
        token = yield [mine, more], got
        part = [mine] + [tie(value, token) for value in got]
        got = between_planes(tie(more, token), [(0, 2), (3, 1)])
        token = yield [more], [got]
        part = total(*part, tie(got, token))
        parts[1] = parts[2] = part
        return
    (part,) = plane_call(join_parts, place, last, [(count, window, LANES)])
    rest = [part[n] for n in range(count)]
    for n in range(len(toward(planes[0], size))):
        got = [
            between_planes(value, toward(plane, size)[n]) for value, plane in zip(rest, planes)
        ]
        token = yield rest, got
        rest = [total(value, tie(more, token)) for value, more in zip(rest, got)]
    parts.update(zip(planes, rest))


def set_out(flows):
    return move_on(flows, None)


def move_on(flows, token):
    sent, got = [], []
    for flow in flows:
        try:
            out, into = flow.send(token)
        except StopIteration:
            continue
        sent += out
        got += into
    return sent, got


def adam_body(
    place_ref, grad_ref, params_ref, first_ref, second_ref, out_ref, new_first_ref,
    new_second_ref,
    *, devices,
):
    core, first_row = place_ref[0], place_ref[1]
    rows = first_ref.shape[0]
    shift = grad_ref.shape[0] - rows
    grads = grad_ref[...].astype(f32)
    mean = jnp.where(core == 0, grads[:rows], grads[shift:]) * (1.0 / devices)
    first = first_decay * first_ref[...] + (1.0 - first_decay) * mean
    second = second_decay * second_ref[...] + (1.0 - second_decay) * mean * mean
    new_first_ref[...] = first
    new_second_ref[...] = second
    fix_one = 1.0 - first_decay**STEP
    fix_two = 1.0 - second_decay**STEP
    update = first / fix_one / (jnp.sqrt(second / fix_two) + adam_epsilon)
    row = first_row + iota((rows, LANES), 0)
    in_matrix = row < 0
    for low, high in (
        (ROW_QKV, ROW_BQ),
        (ROW_WO, ROW_BO),
        (ROW_FC, ROW_BFC),
        (ROW_PR, ROW_BPR),
    ):
        in_matrix = in_matrix | ((row >= low) & (row < high))
    out_ref[...] = params_ref[...] - jnp.where(in_matrix, base_rate / D, base_rate) * update


def adam(place, grads, params, first, second, devices):
    shape = jax.ShapeDtypeStruct(first.shape, f32)
    return pl.pallas_call(
        partial(adam_body, devices=devices),
        in_specs=[smem] + [vmem] * 4,
        out_specs=[vmem] * 3,
        out_shape=[shape] * 3,
        compiler_params=params_of(8),
        cost_estimate=cost(1e6, 6e6),
    )(place, grads, params, first, second)


def total_of(result, value):
    bits = [("seq", 1)]
    bits += [("dp", 1 << n) for n in range(1, lax.axis_size("dp").bit_length() - 1)]
    bits += [("dp", 1)]
    bits += [("seq", 1 << n) for n in range(1, lax.axis_size("seq").bit_length() - 1)]
    for axis, bit in bits:
        got = swap(value, axis, bit)
        token = yield [value], [got]
        value = value + tie(got, token)
    result.append(value)


def gate(value, after):
    return kernel_call(
        lambda *_: None,
        [value],
        [anywhere],
        after,
        out_specs=anywhere,
        out_shape=jax.ShapeDtypeStruct(value.shape, value.dtype),
        input_output_aliases={0: 0},
        compiler_params=params_of(4),
        cost_estimate=cost(1e6, 1e4),
    )


def shards(tokens, cotangent, loss_mask, segments, params, first_moment, second_moment):
    block = tokens.shape[0]
    seq_index = lax.axis_index("seq")
    core = seq_index % 2
    x = seq_index // 2
    shard_rows = first_moment.shape[0]
    total_rows = params.shape[0]
    chip = 2 * block
    device_count = lax.axis_size(("dp", "seq"))

    def unpick(value):
        low, high = value[:BLK], value[BLK:]
        got = swap(jnp.where(core == 0, high, low), "seq", 1)
        return jnp.where(
            core == 0, jnp.concatenate([low, got]), jnp.concatenate([high, got])
        )

    own_x = tokens.reshape(block, D)
    got_x = swap(own_x, "seq", 1)
    far_own = swap(own_x, "seq", 2)
    far_got = swap(far_own, "seq", 1)
    own_dy = cotangent.reshape(block, D) * loss_mask.astype(bf16)
    got_dy = swap(own_dy, "seq", 1)

    w_qkv = unpack_matrix(params, ROW_QKV, D, 3 * D, 4)
    w_out = unpack_matrix(params, ROW_WO, D, D, 2)
    w_up = unpack_matrix(params, ROW_FC, D, FF, 4)
    w_down = unpack_matrix(params, ROW_PR, FF, D, 4)

    norm_rows, bias_rows, *feed_rows = take_rows(
        params, [(ROW_G1, 16), (ROW_BQ, 16), (ROW_BO, 24), (ROW_BFC, 32), (ROW_BPR, 8)]
    )
    seg_row = segments.reshape(1, -1)
    near_rows = [core * BLK, (3 - core) * BLK]
    q_place = [x * chip + row for row in near_rows]
    place = jnp.stack(q_place + [core, x] + near_rows).astype(jnp.int32)
    masks = (place, seg_row, seg_row.astype(f32))

    bias_sum = jnp.sum(rounded(branch_scale * own_dy.astype(f32)).astype(f32), axis=0)
    bias_total = []
    sums = [total_of(bias_total, bias_sum.reshape(-1, LANES))]
    near_n, near_k, near_kt, near_v, near_vt, queries = project(
        place, own_x, got_x, norm_rows, bias_rows, w_qkv, True, []
    )
    state = attend(*masks, queries, near_k, near_vt, None, [])
    far_n, far_k, far_kt, far_v, far_vt = project(
        place, far_own, far_got, norm_rows, bias_rows, w_qkv, False, []
    )
    attn, attn_t, log_sum = attend(*masks, queries, far_k, far_vt, state, [])
    (
        active, d_up, two_n, d_mlp, d_attn, d_resid, d_heads, delta, block_low, vec, d_bias_up
    ) = feed(
        place, attn, attn_t, own_x, got_x, own_dy, got_dy, feed_rows, w_out, w_up, w_down
    )
    up_rows = d_bias_up.reshape(24, LANES)

    core_x = jnp.stack([core, x]).astype(jnp.int32)
    parts = {}

    def grads(*given, **options):
        planes, halves_of, left = weight_grad(core_x, *given, **options)
        return [reduce_planes(parts, planes, *halves_of)] if planes else [], left

    plane_rows = 8 * shard_rows
    down, left = grads(
        [(active, d_mlp, 0, False)], [up_rows, vec], None, None, ROW_PR, [(0, 0, 22, 2)],
        [(2, 1, 18, 6)], shard_rows, total_rows, [], 15e9,
    )
    _, core_down = set_out(down)
    _, out_rows = grads(
        [(attn, d_attn, 0, False)], [vec], None, None, ROW_WO, [], [(8, 0, 0, 8)], shard_rows,
        down16(ROW_FC), [], 4e9, whole=False,
    )
    up, left = grads(
        [(two_n, d_up, 0, False)], [up_rows, vec], out_rows, left, ROW_FC, [(0, 1, 8, 10)],
        [(10, 0, 0, 22)], shard_rows, -(-down16(ROW_PR) // plane_rows) * plane_rows, [], 10e9,
    )
    sent_up, core_up = set_out(up)
    sent_down, one_down = move_on(down, None)

    given = (*masks, queries, d_heads, log_sum, delta)
    d_near, dq_t = attend_back(
        *given, (near_k, near_kt, near_v), None, core_down + sent_up + sent_down
    )
    sent_up, one_up = move_on(up, dq_t)
    sent_down, two_down = move_on(down, dq_t)
    d_far, dq = attend_back(
        *given, (far_k, far_kt, far_v), dq_t, core_up + one_down + sent_up + sent_down
    )
    sent_down, z_down = move_on(down, d_far)
    sent_up, two_up = move_on(up, d_far)
    far_in, near_in, one_vec = input_back(
        place, (far_own, far_got), (own_x, got_x), d_far, d_near, dq, d_resid, w_qkv, norm_rows,
        two_down + sent_up + sent_down,
    )

    own_far, other_far = halves(far_in, 0, core)
    other_far = rounded(other_far)
    far_got = swap(other_far, "seq", 1)
    own, other = halves(near_in, 0, core)
    other = rounded(other)
    near_got = swap(other, "seq", 1)
    sent_up, z_up = move_on(up, one_vec)
    sent_down, last_down = move_on(down, one_vec)
    if left is not None:
        extra = jnp.concatenate([one_vec[16:], jnp.zeros((left.shape[0] - 8, LANES), f32)])
        left = rounded(left.astype(f32) + extra)
    planes, (own_qkv, other_qkv), _ = weight_grad(
        core_x, [(near_n, dq, 0, False), (near_n, d_near, D, False), (far_n, d_far, D, True)], [one_vec],
        None, left, ROW_QKV, [(0, 0, 0, 12)], [(12, 0, 12, 4)], shard_rows,
        -(-down16(ROW_WO) // plane_rows) * plane_rows,
        two_up + z_down + sent_up + sent_down + [other_far, other], 15e9,
    )
    qkv = [reduce_planes(parts, planes, own_qkv, gate(other_qkv, z_up + last_down))]
    sent_qkv, _ = set_out(qkv)
    set_out(sums)
    sent_qkv, _ = move_on(qkv, None)
    _, z_up = move_on(up, sent_qkv)
    move_on(sums, sent_qkv)
    sent_qkv, _ = move_on(qkv, z_up)
    move_on(sums, sent_qkv)
    far_sum = rounded(own_far + tie(far_got, sent_qkv).astype(f32))
    from_far = swap(far_sum, "seq", 2)
    move_on(up, sent_qkv)
    sent_qkv, _ = move_on(qkv, None)
    move_on(sums, sent_qkv)
    input_grad = own + tie(near_got, sent_qkv).astype(f32)
    block_output = unpick(tie(block_low, sent_qkv))
    sent_qkv, _ = move_on(qkv, None)
    move_on(sums, sent_qkv)
    while move_on(qkv + up + down + sums, None)[0]:
        pass
    input_grad = rounded(jnp.where(x == 0, input_grad + from_far.astype(f32), input_grad))
    bias_down_grad = bias_total[0].reshape(-1) / device_count

    own_plane = lax.axis_index("dp") // 2
    summed = jnp.zeros((core_window(shard_rows), LANES), bf16)
    for plane in sorted(parts, reverse=True):
        summed = jnp.where(own_plane == plane, parts[plane], summed)
    first_row = lax.axis_index(("dp", "seq")) * shard_rows
    own_params = lax.dynamic_slice_in_dim(params, first_row, shard_rows, 0)
    new_params, new_first, new_second = adam(
        jnp.stack([core, first_row]).astype(jnp.int32), summed, own_params, first_moment,
        second_moment, device_count,
    )
    return (
        block_output.reshape(tokens.shape),
        input_grad.reshape(tokens.shape),
        new_params,
        new_first,
        new_second,
        bias_down_grad,
    )


def solution(mesh):
    return jax.shard_map(
        shards,
        mesh=mesh,
        in_specs=(
            P("seq", "dp", None),
            P("seq", "dp", None),
            P("seq", "dp"),
            P(None, "dp"),
            P(),
            P(("dp", "seq"), None),
            P(("dp", "seq"), None),
        ),
        out_specs=(
            P("seq", "dp", None),
            P("seq", "dp", None),
            P(("dp", "seq"), None),
            P(("dp", "seq"), None),
            P(("dp", "seq"), None),
            P(),
        ),
        check_vma=False,
    )
```

```python
from functools import partial
import math

import jax
import jax.numpy as jnp
from jax import lax
from jax.experimental import pallas as pl
from jax.experimental.pallas import tpu as pltpu
from jax.sharding import PartitionSpec as P

D = 768
HEADS = 12
HEAD_DIM = 64
FF = 3072
STEP = 4
LANES = 128
BLK = 256

norm_epsilon = 1e-05
branch_scale = 48.0 ** (-0.5)
first_decay = 0.9
second_decay = 0.95
adam_epsilon = 1e-08
base_rate = 0.1
masked_score = -1e30
LOG2E = 1.4426950408889634
score_factor = LOG2E / HEAD_DIM

f32 = jnp.float32
bf16 = jnp.bfloat16

ROW_G1, ROW_S1 = 0, 6
ROW_QKV = 12
ROW_BQ = ROW_QKV + D * 3 * D // LANES
ROW_BV = ROW_BQ + 6
ROW_WO = ROW_BV + 6
ROW_BO = ROW_WO + D * D // LANES
ROW_G2, ROW_S2 = ROW_BO + 6, ROW_BO + 12
ROW_FC = ROW_BO + 18
ROW_BFC = ROW_FC + D * FF // LANES
ROW_PR = ROW_BFC + FF // LANES
ROW_BPR = ROW_PR + D * FF // LANES
ROW_END = ROW_BPR + 6

VMEM = 56 * 1024 * 1024


nt_dims = (((1,), (1,)), ((), ()))
nn_dims = (((1,), (0,)), ((), ()))
tn_dims = (((0,), (0,)), ((), ()))

smem = pl.BlockSpec(memory_space=pltpu.SMEM)
vmem = pl.BlockSpec(memory_space=pltpu.VMEM)
anywhere = pl.BlockSpec(memory_space=pl.ANY)


def params_of(mebibytes):
    return pltpu.CompilerParams(vmem_limit_bytes=mebibytes << 20)


def cost(flops, moved):
    return pl.CostEstimate(flops=int(flops), bytes_accessed=int(moved), transcendentals=0)


def few_rows(count):
    return pl.BlockSpec((count, LANES), lambda *_: (0, 0))


def row_of(ref, start, rows=6):
    return jnp.concatenate([ref[start + j : start + j + 1, :] for j in range(rows)], axis=1)


def column_of(row):
    return jnp.broadcast_to(row, (8, row.shape[1])).T[:, :1]


def dot(a, b, dims=nn_dims):
    return lax.dot_general(a, b, dims, preferred_element_type=f32)


def iota(shape, axis):
    return lax.broadcasted_iota(jnp.int32, shape, axis)


def kernel_call(body, operands, in_specs, after=(), **options):
    count = len(operands)

    def without(*refs):
        body(*refs[:count], *refs[count + len(after) :])

    return pl.pallas_call(without, in_specs=in_specs + [anywhere] * len(after), **options)(
        *operands, *after
    )


def down16(row):
    return row // 16 * 16


def group_rows(blocks):
    return 8 if blocks > 8 else 32


def side_by_side(value, other):
    return jnp.concatenate([value, other], axis=1)


def unpack_body(x_ref, o_ref, move, *, shift, rows, blocks, pairs):
    size = rows * blocks
    bits = rows.bit_length() - 1

    @pl.when(pl.program_id(0) == 0)
    def _():
        to, come = iota(move.shape, 0), iota(move.shape, 1)
        move[...] = (come == shift + (to & (rows - 1)) * blocks + (to >> bits)).astype(bf16)

    for n in range(pairs):
        both = side_by_side(
            *[x_ref[pl.ds((2 * n + side) * size, size + 16), :].astype(bf16) for side in (0, 1)]
        )
        moved = dot(move[...], both)
        for j in range(blocks):
            part = moved[j * rows : (j + 1) * rows]
            part = jnp.concatenate([part[:, :LANES], part[:, LANES:]], axis=0).astype(bf16)
            o_ref[2 * n * rows : 2 * (n + 1) * rows, j * LANES : (j + 1) * LANES] = part


def take_body(*refs):
    count = len(refs) // 2
    for x_ref, o_ref in zip(refs[:count], refs[count:]):
        o_ref[...] = x_ref[...]


def take_rows(params, runs):
    runs = [(first // 8 * 8, count) for first, count in runs]

    def window(first, count):
        return pl.BlockSpec((pl.Element(count), pl.Element(LANES)), lambda i: (first, 0))

    return pl.pallas_call(
        take_body,
        grid=(1,),
        in_specs=[window(first, count) for first, count in runs],
        out_specs=[pl.BlockSpec((count, LANES), lambda i: (0, 0)) for _, count in runs],
        out_shape=[jax.ShapeDtypeStruct((count, LANES), f32) for _, count in runs],
        compiler_params=params_of(48),
    )(*[params] * len(runs))


def unpack_matrix(params, row, matrix_rows, columns, steps):
    blocks = columns // LANES
    rows = group_rows(blocks)
    base = row // 8 * 8
    chunk = matrix_rows // steps
    size = chunk * blocks
    return pl.pallas_call(
        partial(
            unpack_body, shift=row - base, rows=rows, blocks=blocks, pairs=chunk // rows // 2
        ),
        grid=(steps,),
        in_specs=[
            pl.BlockSpec(
                (pl.Element(size + 16), pl.Element(LANES)),
                lambda i: (pl.multiple_of(base + i * size, 8), 0),
            )
        ],
        out_specs=pl.BlockSpec((chunk, columns), lambda i: (i, 0)),
        out_shape=jax.ShapeDtypeStruct((matrix_rows, columns), bf16),
        scratch_shapes=[pltpu.VMEM((rows * blocks, rows * blocks + 16), bf16)],
        compiler_params=params_of(38),
        cost_estimate=cost(8e9, 6 * matrix_rows * columns),
    )(params)


def grad_body(
    core_ref,
    *refs,
    products,
    vectors,
    below,
    rest,
    base,
    row,
    matrix_rows,
    columns,
    head,
    tail,
    planes,
    plane_rows,
    keep,
):
    refs = list(refs)
    factors = [refs.pop(0) for _ in range(2 * len(products))]
    vector_refs = [refs.pop(0) for _ in range(vectors)]
    below_ref = refs.pop(0) if below else None
    rest_ref = refs.pop(0) if rest else None
    own_ref, other_ref = (refs.pop(0), refs.pop(0)) if planes else (None, None)
    keep_ref = refs.pop(0) if keep else None
    window, grad, move, carry, last = refs
    blocks = columns // LANES
    rows = group_rows(blocks)
    bits = rows.bit_length() - 1
    size = rows * blocks
    shift = row - base
    body_rows = matrix_rows * blocks
    tail_rows = last.shape[0]
    if below:
        window[pl.ds(0, below), :] = below_ref[...]
    if rest:
        window[pl.ds(below + body_rows + tail_rows, rest), :] = rest_ref[...]
    to, come = iota(move.shape, 0), iota(move.shape, 1)
    move[...] = (to == shift + (come & (rows - 1)) * blocks + (come >> bits)).astype(bf16)
    carry[...] = jnp.zeros_like(carry)
    last[...] = jnp.zeros_like(last)
    for place, n, start, count in head:
        carry[place : place + count, :] = vector_refs[n][start : start + count, :]
    for place, n, start, count in tail:
        last[place : place + count, :] = vector_refs[n][start : start + count, :]

    core = core_ref[0]
    wide_rows = grad.shape[0]

    def multiply(c, state):
        lanes = pl.ds(pl.multiple_of(c * wide_rows, wide_rows), wide_rows)
        for n, (at, far) in enumerate(products):
            a_ref, b_ref = factors[2 * n], factors[2 * n + 1]
            span = slice(at, at + b_ref.shape[1])
            if far:

                @pl.when(core_ref[1] == 1)
                def _():
                    grad[:, span] += dot(a_ref[:, lanes], b_ref[...], tn_dims)

            else:
                grad[:, span] = dot(a_ref[:, lanes], b_ref[...], tn_dims)

        left = carry[...]
        for pair in range(wide_rows // rows // 2):
            both = side_by_side(
                *[
                    jnp.concatenate(
                        [
                            grad[at : at + rows, j * LANES : (j + 1) * LANES]
                            for j in range(blocks)
                        ],
                        axis=0,
                    ).astype(bf16)
                    for at in (2 * pair * rows, (2 * pair + 1) * rows)
                ]
            )
            moved = dot(move[...], both)
            for side in (0, 1):
                part = moved[:, side * LANES : (side + 1) * LANES]
                at = (c * (wide_rows // rows) + 2 * pair + side) * size + below
                at = pl.multiple_of(at, 16)
                window[pl.ds(at, 16), :] = (part[:16] + left).astype(bf16)
                window[pl.ds(at + 16, size - 16), :] = part[16:size].astype(bf16)
                left = part[size:]
        carry[...] = left
        return state

    lax.fori_loop(0, matrix_rows // wide_rows, multiply, 0)
    last[pl.ds(0, 16), :] = last[pl.ds(0, 16), :] + carry[...]
    window[pl.ds(below + body_rows, tail_rows), :] = last[...].astype(bf16)
    half = plane_rows // 4
    for n, plane in enumerate(planes):
        part_rows = own_ref.shape[1]
        for block in range(4):
            for ref, which in ((own_ref, core), (other_ref, 1 - core)):
                at = plane * plane_rows - (base - below) + block * half
                at = pl.multiple_of(at + which * (half - part_rows), 16)
                ref[4 * n + block] = window[pl.ds(at, part_rows), :]
    if keep:
        keep_ref[...] = window[pl.ds(0, keep), :]


def weight_grad(
    place, products, vectors, below, rest, row, head, tail, shard_rows, top, after, work,
    whole=True,
):
    base = down16(row)
    matrix_rows = products[0][0].shape[1]
    columns = max(at + b.shape[1] for _, b, at, _ in products)
    blocks = columns // LANES
    rows = group_rows(blocks)
    size = rows * blocks
    plane_rows = 8 * shard_rows
    below_rows = 0 if below is None else below.shape[0]
    rest_rows = 0 if rest is None else rest.shape[0]
    first_row = base - below_rows
    chunk_rows = matrix_rows
    while matrix_rows % chunk_rows or chunk_rows * columns > 900000 or chunk_rows > 512:
        chunk_rows -= LANES
    tail_rows = top - rest_rows - base - matrix_rows * blocks
    first_plane = -(-first_row // plane_rows)
    planes = list(range(first_plane, top // plane_rows)) if whole else []
    keep = first_plane * plane_rows - first_row if whole else top - first_row
    part = jax.ShapeDtypeStruct((4 * len(planes), core_window(shard_rows), LANES), bf16)
    out_shape = [part, part] if planes else []
    if keep:
        out_shape.append(jax.ShapeDtypeStruct((keep, LANES), bf16))
    operands = [value for pair in products for value in pair[:2]] + list(vectors)
    operands += [value for value in (below, rest) if value is not None]
    outs = kernel_call(
        partial(
            grad_body,
            products=[pair[2:] for pair in products],
            vectors=len(vectors),
            below=below_rows,
            rest=rest_rows,
            base=base,
            row=row,
            matrix_rows=matrix_rows,
            columns=columns,
            head=head,
            tail=tail,
            planes=planes,
            plane_rows=plane_rows,
            keep=keep,
        ),
        [place] + operands,
        [smem] + [vmem] * len(operands),
        after,
        out_specs=[vmem] * len(out_shape),
        out_shape=out_shape,
        scratch_shapes=[
            pltpu.VMEM((top - first_row, LANES), bf16),
            pltpu.VMEM((chunk_rows, columns), f32),
            pltpu.VMEM((size + 16, size), bf16),
            pltpu.VMEM((16, LANES), f32),
            pltpu.VMEM((tail_rows, LANES), f32),
        ],
        compiler_params=params_of(16),
        cost_estimate=cost(work, 4 * matrix_rows * columns),
    )
    return planes, tuple(outs[:2]) if planes else None, outs[-1] if keep else None


def row_mean(value):
    return jnp.sum(value, axis=-1, keepdims=True) * (1.0 / value.shape[-1])


def norm_parts(values):
    center = values - row_mean(values)
    rstd = lax.rsqrt(row_mean(center * center) + norm_epsilon)
    return center * rstd, rstd


def norm_back(unit, rstd, gain, grad):
    scaled = grad * gain
    return rstd * (scaled - row_mean(scaled) - unit * row_mean(scaled * unit))


def project_body(place_ref, own_ref, got_ref, norm_ref, bias_ref, w_ref, *outs, with_query):
    n_ref, k_ref, kt_ref, v_ref, vt_ref = outs[:5]
    mine = pl.program_id(0) // 2 == place_ref[2]
    x = jnp.where(mine, own_ref[...], got_ref[...])
    unit, _ = norm_parts(x.astype(f32))
    normed = (unit * row_of(norm_ref, 0) + row_of(norm_ref, 6)).astype(bf16)
    n_ref[...] = normed
    keys = dot(normed, w_ref[:, D : 2 * D]).astype(bf16)
    k_ref[...] = keys
    kt_ref[...] = keys.T
    bias = ROW_BQ % 8
    values = (dot(normed, w_ref[:, 2 * D :]) + row_of(bias_ref, bias + 6)).astype(bf16)
    v_ref[...] = values
    vt_ref[...] = values.T
    if with_query:
        outs[5][...] = (dot(normed, w_ref[:, :D]) + row_of(bias_ref, bias)).astype(bf16)


def project(place, own, got, norm_rows, bias_rows, w_qkv, with_query, after):
    count = 2 * own.shape[0]
    half = own.shape[0] // BLK
    by_rows = pl.BlockSpec((BLK, D), lambda i: (i, 0))
    by_halves = pl.BlockSpec((BLK, D), lambda i: (i % half, 0))
    by_columns = pl.BlockSpec((D, BLK), lambda i: (0, i))
    tall = jax.ShapeDtypeStruct((count, D), bf16)
    wide = jax.ShapeDtypeStruct((D, count), bf16)
    return kernel_call(
        partial(project_body, with_query=with_query),
        [place, own, got, norm_rows, bias_rows, w_qkv],
        [
            smem,
            by_halves,
            by_halves,
            few_rows(16),
            few_rows(16),
            pl.BlockSpec((D, 3 * D), lambda i: (0, 0)),
        ],
        after,
        grid=(count // BLK,),
        out_specs=[by_rows, by_rows, by_columns, by_rows, by_columns]
        + [by_rows] * with_query,
        out_shape=[tall, tall, wide, tall, wide] + [tall] * with_query,
        compiler_params=params_of(12),
        cost_estimate=cost(2 * count * D * (2 + with_query) * D, 12 * count * D),
    )


def head_lanes(value, odd):
    lane = iota(value.shape, 1)
    keep = (lane >= HEAD_DIM) if odd else (lane < HEAD_DIM)
    return jnp.where(keep, value, jnp.zeros_like(value))


def visit_block(place_ref, seg_ref, segs_ref, bias_ref, i, k_start, valid, step):
    q_start = place_ref[i]
    q_first = seg_ref[0, q_start]
    q_last = seg_ref[0, q_start + BLK - 1]
    k_first = seg_ref[0, k_start]
    k_last = seg_ref[0, k_start + BLK - 1]
    active = valid & (k_start <= q_start) & (k_last >= q_first)
    plain = (k_first == q_last) & (k_start + BLK <= q_start)

    @pl.when(active & plain)
    def _():
        step(False)

    @pl.when(active & jnp.logical_not(plain))
    def _():
        k_pos = k_start + iota((BLK, BLK), 0)
        q_pos = q_start + iota((BLK, BLK), 1)
        segk = column_of(segs_ref[:, pl.ds(pl.multiple_of(k_start, BLK), BLK)])
        same = segk == segs_ref[:, pl.ds(pl.multiple_of(q_start, BLK), BLK)]
        bias_ref[...] = jnp.where((k_pos <= q_pos) & same, 0.0, masked_score)
        step(True)


ACC = HEAD_DIM + 16


def attend_body(
    place_ref, seg_ref, segs_ref, q_ref, k_ref, vt_ref, *refs, first
):
    if first:
        acc_ref, top_ref, bias_ref, s_ref = refs
        acc_ref[...] = jnp.zeros_like(acc_ref)
        top_ref[...] = jnp.full_like(top_ref, masked_score)
    else:
        acc_in, top_in, out_ref, outt_ref, total_ref, bias_ref, s_ref, acc_ref, top_ref = refs
        acc_ref[...] = acc_in[...]
        top_ref[...] = top_in[...]
    ones = jnp.ones((16, BLK), bf16)
    count = k_ref.shape[0] // BLK
    x = place_ref[3]
    base = x * (count * BLK) if first else 0 * x
    valid = (x >= 0) if first else (x == 1)
    for i in range(2):
        cols = slice(i * BLK, (i + 1) * BLK)

        def visit(n, carry):
            kb = count - 1 - n
            k_rows = pl.ds(pl.multiple_of(kb * BLK, BLK), BLK)
            q_rows = pl.ds(pl.multiple_of(place_ref[4 + i], BLK), BLK)

            def step(masked):
                tops = []
                for h in range(HEADS):
                    pair, odd = h // 2, h % 2
                    lanes = slice(pair * LANES, (pair + 1) * LANES)
                    s = dot(k_ref[k_rows, lanes], head_lanes(q_ref[q_rows, lanes], odd), nt_dims)
                    s = s * score_factor
                    if masked:
                        s = s + bias_ref[...]
                    s_ref[h] = s
                    tops.append(jnp.max(s, axis=0, keepdims=True))
                old = top_ref[:HEADS, cols]
                new = jnp.maximum(old, jnp.concatenate(tops, axis=0))
                top_ref[:HEADS, cols] = new
                scale = jnp.exp2(old - new)
                for h in range(HEADS):
                    p = jnp.exp2(s_ref[h] - new[h : h + 1]).astype(bf16)
                    v_part = jnp.concatenate(
                        [vt_ref[h * HEAD_DIM : (h + 1) * HEAD_DIM, k_rows], ones], axis=0
                    )
                    acc_ref[h, :, cols] = acc_ref[h, :, cols] * scale[h : h + 1] + dot(v_part, p)

            visit_block(
                place_ref, seg_ref, segs_ref, bias_ref, i, base + kb * BLK, valid, step
            )
            return carry

        lax.fori_loop(0, count, visit, 0)
    if not first:
        for h in range(HEADS):
            total = acc_ref[h, HEAD_DIM : HEAD_DIM + 1, :]
            outt_ref[h * HEAD_DIM : (h + 1) * HEAD_DIM, :] = acc_ref[h, :HEAD_DIM, :] / total
            total_ref[h : h + 1, :] = top_ref[h : h + 1, :] + jnp.log2(total)
        for i in range(2):
            cols = slice(i * BLK, (i + 1) * BLK)
            out_ref[cols, :] = outt_ref[:, cols].T.astype(bf16)


def attend(place, seg, segs, q, k, vt, state, after):
    count = 2 * BLK
    first = state is None
    acc_shape = jax.ShapeDtypeStruct((HEADS, ACC, count), f32)
    row_shape = jax.ShapeDtypeStruct((16, count), f32)
    if first:
        outs = (acc_shape, row_shape)
    else:
        outs = (
            jax.ShapeDtypeStruct((count, D), bf16),
            jax.ShapeDtypeStruct((D, count), f32),
            row_shape,
        )
    extra = () if first else state
    held = [] if first else [pltpu.VMEM((HEADS, ACC, count), f32), pltpu.VMEM((16, count), f32)]
    return kernel_call(
        partial(attend_body, first=first),
        [place, seg, segs, q, k, vt, *extra],
        [smem, smem] + [vmem] * (4 + len(extra)),
        after,
        out_specs=(vmem,) * len(outs),
        out_shape=outs,
        scratch_shapes=[pltpu.VMEM((BLK, BLK), f32), pltpu.VMEM((HEADS, BLK, BLK), f32)] + held,
        compiler_params=params_of(14),
        cost_estimate=cost(15e9, 8e6),
    )


def two_heads(value):
    return jnp.concatenate([head_lanes(value, 0), head_lanes(value, 1)], axis=0)


def attend_back_body(
    place_ref, seg_ref, segs_ref, q_ref, do_ref, total_ref, delta_ref, k_ref, kt_ref,
    v_ref, *refs, near
):
    if near:
        out_ref, dqt_ref, bias_ref, dk_acc, dv_acc, q_two, do_two, s_ref, da_ref = refs
        dqt_ref[...] = jnp.zeros_like(dqt_ref)
    else:
        dqt_in, out_ref, dq_ref, bias_ref, dk_acc, dv_acc, q_two, do_two, s_ref, da_ref, dqt_ref = (
            refs
        )
        dqt_ref[...] = dqt_in[...]
        dq_ref[...] = jnp.zeros_like(dq_ref)
    count = k_ref.shape[0] // BLK
    x = place_ref[3]
    base = x * (count * BLK) if near else 0 * x
    valid = (x >= 0) if near else (x == 1)
    pairs = HEADS // 2

    @pl.when(valid)
    def _():
        for i in range(2):
            q_rows = pl.ds(pl.multiple_of(place_ref[4 + i], BLK), BLK)
            for pair in range(pairs):
                lanes = slice(pair * LANES, (pair + 1) * LANES)
                q_two[i, pair] = two_heads(q_ref[q_rows, lanes])
                do_two[i, pair] = two_heads(do_ref[i * BLK : (i + 1) * BLK, lanes])

    def visit(kb, carry):
        k_rows = pl.ds(pl.multiple_of(kb * BLK, BLK), BLK)
        dk_acc[...] = jnp.zeros_like(dk_acc)
        dv_acc[...] = jnp.zeros_like(dv_acc)
        for i in range(2):
            cols = slice(i * BLK, (i + 1) * BLK)

            def step(masked):
                def row_two(ref, pair):
                    return jnp.concatenate(
                        [ref[2 * pair : 2 * pair + 1, cols], ref[2 * pair + 1 : 2 * pair + 2, cols]],
                        axis=1,
                    )

                def scores(pair):
                    lanes = slice(pair * LANES, (pair + 1) * LANES)
                    s_ref[pair % 2] = dot(k_ref[k_rows, lanes], q_two[i, pair], nt_dims)
                    da_ref[pair % 2] = dot(v_ref[k_rows, lanes], do_two[i, pair], nt_dims)

                scores(0)
                for pair in range(pairs):
                    if pair + 1 < pairs:
                        scores(pair + 1)
                    lanes = slice(pair * LANES, (pair + 1) * LANES)
                    s = s_ref[pair % 2] * score_factor
                    if masked:
                        s = s + jnp.concatenate([bias_ref[...], bias_ref[...]], axis=1)
                    p = jnp.exp2(s - row_two(total_ref, pair))
                    ds = (p * (da_ref[pair % 2] - row_two(delta_ref, pair))).astype(bf16)
                    dv_acc[:, lanes] += dot(p.astype(bf16), do_two[i, pair])
                    dk_acc[:, lanes] += dot(ds, q_two[i, pair])
                    for odd in range(2):
                        h = 2 * pair + odd
                        head = slice(h * HEAD_DIM, (h + 1) * HEAD_DIM)
                        dqt_ref[head, cols] += dot(
                            kt_ref[head, k_rows], ds[:, odd * BLK : (odd + 1) * BLK]
                        )

            visit_block(
                place_ref, seg_ref, segs_ref, bias_ref, i, base + kb * BLK, valid, step
            )
        out_ref[k_rows, :D] = (dk_acc[...] * (1.0 / HEAD_DIM)).astype(bf16)
        out_ref[k_rows, D:] = dv_acc[...].astype(bf16)
        return carry

    lax.fori_loop(0, count, visit, 0)
    if not near:
        for i in range(2):
            q_rows = pl.ds(pl.multiple_of(place_ref[4 + i], BLK), BLK)
            part = dqt_ref[:, i * BLK : (i + 1) * BLK] * (1.0 / HEAD_DIM)
            dq_ref[q_rows, :] = part.T.astype(bf16)


def attend_back(place, seg, segs, q, do, total, delta, keys, dqt, after):
    near = dqt is None
    rows = q.shape[0]
    two = pltpu.VMEM((2, HEADS // 2, 2 * BLK, LANES), bf16)
    wide = pltpu.VMEM((2, BLK, 2 * BLK), f32)
    sums_of = pltpu.VMEM((BLK, D), f32)
    blocks = [pltpu.VMEM((BLK, BLK), f32), sums_of, sums_of, two, two, wide, wide]
    sums = jax.ShapeDtypeStruct((D, 2 * BLK), f32)
    operands = [place, seg, segs, q, do, total, delta, *keys] + ([] if near else [dqt])
    return kernel_call(
        partial(attend_back_body, near=near),
        operands,
        [smem, smem] + [vmem] * (len(operands) - 2),
        after,
        out_specs=[vmem] * 2,
        out_shape=[
            jax.ShapeDtypeStruct((rows, 2 * D), bf16),
            sums if near else jax.ShapeDtypeStruct((rows, D), bf16),
        ],
        scratch_shapes=blocks + ([] if near else [pltpu.VMEM((D, 2 * BLK), f32)]),
        compiler_params=params_of(16),
        cost_estimate=cost(30e9, 1e7),
    )


GELU_A = math.sqrt(2.0 / math.pi)
GELU_B = 0.044715
FF_BLK = 512
FF_PART = 256


def put_rows(ref, at, value):
    for j in range(value.shape[1] // LANES):
        ref[at + j : at + j + 1, :] = value[:, j * LANES : (j + 1) * LANES]


def column_sum(value):
    return jnp.sum(value, axis=0, keepdims=True)


def feed_body(
    place_ref, attn_ref, outt_ref, xo_ref, xg_ref, dyo_ref, dyg_ref, wo_ref, two_vec, wu_ref,
    bu_ref, wd_ref, bd_ref,
    act_ref, dup_ref, two_ref, dmlp_ref, dattn_ref, dresid_ref, dheads_ref, delta_ref, block_ref,
    vec_ref, dbu_ref,
    r1, unit, rstd, ym, dtwo,
):
    step = pl.program_id(0)
    core = place_ref[2]

    def picked(own_ref, got_ref, i):
        return jnp.where(core == i, own_ref[:BLK, :], got_ref[BLK:, :])

    @pl.when(step == 0)
    def _():
        for i in range(2):
            rows = slice(i * BLK, (i + 1) * BLK)
            ya = dot(attn_ref[rows, :], wo_ref[...]) + row_of(two_vec, 0)
            resid = picked(xo_ref, xg_ref, i).astype(f32) + branch_scale * ya
            r1[rows, :] = resid
            one, inverse = norm_parts(resid)
            unit[rows, :] = one
            rstd[rows, :] = inverse
            two_ref[rows, :] = (one * row_of(two_vec, 6) + row_of(two_vec, 12)).astype(bf16)
            dy = picked(dyo_ref, dyg_ref, i).astype(f32)
            dmlp_ref[rows, :] = (branch_scale * dy).astype(bf16)
        ym[...] = jnp.zeros_like(ym)
        dtwo[...] = jnp.zeros_like(dtwo)

    two, dmlp = two_ref[...], dmlp_ref[...]
    parts = [slice(n, n + FF_PART) for n in range(0, FF_BLK, FF_PART)]

    lane_rows = FF_BLK // LANES
    bias = bu_ref[pl.ds(ROW_BFC % 8 + step * lane_rows, lane_rows), :]
    bias = jnp.concatenate([bias[j : j + 1, :] for j in range(lane_rows)], axis=1)

    def ahead(part):
        return dot(two, wu_ref[:, part]) + bias[:, part], dot(dmlp, wd_ref[part, :], nt_dims)

    ready = ahead(parts[0])
    for n, part in enumerate(parts):
        u, dact = ready
        if n + 1 < len(parts):
            ready = ahead(parts[n + 1])
        square = u * u
        t = jnp.tanh(u * (GELU_A + (GELU_A * GELU_B) * square))
        half = 0.5 + 0.5 * t
        act = (u * half).astype(bf16)
        act_ref[:, part] = act
        slope = half + u * (half * (1.0 - t)) * (GELU_A + (3.0 * GELU_A * GELU_B) * square)
        dup = dact * slope
        dup_low = dup.astype(bf16)
        dup_ref[:, part] = dup_low
        put_rows(dbu_ref, part.start // LANES, column_sum(dup_low.astype(f32)))
    ym[...] += dot(act_ref[...], wd_ref[...])
    dtwo[...] += dot(dup_ref[...], wu_ref[...], nt_dims)

    @pl.when(step == pl.num_programs(0) - 1)
    def _():
        dg = jnp.zeros((1, D), f32)
        ds = jnp.zeros((1, D), f32)
        db = jnp.zeros((1, D), f32)
        dbd = jnp.zeros((1, D), f32)
        for i in range(2):
            rows = slice(i * BLK, (i + 1) * BLK)
            down = ym[rows, :] + row_of(bd_ref, ROW_BPR % 8)
            block_ref[rows, :] = (r1[rows, :] + branch_scale * down).astype(bf16)
            grad = dtwo[rows, :]
            one = unit[rows, :]
            dy = picked(dyo_ref, dyg_ref, i).astype(f32)
            dresid = dy + norm_back(one, rstd[rows, :], row_of(two_vec, 6), grad)
            dresid_ref[rows, :] = dresid
            dattn = (branch_scale * dresid).astype(bf16)
            dattn_ref[rows, :] = dattn
            dg = dg + column_sum(grad * one)
            ds = ds + column_sum(grad)
            db = db + column_sum(dattn.astype(f32))
            dbd = dbd + column_sum(dmlp_ref[rows, :].astype(f32))
            dheads_ref[rows, :] = dot(dattn, wo_ref[...], nt_dims).astype(bf16)
            back = dot(wo_ref[...], dattn, nt_dims).astype(bf16).astype(f32)
            both = back * outt_ref[:, rows]
            for h in range(HEADS):
                delta_ref[h : h + 1, rows] = column_sum(both[h * HEAD_DIM : (h + 1) * HEAD_DIM])
        vec_ref[...] = jnp.zeros_like(vec_ref)
        put_rows(vec_ref, 0, db)
        put_rows(vec_ref, 6, dg)
        put_rows(vec_ref, 12, ds)
        put_rows(vec_ref, 18, dbd)


def feed(place, attn, attn_t, x_own, x_got, dy_own, dy_got, rows, w_out, w_up, w_down):
    count = attn.shape[0]

    def whole(*shape):
        return pl.BlockSpec(shape, lambda k: (0,) * len(shape))

    wide = pl.BlockSpec((count, FF_BLK), lambda k: (0, k))
    tall = whole(count, D)
    steps = FF // FF_BLK
    lane_rows = FF_BLK // LANES
    shapes = [
        ((count, FF), bf16, wide),
        ((count, FF), bf16, wide),
        ((count, D), bf16, tall),
        ((count, D), bf16, tall),
        ((count, D), bf16, tall),
        ((count, D), f32, tall),
        ((count, D), bf16, tall),
        ((16, count), f32, whole(16, count)),
        ((count, D), bf16, tall),
        ((24, LANES), f32, whole(24, LANES)),
        (
            (steps, lane_rows, LANES),
            f32,
            pl.BlockSpec((pl.Squeezed(), lane_rows, LANES), lambda k: (k, 0, 0)),
        ),
    ]
    return pl.pallas_call(
        feed_body,
        grid=(steps,),
        in_specs=[
            smem,
            tall,
            whole(D, count),
            tall,
            tall,
            tall,
            tall,
            whole(D, D),
            few_rows(24),
            pl.BlockSpec((D, FF_BLK), lambda k: (0, k)),
            few_rows(32),
            pl.BlockSpec((FF_BLK, D), lambda k: (k, 0)),
            few_rows(8),
        ],
        out_specs=[spec for _, _, spec in shapes],
        out_shape=[jax.ShapeDtypeStruct(shape, kind) for shape, kind, _ in shapes],
        scratch_shapes=[
            pltpu.VMEM((count, D), f32),
            pltpu.VMEM((count, D), f32),
            pltpu.VMEM((count, 1), f32),
            pltpu.VMEM((count, D), f32),
            pltpu.VMEM((count, D), f32),
        ],
        compiler_params=params_of(20),
        cost_estimate=cost(40e9, 2e7),
    )(
        place, attn, attn_t, x_own, x_got, dy_own, dy_got, w_out, rows[0], w_up, rows[1], w_down,
        rows[2],
    )


def input_body(
    place_ref, fo_ref, fg_ref, no_ref, ng_ref, dfar_ref, dnear_ref, dq_ref, dresid_ref, w_ref,
    gain_ref, far_ref, near_ref, vec_ref, dg, ds, dbq, dbv,
):
    step = pl.program_id(0)
    count = pl.num_programs(0) // 2
    gain = row_of(gain_ref, 0)

    @pl.when(step == 0)
    def _():
        for ref in (dg, ds, dbq, dbv):
            ref[...] = jnp.zeros_like(ref)

    def back(own_ref, got_ref, dkv_ref, at, more):
        mine = at // 2 == place_ref[2]
        x = jnp.where(mine, own_ref[...], got_ref[...])
        unit, rstd = norm_parts(x.astype(f32))
        grad = dot(dkv_ref[...], w_ref[:, D:], nt_dims)
        if more:
            grad = grad + dot(dq_ref[...], w_ref[:, :D], nt_dims)
            dbq[...] += column_sum(dq_ref[...].astype(f32))
        dg[...] += column_sum(grad * unit)
        ds[...] += column_sum(grad)
        dbv[...] += column_sum(dkv_ref[:, D:].astype(f32))
        return norm_back(unit, rstd, gain, grad)

    @pl.when(step < count)
    def _():
        far_ref[...] = back(fo_ref, fg_ref, dfar_ref, step, False)

    @pl.when(step >= count)
    def _():
        at = step - count
        near_ref[...] = back(no_ref, ng_ref, dnear_ref, at, True)
        for i in range(2):

            @pl.when(at * BLK == place_ref[4 + i])
            def _():
                near_ref[...] += dresid_ref[i * BLK : (i + 1) * BLK, :]

    @pl.when(step == pl.num_programs(0) - 1)
    def _():
        put_rows(vec_ref, 0, dg[...])
        put_rows(vec_ref, 6, ds[...])
        put_rows(vec_ref, 12, dbq[...])
        put_rows(vec_ref, 18, dbv[...])


def input_back(place, far, near, d_far, d_near, dq, dresid, w_qkv, norm_rows, after):
    count = d_far.shape[0]
    steps = count // BLK

    def rows(width, index):
        return pl.BlockSpec((BLK, width), lambda i: (index(i), 0))

    def early(i):
        return jnp.minimum(i, steps - 1)

    def late(i):
        return jnp.maximum(i - steps, 0)

    return kernel_call(
        input_body,
        [place, *far, *near, d_far, d_near, dq, dresid, w_qkv, norm_rows],
        [
            smem,
            rows(D, lambda i: early(i) % 2),
            rows(D, lambda i: early(i) % 2),
            rows(D, lambda i: late(i) % 2),
            rows(D, lambda i: late(i) % 2),
            rows(2 * D, early),
            rows(2 * D, late),
            rows(D, late),
            pl.BlockSpec((2 * BLK, D), lambda i: (0, 0)),
            pl.BlockSpec((D, 3 * D), lambda i: (0, 0)),
            few_rows(16),
        ],
        after,
        grid=(2 * steps,),
        out_specs=[rows(D, early), rows(D, late), few_rows(24)],
        out_shape=[
            jax.ShapeDtypeStruct((count, D), f32),
            jax.ShapeDtypeStruct((count, D), f32),
            jax.ShapeDtypeStruct((24, LANES), f32),
        ],
        scratch_shapes=[pltpu.VMEM((1, D), f32)] * 4,
        compiler_params=params_of(12),
        cost_estimate=cost(15e9, 1e6),
    )


def rounded(value):
    return lax.reduce_precision(value, 8, 7).astype(bf16)


def bit_pairs(size, bit, sender=lambda place: True):
    return [(n, n ^ bit) for n in range(size) if sender(n)]


def swap(value, axis, bit):
    return lax.ppermute(value, axis, bit_pairs(lax.axis_size(axis), bit))


def halves(value, axis, which):
    size = value.shape[axis] // 2
    own = lax.dynamic_slice_in_dim(value, which * size, size, axis)
    other = lax.dynamic_slice_in_dim(value, (1 - which) * size, size, axis)
    return own, other


def total(*values):
    return rounded(sum(value.astype(f32) for value in values))


def core_window(shard_rows):
    return (shard_rows + 15) // 16 * 16


def toward(plane, size):
    if size == 4:
        return [
            [[(1, 0), (3, 2)], [(2, 0)]],
            [[(0, 1), (3, 2)], [(2, 1)]],
            [[(0, 1), (3, 2)], [(1, 2)]],
            [[(0, 1), (2, 3)], [(1, 3)]],
        ][plane]
    steps = []
    bit = 1
    while bit < size:
        away = [z for z in range(size) if (z ^ plane) & bit and not (z ^ plane) & (bit - 1)]
        steps.append([(z, z ^ bit) for z in away])
        bit *= 2
    return steps


def tie(value, token):
    return value if token is None else lax.optimization_barrier((value, token))[0]


def between_planes(value, step):
    pairs = [(2 * a + side, 2 * b + side) for a, b in step for side in (0, 1)]
    return lax.ppermute(value, "dp", pairs)


def plane_call(body, place, operands, shapes, after=()):
    operands = [place] + operands
    shapes = [jax.ShapeDtypeStruct(shape, bf16) for shape in shapes]
    return kernel_call(
        body,
        operands,
        [smem] + [vmem] * (len(operands) - 1),
        after,
        out_specs=[vmem] * len(shapes),
        out_shape=shapes,
        compiler_params=params_of(24),
        cost_estimate=cost(1e9, 1e6),
    )


def plus(a, b):
    return (a.astype(f32) + b.astype(f32)).astype(bf16)


def split_first(place_ref, own_ref, got_ref, one_ref, sent_one_ref, two_ref, sent_two_ref):
    x, y = place_ref[0], place_ref[1]
    cut = one_ref.shape[2]
    for n in range(one_ref.shape[0]):
        for side in (0, 1):
            for out, block in (
                (one_ref, 2 * side + x),
                (sent_one_ref, 2 * side + 1 - x),
            ):
                block = 4 * n + block
                out[n, side] = plus(own_ref[block, :cut, :], got_ref[block, :cut, :])
            for out, block in (
                (two_ref, 2 * y + side),
                (sent_two_ref, 2 * (1 - y) + side),
            ):
                block = 4 * n + block
                out[n, side] = plus(own_ref[block, cut:, :], got_ref[block, cut:, :])


def split_second(
    place_ref, one_ref, got_one_ref, two_ref, got_two_ref,
    one_out, sent_one_ref, two_out, sent_two_ref,
):
    x, y = place_ref[0], place_ref[1]
    for n in range(one_out.shape[0]):
        for out, left, right, at in (
            (one_out, one_ref, got_one_ref, y),
            (sent_one_ref, one_ref, got_one_ref, 1 - y),
            (two_out, two_ref, got_two_ref, x),
            (sent_two_ref, two_ref, got_two_ref, 1 - x),
        ):
            out[n] = plus(left[n, at], right[n, at])


def join_parts(place_ref, one_ref, got_one_ref, two_ref, got_two_ref, *outs):
    cut = one_ref.shape[1]
    swapped = place_ref[2] >= 2
    for n in range(one_ref.shape[0]):
        upper = plus(one_ref[n], got_one_ref[n])
        lower = plus(two_ref[n], got_two_ref[n])
        if len(outs) == 1:
            outs[0][n, :cut, :] = upper
            outs[0][n, cut:, :] = lower
        else:
            for keep, out in ((n == 0, outs[0]), (n == 1, outs[1])):

                @pl.when(swapped != keep)
                def _():
                    out[:cut, :] = upper
                    out[cut:, :] = lower


def reduce_planes(parts, planes, own, other):
    x = lax.axis_index("seq") // 2
    y = lax.axis_index("dp") % 2
    z = lax.axis_index("dp") // 2
    place = jnp.stack([x, y, z]).astype(jnp.int32)
    count, window = len(planes), own.shape[1]
    cut = window // 32 * 16
    got = swap(other, "seq", 1)
    token = yield [other], [got]
    upper, lower = (count, 2, cut, LANES), (count, 2, window - cut, LANES)
    one, sent_one, two, sent_two = plane_call(
        split_first, place, [own, tie(got, token)], [upper, upper, lower, lower]
    )
    got_one, got_two = swap(sent_one, "seq", 2), swap(sent_two, "dp", 1)
    token = yield [sent_one, sent_two], [got_one, got_two]
    upper, lower = (count, cut, LANES), (count, window - cut, LANES)
    one, sent_one, two, sent_two = plane_call(
        split_second, place, [one, tie(got_one, token), two, tie(got_two, token)],
        [upper, upper, lower, lower],
    )
    got_one, got_two = swap(sent_one, "dp", 1), swap(sent_two, "seq", 2)
    token = yield [sent_one, sent_two], [got_one, got_two]
    last = [one, tie(got_one, token), two, tie(got_two, token)]
    size = lax.axis_size("dp") // 2
    if size == 4 and planes == [1, 2]:
        mine, more = plane_call(join_parts, place, last, [(window, LANES)] * 2)
        got = [between_planes(mine, [(0, 1), (3, 2)]), between_planes(more, [(1, 2), (2, 1)])]
        token = yield [mine, more], got
        part = [mine] + [tie(value, token) for value in got]
        got = between_planes(tie(more, token), [(0, 2), (3, 1)])
        token = yield [more], [got]
        part = total(*part, tie(got, token))
        parts[1] = parts[2] = part
        return
    (part,) = plane_call(join_parts, place, last, [(count, window, LANES)])
    rest = [part[n] for n in range(count)]
    for n in range(len(toward(planes[0], size))):
        got = [
            between_planes(value, toward(plane, size)[n]) for value, plane in zip(rest, planes)
        ]
        token = yield rest, got
        rest = [total(value, tie(more, token)) for value, more in zip(rest, got)]
    parts.update(zip(planes, rest))


def set_out(flows):
    return move_on(flows, None)


def move_on(flows, token):
    sent, got = [], []
    for flow in flows:
        try:
            out, into = flow.send(token)
        except StopIteration:
            continue
        sent += out
        got += into
    return sent, got


def adam_body(
    place_ref, grad_ref, params_ref, first_ref, second_ref, out_ref, new_first_ref,
    new_second_ref,
    *, devices,
):
    core, first_row = place_ref[0], place_ref[1]
    rows = first_ref.shape[0]
    shift = grad_ref.shape[0] - rows
    grads = grad_ref[...].astype(f32)
    mean = jnp.where(core == 0, grads[:rows], grads[shift:]) * (1.0 / devices)
    first = first_decay * first_ref[...] + (1.0 - first_decay) * mean
    second = second_decay * second_ref[...] + (1.0 - second_decay) * mean * mean
    new_first_ref[...] = first
    new_second_ref[...] = second
    fix_one = 1.0 - first_decay**STEP
    fix_two = 1.0 - second_decay**STEP
    update = first / fix_one / (jnp.sqrt(second / fix_two) + adam_epsilon)
    row = first_row + iota((rows, LANES), 0)
    in_matrix = row < 0
    for low, high in (
        (ROW_QKV, ROW_BQ),
        (ROW_WO, ROW_BO),
        (ROW_FC, ROW_BFC),
        (ROW_PR, ROW_BPR),
    ):
        in_matrix = in_matrix | ((row >= low) & (row < high))
    out_ref[...] = params_ref[...] - jnp.where(in_matrix, base_rate / D, base_rate) * update


def adam(place, grads, params, first, second, devices):
    shape = jax.ShapeDtypeStruct(first.shape, f32)
    return pl.pallas_call(
        partial(adam_body, devices=devices),
        in_specs=[smem] + [vmem] * 4,
        out_specs=[vmem] * 3,
        out_shape=[shape] * 3,
        compiler_params=params_of(8),
        cost_estimate=cost(1e6, 6e6),
    )(place, grads, params, first, second)


def total_of(result, value):
    bits = [("seq", 1)]
    bits += [("dp", 1 << n) for n in range(1, lax.axis_size("dp").bit_length() - 1)]
    bits += [("dp", 1)]
    bits += [("seq", 1 << n) for n in range(1, lax.axis_size("seq").bit_length() - 1)]
    for axis, bit in bits:
        got = swap(value, axis, bit)
        token = yield [value], [got]
        value = value + tie(got, token)
    result.append(value)


def gate(value, after):
    return kernel_call(
        lambda *_: None,
        [value],
        [anywhere],
        after,
        out_specs=anywhere,
        out_shape=jax.ShapeDtypeStruct(value.shape, value.dtype),
        input_output_aliases={0: 0},
        compiler_params=params_of(4),
        cost_estimate=cost(1e6, 1e4),
    )


def shards(tokens, cotangent, loss_mask, segments, params, first_moment, second_moment):
    block = tokens.shape[0]
    seq_index = lax.axis_index("seq")
    core = seq_index % 2
    x = seq_index // 2
    shard_rows = first_moment.shape[0]
    total_rows = params.shape[0]
    chip = 2 * block
    device_count = lax.axis_size(("dp", "seq"))

    def unpick(value):
        low, high = value[:BLK], value[BLK:]
        got = swap(jnp.where(core == 0, high, low), "seq", 1)
        return jnp.where(
            core == 0, jnp.concatenate([low, got]), jnp.concatenate([high, got])
        )

    own_x = tokens.reshape(block, D)
    got_x = swap(own_x, "seq", 1)
    far_own = swap(own_x, "seq", 2)
    far_got = swap(far_own, "seq", 1)
    own_dy = cotangent.reshape(block, D) * loss_mask.astype(bf16)
    got_dy = swap(own_dy, "seq", 1)

    w_qkv = unpack_matrix(params, ROW_QKV, D, 3 * D, 4)
    w_out = unpack_matrix(params, ROW_WO, D, D, 2)
    w_up = unpack_matrix(params, ROW_FC, D, FF, 4)
    w_down = unpack_matrix(params, ROW_PR, FF, D, 4)

    norm_rows, bias_rows, *feed_rows = take_rows(
        params, [(ROW_G1, 16), (ROW_BQ, 16), (ROW_BO, 24), (ROW_BFC, 32), (ROW_BPR, 8)]
    )
    seg_row = segments.reshape(1, -1)
    near_rows = [core * BLK, (3 - core) * BLK]
    q_place = [x * chip + row for row in near_rows]
    place = jnp.stack(q_place + [core, x] + near_rows).astype(jnp.int32)
    masks = (place, seg_row, seg_row.astype(f32))

    bias_sum = jnp.sum(rounded(branch_scale * own_dy.astype(f32)).astype(f32), axis=0)
    bias_total = []
    sums = [total_of(bias_total, bias_sum.reshape(-1, LANES))]
    near_n, near_k, near_kt, near_v, near_vt, queries = project(
        place, own_x, got_x, norm_rows, bias_rows, w_qkv, True, []
    )
    state = attend(*masks, queries, near_k, near_vt, None, [])
    far_n, far_k, far_kt, far_v, far_vt = project(
        place, far_own, far_got, norm_rows, bias_rows, w_qkv, False, []
    )
    attn, attn_t, log_sum = attend(*masks, queries, far_k, far_vt, state, [])
    (
        active, d_up, two_n, d_mlp, d_attn, d_resid, d_heads, delta, block_low, vec, d_bias_up
    ) = feed(
        place, attn, attn_t, own_x, got_x, own_dy, got_dy, feed_rows, w_out, w_up, w_down
    )
    up_rows = d_bias_up.reshape(24, LANES)

    core_x = jnp.stack([core, x]).astype(jnp.int32)
    parts = {}

    def grads(*given, **options):
        planes, halves_of, left = weight_grad(core_x, *given, **options)
        return [reduce_planes(parts, planes, *halves_of)] if planes else [], left

    plane_rows = 8 * shard_rows
    down, left = grads(
        [(active, d_mlp, 0, False)], [up_rows, vec], None, None, ROW_PR, [(0, 0, 22, 2)],
        [(2, 1, 18, 6)], shard_rows, total_rows, [], 15e9,
    )
    _, core_down = set_out(down)
    _, out_rows = grads(
        [(attn, d_attn, 0, False)], [vec], None, None, ROW_WO, [], [(8, 0, 0, 8)], shard_rows,
        down16(ROW_FC), [], 4e9, whole=False,
    )
    up, left = grads(
        [(two_n, d_up, 0, False)], [up_rows, vec], out_rows, left, ROW_FC, [(0, 1, 8, 10)],
        [(10, 0, 0, 22)], shard_rows, -(-down16(ROW_PR) // plane_rows) * plane_rows, [], 10e9,
    )
    sent_up, core_up = set_out(up)
    sent_down, one_down = move_on(down, None)

    given = (*masks, queries, d_heads, log_sum, delta)
    d_near, dq_t = attend_back(
        *given, (near_k, near_kt, near_v), None, core_down + sent_up + sent_down
    )
    sent_up, one_up = move_on(up, dq_t)
    sent_down, two_down = move_on(down, dq_t)
    d_far, dq = attend_back(
        *given, (far_k, far_kt, far_v), dq_t, core_up + one_down + sent_up + sent_down
    )
    sent_down, z_down = move_on(down, d_far)
    sent_up, two_up = move_on(up, d_far)
    far_in, near_in, one_vec = input_back(
        place, (far_own, far_got), (own_x, got_x), d_far, d_near, dq, d_resid, w_qkv, norm_rows,
        two_down + sent_up + sent_down,
    )

    own_far, other_far = halves(far_in, 0, core)
    other_far = rounded(other_far)
    far_got = swap(other_far, "seq", 1)
    own, other = halves(near_in, 0, core)
    other = rounded(other)
    near_got = swap(other, "seq", 1)
    sent_up, z_up = move_on(up, one_vec)
    sent_down, last_down = move_on(down, one_vec)
    if left is not None:
        extra = jnp.concatenate([one_vec[16:], jnp.zeros((left.shape[0] - 8, LANES), f32)])
        left = rounded(left.astype(f32) + extra)
    planes, (own_qkv, other_qkv), _ = weight_grad(
        core_x, [(near_n, dq, 0, False), (near_n, d_near, D, False), (far_n, d_far, D, True)], [one_vec],
        None, left, ROW_QKV, [(0, 0, 0, 12)], [(12, 0, 12, 4)], shard_rows,
        -(-down16(ROW_WO) // plane_rows) * plane_rows,
        two_up + z_down + sent_up + sent_down + [other_far, other], 15e9,
    )
    qkv = [reduce_planes(parts, planes, own_qkv, gate(other_qkv, z_up + last_down))]
    sent_qkv, _ = set_out(qkv)
    set_out(sums)
    sent_qkv, _ = move_on(qkv, None)
    _, z_up = move_on(up, sent_qkv)
    move_on(sums, sent_qkv)
    sent_qkv, _ = move_on(qkv, z_up)
    move_on(sums, sent_qkv)
    far_sum = rounded(own_far + tie(far_got, sent_qkv).astype(f32))
    from_far = swap(far_sum, "seq", 2)
    move_on(up, sent_qkv)
    sent_qkv, _ = move_on(qkv, None)
    move_on(sums, sent_qkv)
    input_grad = own + tie(near_got, sent_qkv).astype(f32)
    block_output = unpick(tie(block_low, sent_qkv))
    sent_qkv, _ = move_on(qkv, None)
    move_on(sums, sent_qkv)
    while move_on(qkv + up + down + sums, None)[0]:
        pass
    input_grad = rounded(jnp.where(x == 0, input_grad + from_far.astype(f32), input_grad))
    bias_down_grad = bias_total[0].reshape(-1) / device_count

    own_plane = lax.axis_index("dp") // 2
    summed = jnp.zeros((core_window(shard_rows), LANES), bf16)
    for plane in sorted(parts, reverse=True):
        summed = jnp.where(own_plane == plane, parts[plane], summed)
    first_row = lax.axis_index(("dp", "seq")) * shard_rows
    own_params = lax.dynamic_slice_in_dim(params, first_row, shard_rows, 0)
    new_params, new_first, new_second = adam(
        jnp.stack([core, first_row]).astype(jnp.int32), summed, own_params, first_moment,
        second_moment, device_count,
    )
    return (
        block_output.reshape(tokens.shape),
        input_grad.reshape(tokens.shape),
        new_params,
        new_first,
        new_second,
        bias_down_grad,
    )


def solution(mesh):
    return jax.shard_map(
        shards,
        mesh=mesh,
        in_specs=(
            P("seq", "dp", None),
            P("seq", "dp", None),
            P("seq", "dp"),
            P(None, "dp"),
            P(),
            P(("dp", "seq"), None),
            P(("dp", "seq"), None),
        ),
        out_specs=(
            P("seq", "dp", None),
            P("seq", "dp", None),
            P(("dp", "seq"), None),
            P(("dp", "seq"), None),
            P(("dp", "seq"), None),
            P(),
        ),
        check_vma=False,
    )
```
